512 devices in a mesh: sect: 2 (over z_hi), tp: 32 (over x, z_lo), grp: 8 (over y, core).
Axes of the slice: x: 4, y: 4, z: 16 (z_hi: 2, z_lo: 8; z = z_hi * 8 + z_lo), core: 2. Of those that a mesh axis runs over, the one named last changes fastest.
Arguments:
- mamba_x: bfloat16 [4096, 16384], P(('sect', 'grp'), 'tp'), may hold values from -6 to 6
- mamba_z: bfloat16 [4096, 16384], P(('sect', 'grp'), 'tp'), may hold values from -6 to 6
- conv_weight: float32 [4, 16384], P(None, 'tp'), may hold values from -3 to 3
- conv_bias: float32 [16384], P('tp'), may hold values from -3 to 3
- x_proj: bfloat16 [16384, 544], P('tp'), may hold values from -0.046875 to 0.046875
- norm_gain: float32 [544], replicated, may hold values from 0.5 to 1.5
- dt_proj: bfloat16 [512, 16384], P(None, 'tp'), may hold values from -0.25 to 0.25
- dt_bias: float32 [16384], P('tp'), may hold values from -4 to 0
- a_log: float32 [16, 16384], P(None, 'tp'), may hold values from -3 to 1
- d_skip: float32 [16384], P('tp'), may hold values from 0.5 to 1.5
- segment_ids: int32 [2, 2048], P('sect', 'grp'), may hold values from 0 to 3, never falling along the last dimension, each value on 1 to 1536 neighbouring positions
- queries: bfloat16 [4096, 8192], P(('sect', 'grp'), 'tp'), may hold values from -6 to 6
- keys_values: bfloat16 [4096, 2, 1024], P(('sect', 'grp')), may hold values from -6 to 6
- kv_owner: int32 [2, 128, 1], P('sect', 'grp'), may hold values from 0 to 7; in each aligned block of 16 rows (0 to 15, 16 to 31, ..., all dimensions but the last counted through in order) at most 4 rows name the same one
- moe_in: bfloat16 [4096, 8192], P(('sect', 'grp'), 'tp'), may hold values from -6 to 6
- moe_gain: float32 [8192], P('tp'), may hold values from 0.5 to 1.5
- router: bfloat16 [8192, 16], P('tp'), may hold values from -0.0625 to 0.0625
- routing: int32 [4096, 2], P(('sect', 'grp')), may hold values from 0 to 15, all different within a row
Outputs:
- mixer_out: bfloat16 [4096, 16384], P(('sect', 'grp'), 'tp')
- final_state: float32 [2, 16, 16384], P('sect', 'grp', 'tp')
- attn_out: bfloat16 [4096, 8192], P(('sect', 'grp'), 'tp')
- kv_pages: bfloat16 [2, 8, 32, 32, 16, 256], P('sect', 'grp', 'tp')
- expert_input: bfloat16 [4096, 8192], P(('sect', 'grp'), 'tp')
- gate_weights: float32 [4096, 2], P(('sect', 'grp'))
The draws below stay inside these ranges and needn't reach their ends.
Inputs may be any that keep to these rules, and one draw needn't show every extreme that they name: `segment_ids`: in each span, ids never fall, start at 0 and number its 4 requests; a request holds at most 1536 positions and one holds exactly that many. `kv_owner`: owner index along grp in the other section. Of the 16 pages of one device's rows, at most 4 share an owner, and in every draw some device has 4 pages for one owner. `routing`: the 2 experts of a token differ.
All inputs are finite; a program needn't handle non-finite values.
Results may differ from the reference program's by a relative error of at most 0.013.
Values may be sent and summed in bfloat16 or wider, within the bound.
A program may use at most 64 MiB of HBM per device.

```python
import math
import jax
import jax.numpy as jnp
import numpy as np
from jax import lax

D = 8192
DI = 16384
NST = 16
DTR = 512
KCONV = 4
HEADS = 64
KVH = 8
HD = 128
EXPERTS = 16
TOPK = 2
BLK = 16
REQS = 4
SPAN = 2048
TOKENS = 4096
PAGES_DEV = 16
PAGES = 128
CAP = 4
SLOTS = 32
N_SECT = 2
N_TP = 32
N_GRP = 8


def draw_queries(key, part):
    own_key = jax.random.fold_in(key, 11)
    values = jnp.clip(jax.random.normal(own_key, (TOKENS, HEADS * HD), jnp.float32), -6.0, 6.0)
    return values.astype(jnp.bfloat16)


def draw_keys_values(key, part):
    own_key = jax.random.fold_in(key, 23)
    values = jnp.clip(jax.random.normal(own_key, (TOKENS, 2, KVH * HD), jnp.float32), -6.0, 6.0)
    return values.astype(jnp.bfloat16)


def level_of(key, dims, cuts, low, largest):
    gain, own = 1.0, jax.random.fold_in(key, 6)
    for dim, shards_of in cuts:
        heights = jnp.exp(jax.random.uniform(jax.random.fold_in(own, dim), (shards_of,), jnp.float32, low / len(cuts), largest / len(cuts)))
        gain = gain * jnp.repeat(heights, dims[dim] // shards_of).reshape([-1 if axis == dim else 1 for axis in range(len(dims))])
    return gain


def distinct(key, rows, count, top, lift):
    ranking = jax.random.permutation(jax.random.fold_in(key, 1), count)
    pull = ranking
    for power in range(3):
        pull = pull * pull // count
    pull = pull * lift // count
    lots = jax.random.randint(jax.random.fold_in(key, 2), (rows, count), 0, 4096) + pull
    fixed_rows = jax.random.permutation(jax.random.fold_in(key, 3), rows)[jnp.arange(count) % rows]
    lots = jnp.where(jnp.arange(rows)[:, None] == fixed_rows[None, :], 1 << 14, lots)
    merit = lots * count + jnp.arange(count)
    return lax.top_k(merit.astype(jnp.int32), top)[1].astype(jnp.int32)


def profile(count, total, limit, slope):
    loads = [(1 << 20) // math.isqrt(rank ** slope) + 1 for rank in range(2, count + 1)]
    surplus, given = total - limit - (count - 1), [1] * (count - 1)
    while surplus > 0:
        movable = [i for i in range(count - 1) if given[i] < limit]
        mass, budget = sum([loads[i] for i in movable]), surplus
        for i in movable:
            addition = min(limit - given[i], max(1, budget * loads[i] // mass), surplus)
            given[i] = given[i] + addition
            surplus = surplus - addition
    return np.array([limit] + given)


def ragged(key, amount, total, most, lean):
    if amount == 2:
        one = jax.random.randint(key, (), max(1, total - most), min(most, total - 1) + 1)
        return jnp.stack([one, total - one])
    lengths = jnp.asarray(profile(amount, total, most, lean), jnp.int32)
    twos = (amount - 1) // 2
    giver, taker = lengths[1:1 + 2 * twos:2], lengths[2:2 + 2 * twos:2]
    margin = jnp.minimum(giver - 1, most - taker)
    shifted = jax.random.randint(jax.random.fold_in(key, 1), (twos,), 0, 1 << 20) % (margin + 1)
    lengths = lengths.at[1:1 + 2 * twos:2].set(giver - shifted).at[2:2 + 2 * twos:2].set(taker + shifted)
    return lengths[jax.random.permutation(jax.random.fold_in(key, 2), amount)]


def shared_out(rng, own, number, rows, count, top, bound, lean):
    sequence = jax.random.permutation(rng, count)
    heavy_load, usual = shares(count, rows * top, bound, lean, True), shares(count, rows * top, bound, lean, False)
    places = jnp.arange(count)

    def named(sizes, offset_by):
        used = int((sizes > 0).sum())
        fixed = max(1, used // 4)
        shifted = fixed + (places - fixed + offset_by * (used - fixed)) % max(1, count - fixed)
        return jnp.zeros((count,), jnp.int32).at[sequence[jnp.where(places < fixed, places, shifted)]].set(jnp.asarray(sizes, jnp.int32))

    sizes = jnp.where(number % 4 == 0, named(heavy_load, number // 4), named(usual, number - number // 4 - 1))
    mixed = jax.random.permutation(jax.random.fold_in(own, 3), count)
    source_of, receiver = mixed[0:count // 2 * 2:2], mixed[1:count // 2 * 2:2]
    margin = jnp.minimum(sizes[source_of] - 1, bound - sizes[receiver]) // 2
    margin = jnp.where((source_of == sequence[0]) | (receiver == sequence[0]) | (sizes[receiver] == 0), 0, jnp.maximum(margin, 0))
    shifted = jax.random.randint(jax.random.fold_in(own, 4), (count // 2,), 0, 1 << 20) % (margin + 1)
    sizes = sizes.at[source_of].add(-shifted).at[receiver].add(shifted)
    labels = jnp.searchsorted(jnp.cumsum(sizes), jnp.arange(rows * top), side="right").astype(jnp.int32)
    grid = labels.reshape(top, rows).T
    grid = grid[jax.random.permutation(jax.random.fold_in(own, 1), rows)]
    offset_by = jax.random.randint(jax.random.fold_in(own, 2), (rows, 1), 0, top)
    return jnp.take_along_axis(grid, (jnp.arange(top)[None, :] + offset_by) % top, axis=1)


def shares(number_of, total, most, slope, full):
    weights = [(1 << 20) // math.isqrt(rank ** slope) + 1 for rank in range(1, number_of + 1)]
    largest = most if full else min(most, max(-(-total // number_of), total * weights[0] // sum(weights)))
    least = 1 if total - largest >= number_of - 1 else 0
    counts, spare = [largest] + [least] * (number_of - 1), total - largest - least * (number_of - 1)
    while spare > 0:
        free = [i for i in range(1, number_of) if counts[i] < largest] or [i for i in range(1, number_of) if counts[i] < most]
        pool, remaining = sum([weights[i] for i in free]), spare
        for i in free:
            addition = min(most - counts[i], max(1, remaining * weights[i] // pool), spare)
            counts[i] = counts[i] + addition
            spare = spare - addition
    return np.array(counts)


def bell_draw(stream_key, extent, width, bound, cuts=(), kind=jnp.bfloat16):
    level = level_of(stream_key, extent, cuts, -0.22, 0.18) if cuts else 1.0
    entries = jax.random.normal(stream_key, extent, jnp.float32) * width * level
    return jnp.minimum(jnp.maximum(entries, -bound), bound).astype(kind)


def setup_inputs(seed: int = 0) -> dict:
    splits = jax.random.split(jax.random.key(seed), 19)
    mamba_x = bell_draw(splits[0], (TOKENS, DI), 1.0, 6.0, ((0, 16), (1, 32)))
    mamba_z = bell_draw(splits[1], (TOKENS, DI), 1.0, 6.0, ((0, 16), (1, 32)))
    conv_weight = bell_draw(splits[2], (KCONV, DI), KCONV ** -0.5, 3.0, ((1, 32),), jnp.float32)
    conv_bias = bell_draw(splits[3], (DI,), 0.5, 3.0, ((0, 32),), jnp.float32)
    x_proj = bell_draw(splits[4], (DI, DTR + 2 * NST), DI ** -0.5, 0.046875, ((0, 32),))
    norm_gain = jnp.clip(1.0 + 0.1 * jax.random.normal(splits[5], (DTR + 2 * NST,), jnp.float32), 0.5, 1.5)
    dt_proj = bell_draw(splits[6], (DTR, DI), DTR ** -0.5, 0.25, ((1, 32),))
    dt_bias = jnp.clip(-4.0 + 4.0 * jax.random.uniform(splits[7], (DI,), jnp.float32) ** level_of(splits[7], (DI,), ((0, 32),), -0.2, 0.2), -4.0, 0.0)
    a_log = jnp.clip(-3.0 + 4.0 * jax.random.uniform(splits[8], (NST, DI), jnp.float32) ** level_of(splits[8], (NST, DI), ((1, 32),), -0.2, 0.2), -3.0, 1.0)
    d_skip = jnp.clip(0.5 + 1.0 * jax.random.uniform(splits[9], (DI,), jnp.float32) ** level_of(splits[9], (DI,), ((0, 32),), -0.2, 0.2), 0.5, 1.5)
    segment_ids = jax.vmap(lambda own: jnp.searchsorted(jnp.cumsum(ragged(own, REQS, SPAN, 3 * SPAN // 4, 2)), jnp.arange(SPAN), side="right"))(jax.random.split(splits[10], N_SECT)).reshape((N_SECT, SPAN)).astype(jnp.int32)
    queries = draw_queries(jax.random.fold_in(splits[18], 71), 0)
    keys_values = draw_keys_values(jax.random.fold_in(splits[18], 71), 0)
    kv_owner_keys = jax.random.split(jax.random.fold_in(splits[13], 1), N_SECT * PAGES // PAGES_DEV)
    kv_owner_turns = jax.random.permutation(jax.random.fold_in(splits[13], 3), N_SECT * PAGES // PAGES_DEV)
    kv_owner = jax.vmap(lambda own, number: shared_out(jax.random.fold_in(splits[13], 2), own, number, PAGES_DEV, N_GRP, 1, CAP, 2))(kv_owner_keys, kv_owner_turns).reshape((N_SECT, PAGES, 1))
    moe_in = bell_draw(splits[14], (TOKENS, D), 1.0, 6.0, ((0, 16), (1, 32)))
    moe_gain = jnp.clip(1.0 + 0.1 * jax.random.normal(splits[15], (D,), jnp.float32), 0.5, 1.5)
    router = bell_draw(splits[16], (D, EXPERTS), D ** -0.5, 0.0625, ((0, 32),))
    routing = distinct(splits[17], TOKENS, EXPERTS, TOPK, 1024)
    return dict(mamba_x=mamba_x, mamba_z=mamba_z, conv_weight=conv_weight, conv_bias=conv_bias, x_proj=x_proj, norm_gain=norm_gain, dt_proj=dt_proj, dt_bias=dt_bias, a_log=a_log, d_skip=d_skip, segment_ids=segment_ids, queries=queries, keys_values=keys_values, kv_owner=kv_owner, moe_in=moe_in, moe_gain=moe_gain, router=router, routing=routing)


EPS = 1e-06
FLOOR_SCORE = -1e+30

def rms_scale(values, scales):
    mean_square = lax.optimization_barrier(jnp.mean(values * values, axis=-1, keepdims=True))
    return values * lax.rsqrt(mean_square + EPS) * scales

def normalize_low(sums, norm_gain):
    groups_list = [rms_scale(sums[:, :DTR], norm_gain[:DTR]), rms_scale(sums[:, DTR:DTR + NST], norm_gain[DTR:DTR + NST]), rms_scale(sums[:, DTR + NST:], norm_gain[DTR + NST:])]
    return jnp.concatenate(groups_list, axis=1).astype(jnp.bfloat16)

def mixer_span(span_x, span_z, segments, conv_weight, conv_bias, x_proj, norm_gain, dt_proj, dt_bias, a_log, d_skip):
    padded_x = jnp.concatenate([jnp.zeros((KCONV - 1, DI), jnp.float32), span_x.astype(jnp.float32)], axis=0)
    padded_seg = jnp.concatenate([jnp.full((KCONV - 1,), -1, jnp.int32), segments], axis=0)
    convolved = jnp.broadcast_to(conv_bias[None, :], (SPAN, DI))
    for offset in range(KCONV):
        same_request = (padded_seg[offset:offset + SPAN] == segments)[:, None]
        convolved = convolved + jnp.where(same_request, padded_x[offset:offset + SPAN] * conv_weight[offset][None, :], 0.0)
    x_conv = jax.nn.silu(convolved).astype(jnp.bfloat16)
    low_rank = normalize_low(jnp.dot(x_conv, x_proj, preferred_element_type=jnp.float32), norm_gain)
    step_size = jax.nn.softplus(jnp.dot(low_rank[:, :DTR], dt_proj, preferred_element_type=jnp.float32) + dt_bias)
    rate = -jnp.exp(a_log)
    x_float = x_conv.astype(jnp.float32)
    b_rows = low_rank[:, DTR:DTR + NST].astype(jnp.float32)
    c_rows = low_rank[:, DTR + NST:].astype(jnp.float32)
    starts = jnp.concatenate([jnp.ones((1,), dtype=bool), segments[1:] != segments[:-1]])

    def advance(state, inputs):
        step_row, x_row, b_row, c_row, start_row = inputs
        decays = jnp.where(start_row, 0.0, jnp.exp(step_row[None, :] * rate))
        state = decays * state + b_row[:, None] * (step_row * x_row)[None, :]
        return (state, lax.optimization_barrier(jnp.sum(c_row[:, None] * state, axis=0)))
    end_state, ssm_rows = lax.scan(advance, jnp.zeros((NST, DI), jnp.float32), (step_size, x_float, b_rows, c_rows, starts))
    mixed = ((ssm_rows + d_skip * x_float) * jax.nn.silu(span_z.astype(jnp.float32))).astype(jnp.bfloat16)
    return (mixed, end_state)

def attend_span(span_q, span_kv, segments):
    query_heads = span_q.reshape(SPAN, HEADS, HD).transpose(1, 0, 2)
    key_heads = span_kv[:, 0].reshape(SPAN, KVH, HD).transpose(1, 0, 2)
    value_heads = span_kv[:, 1].reshape(SPAN, KVH, HD).transpose(1, 0, 2)
    position = jnp.arange(SPAN)
    allowed = (position[None, :] <= position[:, None]) & (segments[None, :] == segments[:, None])

    def one_head(inputs):
        query_block, head_index = inputs
        pair_index = head_index // (HEADS // KVH)
        key_block = lax.dynamic_index_in_dim(key_heads, pair_index, 0, keepdims=False)
        value_block = lax.dynamic_index_in_dim(value_heads, pair_index, 0, keepdims=False)
        scores = jnp.dot(query_block, key_block.T, preferred_element_type=jnp.float32) * HD ** (-0.5)
        masked = jnp.where(allowed, scores, FLOOR_SCORE)
        weights = jnp.where(allowed, jnp.exp(masked - lax.optimization_barrier(jnp.max(masked, axis=1, keepdims=True))), 0.0)
        denominator = lax.optimization_barrier(jnp.sum(weights, axis=1, keepdims=True))
        return jnp.dot(weights.astype(jnp.bfloat16), value_block, preferred_element_type=jnp.float32) / denominator
    outputs = lax.map(one_head, (query_heads, jnp.arange(HEADS, dtype=jnp.int32)))
    return outputs.transpose(1, 0, 2).reshape(SPAN, HEADS * HD).astype(jnp.bfloat16)

def pages_span(span_kv, owners):
    per_head = span_kv.reshape(SPAN, 2, KVH, HD).transpose(2, 0, 1, 3).reshape(KVH, PAGES, BLK, 2 * HD)
    order_index = jnp.arange(PAGES, dtype=jnp.int32)
    source = order_index // PAGES_DEV
    earlier = (owners[None, :] == owners[:, None]) & (source[None, :] == source[:, None]) & (order_index[None, :] < order_index[:, None])
    slot_ranks = lax.optimization_barrier(jnp.sum(earlier.astype(jnp.int32), axis=1))
    targets = (owners * SLOTS + source * CAP + slot_ranks).astype(jnp.int32)
    filled = jnp.zeros((KVH, N_GRP * SLOTS, BLK, 2 * HD), jnp.bfloat16).at[:, targets].set(per_head)
    filled = filled.reshape(KVH, N_GRP, SLOTS, BLK, 2 * HD)
    head_of = (jnp.arange(N_TP) * KVH // N_TP).astype(jnp.int32)
    return jnp.take(filled, head_of, axis=0).transpose(1, 0, 2, 3, 4)

def reference(mamba_x, mamba_z, conv_weight, conv_bias, x_proj, norm_gain, dt_proj, dt_bias, a_log, d_skip, segment_ids, queries, keys_values, kv_owner, moe_in, moe_gain, router, routing):
    mixer_parts = []
    state_parts = []
    attn_parts = []
    page_parts = []
    for section in range(N_SECT):
        offset_row = section * SPAN
        mixed, end_state = mixer_span(mamba_x[offset_row:offset_row + SPAN], mamba_z[offset_row:offset_row + SPAN], segment_ids[section], conv_weight, conv_bias, x_proj, norm_gain, dt_proj, dt_bias, a_log, d_skip)
        mixer_parts.append(mixed)
        state_parts.append(end_state)
        attn_parts.append(attend_span(queries[offset_row:offset_row + SPAN], keys_values[offset_row:offset_row + SPAN], segment_ids[section]))
        page_parts.append(pages_span(keys_values[offset_row:offset_row + SPAN], kv_owner[section, :, 0]))
    mixer_out = jnp.concatenate(mixer_parts, axis=0)
    attn_out = jnp.concatenate(attn_parts, axis=0)
    final_state = jnp.stack([state_parts[(section - 1) % N_SECT] for section in range(N_SECT)])
    kv_pages = jnp.stack([page_parts[(section - 1) % N_SECT] for section in range(N_SECT)])
    moe_rows = moe_in.astype(jnp.float32)
    inverse = lax.rsqrt(lax.optimization_barrier(jnp.mean(moe_rows * moe_rows, axis=1, keepdims=True)) + EPS)
    normed = moe_rows * moe_gain * inverse
    expert_input = normed.astype(jnp.bfloat16)
    logits = jnp.dot(normed, router.astype(jnp.float32), precision=lax.Precision.HIGHEST)
    picked = jnp.take_along_axis(logits, routing, axis=1)
    gate_weights = jax.nn.softmax(picked, axis=1)
    return (mixer_out, final_state, attn_out, kv_pages, expert_input, gate_weights)
```

```python
import jax
import jax.numpy as jnp
from jax import lax
from jax.experimental import pallas as pl
from jax.experimental.pallas import tpu as pltpu
from jax.sharding import PartitionSpec as P

MESH = pl.DeviceIdType.MESH
F32 = jnp.float32
BF16 = jnp.bfloat16
I32 = jnp.int32

ROWS = 256
WIDTH = 512
RANK = 512
NST = 16
HD = 128
BLK = 16
NX, NZ, NG = 4, 8, 8
PAY = 768
HALF = PAY // 2
SLOTS = 4
EPS = 1e-06
LOG2E = 1.4426950408889634
HUGE = 1e30
VMEM = pl.BlockSpec(memory_space=pltpu.VMEM)
ANY = pl.BlockSpec(memory_space=pl.ANY)


def iota(shape, dim):
    return lax.broadcasted_iota(I32, shape, dim)


def dot(a, b, **kw):
    return jnp.dot(a, b, preferred_element_type=F32, **kw)


def dot_t(a, b, **kw):
    return lax.dot_general(a, b, (((1,), (1,)), ((), ())), preferred_element_type=F32, **kw)


def remote(src, dst, send, recv, where):
    return pltpu.make_async_remote_copy(
        src_ref=src, dst_ref=dst, send_sem=send, recv_sem=recv, device_id=where, device_id_type=MESH
    )


def greet(places):
    barrier = pltpu.get_barrier_semaphore()
    for place in places:
        pl.semaphore_signal(barrier, inc=1, device_id=place, device_id_type=MESH)
    pl.semaphore_wait(barrier, len(places))


def mix_kernel(
    x_ref, seg_col_ref, seg_row_ref, conv_w_ref, conv_b_ref, x_proj_ref, gain_ref,
    q_ref, pair_ref, page_ref, target_ref, moe_ref, moe_gain_ref, router_ref, routing_ref,
    xconv_ref, rank_ref, bc_ref, start_ref, attn_ref, pages_ref, expert_ref, gate_ref,
    rim, rim_seg, seg_send, seg_out, seg_all, kv_all, ext, ext_seg, pay, rx, chunk, rz, piece, low,
    outgoing, best, total, accum,
    rim_s, rim_r, rseg_s, rseg_r, kv_s, kv_r, sg_s, sg_r, pg_s, pg_r, xs, xr, zs, zr, gs, gr, hs, hr,
):
    sect, tp, grp = lax.axis_index("sect"), lax.axis_index("tp"), lax.axis_index("grp")
    x, z = tp // NZ, tp % NZ
    others_x = [lax.rem(x + d, NX) for d in range(1, NX)]
    others_z = [lax.rem(z + d, NZ) for d in range(1, NZ)]
    others_g = [lax.rem(grp + d, NG) for d in range(1, NG)]
    mirror = x * NZ + (NZ - 1 - z)
    place_x = [{"tp": o * NZ + z} for o in others_x]
    place_z = [{"tp": x * NZ + o} for o in others_z]
    place_g = [{"grp": o} for o in others_g]
    place_p = [{"sect": 1 - sect, "tp": mirror, "grp": o} for o in range(NG)]
    greet(place_x + place_z + place_g + place_p)

    seg_send[...] = jnp.broadcast_to(seg_col_ref[ROWS - 8 :, :], (8, 128))
    seg_out[...] = jnp.broadcast_to(seg_row_ref[...], (8, ROWS))
    rim_copy = remote(x_ref.at[ROWS - 16 : ROWS], rim, rim_s, rim_r, {"grp": lax.rem(grp + 1, NG)})
    rim_copy.start()
    rseg_copy = remote(seg_send, rim_seg, rseg_s, rseg_r, {"grp": lax.rem(grp + 1, NG)})
    rseg_copy.start()

    moe_rows = moe_ref[...].astype(F32)
    scaled = moe_rows * moe_gain_ref[...]
    spread = (iota((16, 128), 0) == iota((16, 128), 1)).astype(BF16)
    router = dot(router_ref[...], spread)
    logits_part = dot(scaled, router, precision=lax.Precision.HIGHEST)
    squares = jnp.sum(moe_rows * moe_rows, axis=1, keepdims=True)
    tail = jnp.where(iota((ROWS, 128), 1) == 16, squares, logits_part)
    pay[:, 640:768] = tail.astype(BF16)
    pay[:, 512:640] = jnp.zeros((ROWS, 128), BF16)

    ext[8:, :] = x_ref[...].astype(F32)
    ext_seg[8:, :] = jnp.broadcast_to(seg_col_ref[...], (ROWS, 128))
    rim_copy.wait()
    rseg_copy.wait()
    ext[0:8, :] = rim[8:16, :].astype(F32)
    ext_seg[0:8, :] = jnp.where(grp == 0, -1, rim_seg[...])
    here = ext_seg[8:, :]
    start_ref[...] = jnp.where(ext_seg[7 : 7 + ROWS, :] != here, HUGE, 0.0).astype(F32)
    for lane in range(0, WIDTH, 128):
        cols = slice(lane, lane + 128)
        value = jnp.broadcast_to(conv_b_ref[:, cols], (ROWS, 128))
        for k in range(4):
            same = ext_seg[5 + k : 5 + k + ROWS, :] == here
            value = value + jnp.where(same, ext[5 + k : 5 + k + ROWS, cols] * conv_w_ref[k : k + 1, cols], 0.0)
        xconv_ref[:, cols] = (value / (1.0 + jnp.exp(-value))).astype(BF16)

    conv = xconv_ref[...]
    pay[:, 0:512] = dot(conv, x_proj_ref[:, 0:512]).astype(BF16)
    pay[:, 512:544] = dot(conv, x_proj_ref[:, 512:544]).astype(BF16)
    x_copies = []
    for d, (o, place) in enumerate(zip(others_x, place_x)):
        rows = pl.ds(pl.multiple_of(o * 64, 64), 64)
        x_copies.append(remote(pay.at[rows], rx.at[x], xs.at[d], xr.at[x], place))
    for copy in x_copies:
        copy.start()

    for d in range(1, NG):
        @pl.when(grp + d < NG)
        def _(d=d):
            place = {"grp": grp + d}
            remote(seg_out, seg_all.at[grp], sg_s.at[d], sg_r.at[grp], place).start()
            remote(pair_ref, kv_all.at[grp], kv_s.at[d], kv_r.at[grp], place).start()

    row, col = iota((512, ROWS), 0), iota((512, ROWS), 1)
    choose = ((target_ref[...] == row // BLK) & (row % BLK == col % BLK)).astype(BF16)
    outgoing[...] = dot(choose, page_ref[...]).astype(BF16).reshape(NG, 64, 256)
    page_copies = []
    for o in range(NG):
        page_copies.append(remote(outgoing.at[o], pages_ref.at[grp], pg_s.at[o], pg_r.at[grp], place_p[o]))
    for copy in page_copies:
        copy.start()

    factor = HD**-0.5 * LOG2E

    def attend(key_block, value_block, allowed, first):
        for h in range(2):
            cols = slice(h * HD, (h + 1) * HD)
            scores = dot_t(q_ref[:, cols], key_block)
            masked = jnp.where(allowed, scores, -HUGE)
            high = jnp.max(masked, axis=1, keepdims=True)
            if first:
                new = high
                weights = jnp.exp2((masked - new) * factor)
                total[h] = jnp.broadcast_to(jnp.sum(weights, axis=1, keepdims=True), (ROWS, 128))
                accum[h] = dot(weights.astype(BF16), value_block)
            else:
                old = best[h][:, 0:1]
                new = jnp.maximum(old, high)
                weights = jnp.exp2((masked - new) * factor)
                fade = jnp.exp2((old - new) * factor)
                total[h] = total[h] * fade + jnp.sum(weights, axis=1, keepdims=True)
                accum[h] = accum[h] * fade + dot(weights.astype(BF16), value_block)
            best[h] = jnp.broadcast_to(new, (ROWS, 128))

    seg_q = seg_col_ref[...]
    causal = iota((ROWS, ROWS), 1) <= iota((ROWS, ROWS), 0)
    attend(pair_ref[:, 0:HD], pair_ref[:, HD:], causal & (seg_row_ref[...] == seg_q), True)

    for o in others_x:
        remote(pay.at[0:64], rx.at[o], xs.at[0], xr.at[o], place_x[0]).wait_recv()
    summed = pay[pl.ds(pl.multiple_of(x * 64, 64), 64), :].astype(F32)
    for o in others_x:
        summed = summed + rx[o].astype(F32)
    for h in range(2):
        for r in range(4):
            chunk[4 * h + r] = summed[16 * r : 16 * r + 16, HALF * h : HALF * (h + 1)].astype(BF16)
    z_copies = []
    for d, (o, place) in enumerate(zip(others_z, place_z)):
        z_copies.append(remote(chunk.at[o], rz.at[z], zs.at[d], zr.at[z], place))
    for copy in z_copies:
        copy.start()

    for o in others_z:
        remote(chunk.at[0], rz.at[o], zs.at[0], zr.at[o], place_z[0]).wait_recv()
    summed = chunk[z].astype(F32)
    for o in others_z:
        summed = summed + rz[o].astype(F32)
    low[x, z] = summed.astype(BF16)
    g_copies = []
    for d, place in enumerate(place_z):
        g_copies.append(remote(low.at[x, z], low.at[x, z], gs.at[d], gr.at[z], place))
    for copy in g_copies:
        copy.start()
    for o in others_z:
        remote(low.at[x, z], low.at[x, o], gs.at[0], gr.at[o], place_z[0]).wait_recv()
    h_copies = []
    for d, place in enumerate(place_x):
        h_copies.append(remote(low.at[x], low.at[x], hs.at[d], hr.at[x], place))
    for copy in h_copies:
        copy.start()

    def earlier(j, carry):
        remote(seg_out, seg_all.at[j], sg_s.at[0], sg_r.at[j], place_g[0]).wait_recv()
        remote(pair_ref, kv_all.at[j], kv_s.at[0], kv_r.at[j], place_g[0]).wait_recv()
        attend(kv_all[j, :, 0:HD], kv_all[j, :, HD:], seg_all[j, 0:1, :] == seg_q, False)
        return carry

    lax.fori_loop(0, grp, earlier, 0)
    for h in range(2):
        attn_ref[:, h * HD : (h + 1) * HD] = (accum[h] / total[h]).astype(BF16)

    for o in others_x:
        remote(low.at[x], low.at[o], hs.at[0], hr.at[o], place_x[0]).wait_recv()
    left = low[:, 0:4].reshape(ROWS, HALF).astype(F32)
    right = low[:, 4:8].reshape(ROWS, HALF).astype(F32)
    mean = (jnp.sum(left * left, axis=1, keepdims=True) + jnp.sum(right[:, :128] * right[:, :128], axis=1, keepdims=True)) / RANK
    scale = lax.rsqrt(mean + EPS)
    rank_ref[:, 0:HALF] = (left * scale * gain_ref[:, 0:HALF]).astype(BF16)
    rank_ref[:, HALF:RANK] = (right[:, :128] * scale * gain_ref[:, HALF:RANK]).astype(BF16)
    both = right[:, 128 : 128 + 2 * NST]
    is_b = iota((ROWS, 2 * NST), 1) < NST
    power = both * both
    mean_b = jnp.sum(jnp.where(is_b, power, 0.0), axis=1, keepdims=True) / NST
    mean_c = jnp.sum(jnp.where(is_b, 0.0, power), axis=1, keepdims=True) / NST
    scale = jnp.where(is_b, lax.rsqrt(mean_b + EPS), lax.rsqrt(mean_c + EPS))
    bc_ref[...] = (both * scale * gain_ref[:, RANK : RANK + 2 * NST]).astype(BF16)

    sums = right[:, 256:384]
    inverse = lax.rsqrt(sums[:, 16:17] / (RANK * NST) + EPS)
    expert_ref[...] = (moe_ref[...].astype(F32) * moe_gain_ref[...] * inverse).astype(BF16)
    logits = sums * inverse
    lanes = iota((ROWS, 128), 1)
    first = jnp.sum(jnp.where(lanes == routing_ref[:, 0:1], logits, 0.0), axis=1, keepdims=True)
    second = jnp.sum(jnp.where(lanes == routing_ref[:, 1:2], logits, 0.0), axis=1, keepdims=True)
    top = jnp.maximum(first, second)
    first, second = jnp.exp(first - top), jnp.exp(second - top)
    gate_ref[...] = jnp.where(iota((ROWS, 2), 1) == 0, first, second) / (first + second)

    for copy in x_copies + z_copies + g_copies + h_copies + page_copies:
        copy.wait_send()
    for d in range(1, NG):
        @pl.when(grp + d < NG)
        def _(d=d):
            place = {"grp": grp + d}
            remote(seg_out, seg_all.at[grp], sg_s.at[d], sg_r.at[grp], place).wait_send()
            remote(pair_ref, kv_all.at[grp], kv_s.at[d], kv_r.at[grp], place).wait_send()
    for o in range(NG):
        remote(outgoing.at[0], pages_ref.at[o], pg_s.at[0], pg_r.at[o], place_p[0]).wait_recv()


def spread_b(bc):
    pick = (iota((256, 2 * NST), 0) % NST == iota((256, 2 * NST), 1)).astype(BF16)
    return dot_t(pick, bc)


def forcing(block, b_tiled, driven):
    mine = iota((256, ROWS), 1) == block * 16 + iota((256, ROWS), 0) // NST
    return dot(jnp.where(mine, b_tiled, 0.0).astype(BF16), driven)


def end_kernel(
    rank_ref, dt_ref, dt_bias_ref, a_log_ref, xconv_ref, bc_ref, start_ref,
    step_ref, driven_ref, ends_ref,
    b_tiled, forced,
):
    raw = dot(rank_ref[...], dt_ref[...]) + dt_bias_ref[...]
    step = jnp.maximum(raw, 0.0) + jnp.log(1.0 + jnp.exp(-jnp.abs(raw)))
    driven_ref[...] = (step * xconv_ref[...].astype(F32)).astype(BF16)
    for lane in range(0, WIDTH, 128):
        step_ref[:, lane : lane + 128] = step[:, lane : lane + 128] + start_ref[...]
    b_tiled[...] = spread_b(bc_ref[...])
    rate = jnp.exp(a_log_ref[...]) * (-LOG2E)

    def block(b, state):
        forced[...] = forcing(b, b_tiled[...], driven_ref[...])
        steps = step_ref[pl.ds(pl.multiple_of(b * 16, 16), 16), :]
        for t in range(16):
            state = jnp.exp2(steps[t : t + 1, :] * rate) * state + forced[NST * t : NST * (t + 1), :]
        return state

    ends_ref[0:NST, :] = lax.fori_loop(0, ROWS // 16, block, jnp.zeros((NST, WIDTH), F32))
    ends_ref[NST:, :] = jnp.broadcast_to(jnp.sum(step_ref[...], axis=0, keepdims=True), (8, WIDTH))


def hand_kernel(
    ends_ref, a_log_ref,
    state_ref, final_ref,
    ends, own, landed,
    es, er, fs, fr,
):
    sect, grp = lax.axis_index("sect"), lax.axis_index("grp")
    others = [lax.rem(grp + d, NG) for d in range(1, NG)]
    places = [{"grp": o} for o in others]
    across = {"sect": 1 - sect}
    greet(places + [across])
    copies = []
    for d, place in enumerate(places):
        copies.append(remote(ends_ref, ends.at[grp], es.at[d], er.at[grp], place))
    for copy in copies:
        copy.start()
    ends[grp] = ends_ref[...]
    rate = jnp.exp(a_log_ref[...]) * (-LOG2E)
    for o in others:
        remote(ends_ref, ends.at[o], es.at[0], er.at[o], places[0]).wait_recv()
    state = jnp.zeros((NST, WIDTH), F32)
    mine = state
    for j in range(NG):
        mine = jnp.where(grp == j, state, mine)
        state = jnp.exp2(ends[j, NST : NST + 1, :] * rate) * state + ends[j, 0:NST, :]
    state_ref[...] = mine
    for k in range(NG):
        own[k] = jnp.concatenate([state[2 * k : 2 * k + 2], jnp.zeros((6, WIDTH), F32)], axis=0)
    copy = remote(own.at[grp], landed, fs, fr, across)
    copy.start()
    copy.wait()
    final_ref[...] = landed[0:2, :]
    for copy in copies:
        copy.wait_send()


def out_kernel(
    step_ref, driven_ref, a_log_ref, xconv_ref, bc_ref, z_ref, skip_ref, state_ref,
    mixed_ref,
    b_tiled, c_blocks, forced, states,
):
    b_tiled[...] = spread_b(bc_ref[...])
    pick = (iota((2 * NST, 256), 0) == NST + iota((2 * NST, 256), 1) % NST).astype(BF16)
    own = iota((ROWS, 256), 1) // NST == iota((ROWS, 256), 0) % 16
    c_blocks[...] = jnp.where(own, dot(bc_ref[...], pick), 0.0).astype(BF16)
    rate = jnp.exp(a_log_ref[...]) * (-LOG2E)

    def block(b, state):
        forced[...] = forcing(b, b_tiled[...], driven_ref[...])
        rows = pl.ds(pl.multiple_of(b * 16, 16), 16)
        steps = step_ref[rows, :]
        for t in range(16):
            state = jnp.exp2(steps[t : t + 1, :] * rate) * state + forced[NST * t : NST * (t + 1), :]
            states[NST * t : NST * (t + 1), :] = state.astype(BF16)
        rows_out = dot(c_blocks[rows, :], states[...])
        gate = z_ref[rows, :].astype(F32)
        gate = gate / (1.0 + jnp.exp(-gate))
        mixed_ref[rows, :] = ((rows_out + skip_ref[...] * xconv_ref[rows, :].astype(F32)) * gate).astype(BF16)
        return state

    lax.fori_loop(0, ROWS // 16, block, state_ref[...])


def params(collective=None):
    if collective is None:
        return pltpu.CompilerParams(vmem_limit_bytes=48 << 20)
    return pltpu.CompilerParams(vmem_limit_bytes=48 << 20, collective_id=collective, has_side_effects=True)


def local(
    mamba_x, mamba_z, conv_weight, conv_bias, x_proj, norm_gain, dt_proj, dt_bias, a_log, d_skip,
    segment_ids, queries, keys_values, kv_owner, moe_in, moe_gain, router, routing,
):
    tp = lax.axis_index("tp")

    def own_pair(index):
        return lax.dynamic_slice_in_dim(keys_values, index * HD, HD, 2).reshape(ROWS, 2 * HD)

    pair = own_pair(tp // 4)
    page_rows = own_pair((tp // NZ) * 2 + (NZ - 1 - tp % NZ) // 4)
    owners = kv_owner[0, :, 0]
    order = jnp.arange(16)
    before = (owners[None, :] == owners[:, None]) & (order[None, :] < order[:, None])
    targets = owners * SLOTS + jnp.sum(before.astype(I32), axis=1)
    targets = jnp.broadcast_to(targets[:, None], (16, BLK)).reshape(1, ROWS)

    shape = jax.ShapeDtypeStruct
    dma = pltpu.SemaphoreType.DMA
    xconv, rank, bc, start, attn_out, pages, expert_input, gates = pl.pallas_call(
        mix_kernel,
        out_shape=(
            shape((ROWS, WIDTH), BF16),
            shape((ROWS, RANK), BF16),
            shape((ROWS, 2 * NST), BF16),
            shape((ROWS, 128), F32),
            shape((ROWS, 256), BF16),
            shape((NG, 64, 256), BF16),
            shape((ROWS, 256), BF16),
            shape((ROWS, 2), F32),
        ),
        in_specs=[VMEM] * 15,
        out_specs=(VMEM, VMEM, VMEM, VMEM, VMEM, ANY, VMEM, VMEM),
        scratch_shapes=[
            pltpu.VMEM((16, WIDTH), BF16),
            pltpu.VMEM((8, 128), I32),
            pltpu.VMEM((8, 128), I32),
            pltpu.VMEM((8, ROWS), I32),
            pltpu.VMEM((NG, 8, ROWS), I32),
            pltpu.VMEM((NG, ROWS, 256), BF16),
            pltpu.VMEM((8 + ROWS, WIDTH), F32),
            pltpu.VMEM((8 + ROWS, 128), I32),
            pltpu.VMEM((ROWS, PAY), BF16),
            pltpu.VMEM((NX, 64, PAY), BF16),
            pltpu.VMEM((NZ, 16, HALF), BF16),
            pltpu.VMEM((NZ, 16, HALF), BF16),
            pltpu.VMEM((16, HALF), BF16),
            pltpu.VMEM((NX, NZ, 16, HALF), BF16),
            pltpu.VMEM((NG, 64, 256), BF16),
            pltpu.VMEM((2, ROWS, 128), F32),
            pltpu.VMEM((2, ROWS, 128), F32),
            pltpu.VMEM((2, ROWS, 128), F32),
            dma, dma, dma, dma,
            dma((NG,)), dma((NG,)), dma((NG,)), dma((NG,)), dma((NG,)), dma((NG,)),
            dma((NX,)), dma((NX,)), dma((NZ,)), dma((NZ,)), dma((NZ,)), dma((NZ,)), dma((NX,)), dma((NX,)),
        ],
        compiler_params=params(0),
        name="mix",
    )(
        mamba_x, segment_ids.reshape(ROWS, 1), segment_ids, conv_weight, conv_bias.reshape(1, WIDTH), x_proj,
        norm_gain.reshape(1, -1), queries, pair, page_rows, targets, moe_in, moe_gain.reshape(1, 256), router,
        routing,
    )
    step, driven, ends = pl.pallas_call(
        end_kernel,
        out_shape=(shape((ROWS, WIDTH), F32), shape((ROWS, WIDTH), BF16), shape((NST + 8, WIDTH), F32)),
        in_specs=[VMEM] * 7,
        out_specs=(VMEM,) * 3,
        scratch_shapes=[pltpu.VMEM((256, ROWS), F32), pltpu.VMEM((256, WIDTH), F32)],
        compiler_params=params(),
        name="ends",
    )(rank, dt_proj, dt_bias.reshape(1, WIDTH), a_log, xconv, bc, start)
    state, final = pl.pallas_call(
        hand_kernel,
        out_shape=(shape((NST, WIDTH), F32), shape((2, WIDTH), F32)),
        in_specs=[VMEM] * 2,
        out_specs=(VMEM,) * 2,
        scratch_shapes=[
            pltpu.VMEM((NG, NST + 8, WIDTH), F32),
            pltpu.VMEM((NG, 8, WIDTH), F32),
            pltpu.VMEM((8, WIDTH), F32),
            dma((NG,)), dma((NG,)), dma, dma,
        ],
        compiler_params=params(1),
        name="hand",
    )(ends, a_log)
    mixed = pl.pallas_call(
        out_kernel,
        out_shape=shape((ROWS, WIDTH), BF16),
        in_specs=[VMEM] * 8,
        out_specs=VMEM,
        scratch_shapes=[
            pltpu.VMEM((256, ROWS), F32),
            pltpu.VMEM((ROWS, 256), BF16),
            pltpu.VMEM((256, WIDTH), F32),
            pltpu.VMEM((256, WIDTH), BF16),
        ],
        compiler_params=params(),
        name="out",
    )(step, driven, a_log, xconv, bc, mamba_z, d_skip.reshape(1, WIDTH), state)
    kv_pages = pages.reshape(1, 1, 1, NG * SLOTS, BLK, 2 * HD)
    return (mixed, final[None], attn_out, kv_pages, expert_input, gates)


def solution(mesh):
    placed = (
        P(("sect", "grp"), "tp"),
        P(("sect", "grp"), "tp"),
        P(None, "tp"),
        P("tp"),
        P("tp", None),
        P(),
        P(None, "tp"),
        P("tp"),
        P(None, "tp"),
        P("tp"),
        P("sect", "grp"),
        P(("sect", "grp"), "tp"),
        P(("sect", "grp"), None, None),
        P("sect", "grp", None),
        P(("sect", "grp"), "tp"),
        P("tp"),
        P("tp", None),
        P(("sect", "grp"), None),
    )
    return jax.shard_map(
        local,
        mesh=mesh,
        in_specs=placed,
        out_specs=(
            P(("sect", "grp"), "tp"),
            P("sect", "grp", "tp"),
            P(("sect", "grp"), "tp"),
            P("sect", "grp", "tp", None, None, None),
            P(("sect", "grp"), "tp"),
            P(("sect", "grp"), None),
        ),
        check_vma=False,
    )
```

```python
import jax
import jax.numpy as jnp
from jax import lax
from jax.experimental import pallas as pl
from jax.experimental.pallas import tpu as pltpu
from jax.sharding import PartitionSpec as P

MESH = pl.DeviceIdType.MESH
F32 = jnp.float32
BF16 = jnp.bfloat16
I32 = jnp.int32

ROWS = 256
WIDTH = 512
RANK = 512
NST = 16
HD = 128
BLK = 16
LANES = 128
NX, NZ, NG = 4, 8, 8
PAY = 768
HALF = PAY // 2
SLOTS = 4
FEATURES = 8192
EPS = 1e-06
LOG2E = 1.4426950408889634
HUGE = 1e30
VMEM = pl.BlockSpec(memory_space=pltpu.VMEM)
ANY = pl.BlockSpec(memory_space=pl.ANY)
DMA = pltpu.SemaphoreType.DMA


def iota(shape, dim):
    return lax.broadcasted_iota(I32, shape, dim)


def dot(a, b, **kw):
    return jnp.dot(a, b, preferred_element_type=F32, **kw)


def dot_t(a, b, **kw):
    return lax.dot_general(a, b, (((1,), (1,)), ((), ())), preferred_element_type=F32, **kw)


def remote(src, dst, send, recv, where):
    return pltpu.make_async_remote_copy(
        src_ref=src, dst_ref=dst, send_sem=send, recv_sem=recv, device_id=where, device_id_type=MESH
    )


INPUTS = (
    ("x", (ROWS, WIDTH), BF16),
    ("seg", (1, ROWS), I32),
    ("conv_w", (4, WIDTH), F32),
    ("conv_b", (1, WIDTH), F32),
    ("proj", (RANK + 2 * NST, WIDTH), BF16),
    ("owner", (1, 16), I32),
    ("page", (ROWS, 2, HD), BF16),
    ("pair", (ROWS, 2, HD), BF16),
    ("moe", (ROWS, 256), BF16),
    ("moe_gain", (1, 256), F32),
    ("router", (16, 256), BF16),
    ("q", (ROWS, 2 * HD), BF16),
    ("z", (ROWS, WIDTH), BF16),
    ("gain", (1, RANK + 2 * NST), F32),
    ("dt", (RANK, WIDTH), BF16),
    ("dt_bias", (1, WIDTH), F32),
    ("a_log", (NST, WIDTH), F32),
    ("skip", (1, WIDTH), F32),
    ("routing", (2, ROWS), I32),
)
OUTPUTS = (
    ("mixed", (ROWS, WIDTH), BF16),
    ("final", (2, WIDTH), F32),
    ("attn", (ROWS, 2 * HD), BF16),
    ("pages", (NG, SLOTS, BLK, 2 * HD), BF16),
    ("expert", (ROWS, 256), BF16),
    ("gate", (2, ROWS), F32),
)
OPERANDS = [n for n, _, _ in INPUTS if n not in ("page", "pair")] + ["keys_values"]
SCRATCH = (
    ("page", (ROWS, 2 * HD), BF16),
    ("pair", (ROWS, 2 * HD), BF16),
    ("rim", (16, WIDTH), BF16),
    ("rim_seg", (8, LANES), F32),
    ("seg_send", (8, LANES), F32),
    ("seg_out", (8, ROWS), F32),
    ("seg_all", (NG, 8, ROWS), F32),
    ("kv_all", (NG, ROWS, 2 * HD), BF16),
    ("ext", (8 + ROWS, WIDTH), F32),
    ("ext_seg", (8 + ROWS, LANES), F32),
    ("conv", (ROWS, WIDTH), BF16),
    ("pay", (ROWS, PAY), BF16),
    ("rx", (2, NX, 64, HALF), BF16),
    ("chunk", (NZ, 16, HALF), BF16),
    ("rz", (NZ, 16, HALF), BF16),
    ("low", (NX, NZ, 16, HALF), BF16),
    ("outgoing", (NG, BLK, 2 * HD), BF16),
    ("best", (2, ROWS, LANES), F32),
    ("accum", (2, ROWS, 2 * HD), F32),
    ("silu_z", (ROWS, WIDTH), F32),
    ("rank", (ROWS, RANK), BF16),
    ("bc", (ROWS, 2 * NST), BF16),
    ("step", (ROWS, WIDTH), F32),
    ("driven", (ROWS, WIDTH), BF16),
    ("b_tiled", (256, ROWS), F32),
    ("c_blocks", (ROWS, 256), BF16),
    ("forced", (256, WIDTH), F32),
    ("states", (256, WIDTH), BF16),
    ("growth", (16, 256, WIDTH), BF16),
    ("rows_out", (ROWS, WIDTH), F32),
    ("ends", (NG, 80, LANES), BF16),
    ("own_end", (80, LANES), BF16),
    ("own_final", (NG, 8, LANES), F32),
    ("landed", (8, LANES), F32),
)
SEMS = (
    ("load", (len(INPUTS),)), ("store", (len(OUTPUTS),)),
    ("rim_s", ()), ("rim_r", ()), ("rseg_s", ()), ("rseg_r", ()),
    ("kv_s", (NG,)), ("kv_r", (NG,)), ("sg_s", (NG,)), ("sg_r", (NG,)),
    ("pg_s", (NG,)), ("pg_r", (NG,)), ("pf_s", (4,)), ("pf_r", (4,)),
    ("x_s", (2, NX)), ("x_r", (2, NX)), ("z_s", (NZ,)), ("z_r", (NZ,)),
    ("g_s", (NZ,)), ("g_r", (NZ,)), ("h_s", (NZ, NX)), ("h_r", (NX, NZ)),
    ("e_s", (NG,)), ("e_r", (NG,)), ("f_s", ()), ("f_r", ()),
)


class Refs:
    pass


def main_kernel(*refs):
    k = Refs()
    names = ["hbm_" + n for n in OPERANDS] + ["hbm_out_" + n for n, _, _ in OUTPUTS]
    names += [n for n, _, _ in SCRATCH] + ["in_" + n for n, _, _ in INPUTS]
    names += ["out_" + n for n, _, _ in OUTPUTS if n != "pages"] + [n for n, _ in SEMS]
    for name, ref in zip(names, refs, strict=True):
        setattr(k, name, ref)
    k.out_pages = k.hbm_out_pages
    sect, tp, grp = lax.axis_index("sect"), lax.axis_index("tp"), lax.axis_index("grp")
    x, z = tp // NZ, tp % NZ
    heads = {"pair": tp // 4, "page": 2 * x + (NZ - 1 - z) // 4}
    loads = {}
    for i, (n, _, _) in enumerate(INPUTS):
        if n in heads:
            src = k.hbm_keys_values.at[:, :, pl.ds(pl.multiple_of(heads[n] * HD, HD), HD)]
        else:
            src = getattr(k, "hbm_" + n)
        loads[n] = pltpu.make_async_copy(src, getattr(k, "in_" + n), k.load.at[i])
        loads[n].start()
    stores = {}
    for i, (n, _, _) in enumerate(OUTPUTS):
        if n != "pages":
            stores[n] = pltpu.make_async_copy(getattr(k, "out_" + n), getattr(k, "hbm_out_" + n), k.store.at[i])

    quad = z // 4 * 4
    others_x = [lax.rem(x + d, NX) for d in range(1, NX)]
    others_z = [lax.rem(z + d, NZ) for d in range(1, NZ)]
    others_q = [quad + lax.rem(z + d, 4) for d in range(1, 4)]
    others_g = [lax.rem(grp + d, NG) for d in range(1, NG)]
    place_x = [{"tp": o * NZ + z} for o in others_x]
    place_z = [{"tp": x * NZ + o} for o in others_z]
    place_q = [{"tp": x * NZ + o} for o in others_q]
    place_g = [{"grp": o} for o in others_g]
    place_p = [{"sect": 1 - sect, "tp": x * NZ + (NZ - 1 - z), "grp": o} for o in range(NG)]
    across = {"sect": 1 - sect}
    partners = place_x + place_z + place_g + place_p + [across]
    barrier = pltpu.get_barrier_semaphore()
    for place in partners:
        pl.semaphore_signal(barrier, inc=1, device_id=place, device_id_type=MESH)

    loads["seg"].wait()
    seg_row = k.in_seg[...].astype(F32)
    seg_cols = jnp.broadcast_to(seg_row, (LANES, ROWS)).T
    k.ext_seg[8:, :] = seg_cols
    k.ext_seg[0:8, :] = jnp.full((8, LANES), -1.0, F32)
    k.seg_send[...] = seg_cols[ROWS - 8 :, :]
    k.seg_out[...] = jnp.broadcast_to(seg_row, (8, ROWS))
    loads["x"].wait()
    k.ext[8:, :] = k.in_x[...].astype(F32)
    k.ext[0:8, :] = jnp.zeros((8, WIDTH), F32)
    loads["conv_w"].wait()
    loads["conv_b"].wait()

    def convolve(count):
        here = k.ext_seg[8 : 8 + count, :]
        same = [k.ext_seg[5 + i : 5 + i + count, :] == here for i in range(3)]
        for lane in range(0, WIDTH, LANES):
            cols = slice(lane, lane + LANES)
            value = jnp.broadcast_to(k.in_conv_b[:, cols], (count, LANES))
            for i in range(4):
                term = k.ext[5 + i : 5 + i + count, cols] * k.in_conv_w[i : i + 1, cols]
                value = value + (jnp.where(same[i], term, 0.0) if i < 3 else term)
            k.conv[0:count, cols] = (value / (1.0 + jnp.exp(-value))).astype(BF16)

    def project(count):
        rows = k.conv[0:count, :]
        k.pay[0:count, 0:RANK] = dot_t(rows, k.in_proj[0:RANK, :]).astype(BF16)
        k.pay[0:count, RANK : RANK + 2 * NST] = dot_t(rows, k.in_proj[RANK:, :]).astype(BF16)

    convolve(ROWS)
    loads["moe"].wait()
    loads["moe_gain"].wait()
    loads["router"].wait()
    moe_rows = k.in_moe[...].astype(F32)
    spread = (iota((LANES, 16), 0) == iota((LANES, 16), 1)).astype(BF16)
    router = dot(spread, k.in_router[...])
    logits_part = dot_t(moe_rows * k.in_moe_gain[...], router, precision=lax.Precision.HIGHEST)
    squares = jnp.sum(moe_rows * moe_rows, axis=1, keepdims=True)
    tail = jnp.where(iota((ROWS, LANES), 1) == 16, squares, logits_part)
    k.pay[:, 640:768] = tail.astype(BF16)
    k.pay[:, 512:640] = jnp.zeros((ROWS, LANES), BF16)
    loads["proj"].wait()
    project(ROWS)

    loads["owner"].wait()
    loads["page"].wait()
    owners = jnp.broadcast_to(k.in_owner[...].astype(F32), (8, 16)).astype(BF16)
    owner_of = dot(owners, (iota((16, ROWS), 0) == iota((16, ROWS), 1) // BLK).astype(BF16))[0:1, :]
    owner_lanes = dot(owners, (iota((16, LANES), 0) == iota((16, LANES), 1)).astype(BF16))[0:1, :]
    owner_rows = jnp.broadcast_to(owner_lanes, (LANES, LANES)).T[0:16, 0:1]
    before = (owner_rows == owner_of) & (iota((16, ROWS), 0) < iota((16, ROWS), 1) // BLK)
    order = jnp.sum(jnp.where(before, 1.0, 0.0), axis=0, keepdims=True)
    slot = jnp.where(order == lax.rem(z, 4).astype(F32), owner_of, -1.0)
    row, col = iota((NG * BLK, ROWS), 0), iota((NG * BLK, ROWS), 1)
    choose = (slot == (row // BLK).astype(F32)) & (row % BLK == col % BLK)
    k.page[...] = k.in_page[...].reshape(ROWS, 2 * HD)
    chosen = dot(jnp.where(choose, 1.0, 0.0).astype(BF16), k.page[...])
    k.outgoing[...] = chosen.astype(BF16).reshape(NG, BLK, 2 * HD)
    loads["pair"].wait()
    k.pair[...] = k.in_pair[...].reshape(ROWS, 2 * HD)
    pl.semaphore_wait(barrier, len(partners))

    behind = {"grp": lax.rem(grp + 1, NG)}
    rim_copy = remote(k.in_x.at[ROWS - 16 : ROWS], k.rim, k.rim_s, k.rim_r, behind)
    rseg_copy = remote(k.seg_send, k.rim_seg, k.rseg_s, k.rseg_r, behind)
    rim_copy.start()
    rseg_copy.start()

    x_copies = {}
    for h in range(2):
        for d, (o, place) in enumerate(zip(others_x, place_x)):
            src = k.pay.at[pl.ds(pl.multiple_of(o * 64, 64), 64), HALF * h : HALF * (h + 1)]
            x_copies[h, d] = remote(src, k.rx.at[h, x], k.x_s.at[h, d], k.x_r.at[h, x], place)
    for (h, d), copy in x_copies.items():
        pl.when(others_x[d] != 0)(copy.start)

    kv_copies = []
    for d in range(1, NG):
        place = {"grp": lax.rem(grp + d, NG)}
        kv_copies.append(remote(k.seg_out, k.seg_all.at[grp], k.sg_s.at[d], k.sg_r.at[grp], place))
        kv_copies.append(remote(k.pair, k.kv_all.at[grp], k.kv_s.at[d], k.kv_r.at[grp], place))
    for i, copy in enumerate(kv_copies):
        pl.when(grp + i // 2 + 1 < NG)(copy.start)

    my_slot, their_slot = lax.rem(z, 4), 3 - lax.rem(z, 4)
    page_copies = []
    for o in range(NG):
        dst = k.out_pages.at[grp, my_slot]
        page_copies.append(remote(k.outgoing.at[o], dst, k.pg_s.at[o], k.pg_r.at[grp], place_p[o]))
    for copy in page_copies:
        copy.start()

    rim_copy.wait()
    rseg_copy.wait()
    k.ext[0:8, :] = k.rim[8:16, :].astype(F32)
    k.ext_seg[0:8, :] = jnp.where(grp == 0, -1.0, k.rim_seg[...])
    convolve(16)
    project(16)
    for (h, d), copy in x_copies.items():
        pl.when(others_x[d] == 0)(copy.start)

    factor = HD**-0.5 * LOG2E

    ones = jnp.ones((ROWS, HD), BF16)

    def attend(key_block, value_block, allowed, first):
        valued = jnp.concatenate([value_block, ones], axis=1)
        for h in range(2):
            scores = dot_t(k.in_q[:, h * HD : (h + 1) * HD], key_block)
            masked = jnp.where(allowed, scores, -HUGE)
            high = jnp.max(masked, axis=1, keepdims=True)
            if first:
                new = high
                weights = jnp.exp2((masked - new) * factor)
                k.accum[h] = dot(weights.astype(BF16), valued)
            else:
                old = k.best[h][:, 0:1]
                new = jnp.maximum(old, high)
                weights = jnp.exp2((masked - new) * factor)
                fade = jnp.exp2((old - new) * factor)
                k.accum[h] = k.accum[h] * fade + dot(weights.astype(BF16), valued)
            k.best[h] = jnp.broadcast_to(new, (ROWS, LANES))

    def earlier(i, carry):
        j = grp - 1 - i
        remote(k.seg_out, k.seg_all.at[j], k.sg_s.at[0], k.sg_r.at[j], place_g[0]).wait_recv()
        remote(k.pair, k.kv_all.at[j], k.kv_s.at[0], k.kv_r.at[j], place_g[0]).wait_recv()
        same = k.seg_all[j, 0:1, :] == k.ext_seg[8:, 0:1]
        attend(k.kv_all[j, :, 0:HD], k.kv_all[j, :, HD:], same, False)
        return carry

    def attend_up_to(first, last):
        lax.fori_loop(jnp.minimum(grp, first), jnp.minimum(grp, last), earlier, 0)

    loads["q"].wait()
    causal = iota((ROWS, ROWS), 1) <= iota((ROWS, ROWS), 0)
    attend(k.pair[:, 0:HD], k.pair[:, HD:], causal & (seg_row == k.ext_seg[8:, 0:1]), True)
    attend_up_to(0, 1)

    z_copies = [
        remote(k.chunk.at[o], k.rz.at[z], k.z_s.at[o], k.z_r.at[z], {"tp": x * NZ + o}) for o in range(NZ)
    ]
    for h in range(2):
        for o in others_x:
            remote(k.rx.at[h, o], k.rx.at[h, o], k.x_s.at[h, 0], k.x_r.at[h, o], place_x[0]).wait_recv()
        summed = k.pay[pl.ds(pl.multiple_of(x * 64, 64), 64), HALF * h : HALF * (h + 1)].astype(F32)
        for o in others_x:
            summed = summed + k.rx[h, o].astype(F32)
        for r in range(4):
            k.chunk[4 * h + r] = summed[16 * r : 16 * r + 16, :].astype(BF16)
        for r in range(4):
            pl.when(z != 4 * h + r)(z_copies[4 * h + r].start)

    loads["z"].wait()
    gate = k.in_z[...].astype(F32)
    k.silu_z[...] = gate / (1.0 + jnp.exp(-gate))

    attend_up_to(1, 2)

    for o in others_z:
        remote(k.chunk.at[0], k.rz.at[o], k.z_s.at[0], k.z_r.at[o], place_z[0]).wait_recv()
    summed = k.chunk[z].astype(F32)
    for o in others_z:
        summed = summed + k.rz[o].astype(F32)
    k.low[x, z] = summed.astype(BF16)
    g_copies = []
    for d, place in enumerate(place_z):
        g_copies.append(remote(k.low.at[x, z], k.low.at[x, z], k.g_s.at[d], k.g_r.at[z], place))
    for copy in g_copies:
        copy.start()
    h_copies = []

    def forward(o):
        for d, place in enumerate(place_x):
            copy = remote(k.low.at[x, o], k.low.at[x, o], k.h_s.at[o, d], k.h_r.at[x, o], place)
            copy.start()
            h_copies.append(copy)

    forward(z)
    for o in others_z:
        remote(k.low.at[x, z], k.low.at[x, o], k.g_s.at[0], k.g_r.at[o], place_z[0]).wait_recv()
        forward(o)

    for o in range(NG):
        remote(k.outgoing.at[0], k.out_pages.at[o, their_slot], k.pg_s.at[0], k.pg_r.at[o], place_p[0]).wait_recv()
    f_copies = []
    for d, place in enumerate(place_q):
        mine = k.out_pages.at[:, their_slot]
        f_copies.append(remote(mine, mine, k.pf_s.at[d], k.pf_r.at[their_slot], place))
    for copy in f_copies:
        copy.start()

    attend_up_to(2, 4)

    for n in ("gain", "dt", "dt_bias", "a_log", "skip", "routing"):
        loads[n].wait()
    for o in others_x:
        for p in range(NZ):
            remote(k.low.at[x, p], k.low.at[o, p], k.h_s.at[0, 0], k.h_r.at[o, p], place_x[0]).wait_recv()
    left = k.low[:, 0:4].reshape(ROWS, HALF).astype(F32)
    right = k.low[:, 4:8].reshape(ROWS, HALF).astype(F32)
    mean = jnp.sum(left * left, axis=1, keepdims=True) + jnp.sum(right[:, :128] * right[:, :128], axis=1, keepdims=True)
    scale = lax.rsqrt(mean / RANK + EPS)
    k.rank[:, 0:HALF] = (left * scale * k.in_gain[:, 0:HALF]).astype(BF16)
    k.rank[:, HALF:RANK] = (right[:, :128] * scale * k.in_gain[:, HALF:RANK]).astype(BF16)
    both = right[:, 128 : 128 + 2 * NST]
    is_b = iota((ROWS, 2 * NST), 1) < NST
    power = both * both
    mean_b = jnp.sum(jnp.where(is_b, power, 0.0), axis=1, keepdims=True) / NST
    mean_c = jnp.sum(jnp.where(is_b, 0.0, power), axis=1, keepdims=True) / NST
    scale = jnp.where(is_b, lax.rsqrt(mean_b + EPS), lax.rsqrt(mean_c + EPS))
    k.bc[...] = (both * scale * k.in_gain[:, RANK : RANK + 2 * NST]).astype(BF16)

    raw = dot(k.rank[...], k.in_dt[...]) + k.in_dt_bias[...]
    step = jnp.maximum(raw, 0.0) + jnp.log(1.0 + jnp.exp(-jnp.abs(raw)))
    k.driven[...] = (step * k.conv[...].astype(F32)).astype(BF16)
    start = jnp.where(k.ext_seg[7 : 7 + ROWS, :] != k.ext_seg[8:, :], HUGE, 0.0)
    for lane in range(0, WIDTH, LANES):
        k.step[:, lane : lane + LANES] = step[:, lane : lane + LANES] + start
    pick = (iota((256, 2 * NST), 0) % NST == iota((256, 2 * NST), 1)).astype(BF16)
    k.b_tiled[...] = dot_t(pick, k.bc[...])
    pick = (iota((2 * NST, 256), 0) == NST + iota((2 * NST, 256), 1) % NST).astype(BF16)
    own = iota((ROWS, 256), 1) // NST == iota((ROWS, 256), 0) % 16
    k.c_blocks[...] = jnp.where(own, dot(k.bc[...], pick), 0.0).astype(BF16)
    rate = jnp.exp(k.in_a_log[...]) * (-LOG2E)

    def scan(b, carry):
        state, left = carry
        mine = iota((256, ROWS), 1) == b * 16 + iota((256, ROWS), 0) // NST
        k.forced[...] = dot(jnp.where(mine, k.b_tiled[...], 0.0).astype(BF16), k.driven[...])
        rows = pl.ds(pl.multiple_of(b * 16, 16), 16)
        steps = k.step[rows, :]
        for t in range(16):
            span = slice(NST * t, NST * (t + 1))
            decay = jnp.exp2(steps[t : t + 1, :] * rate)
            state = decay * state + k.forced[span, :]
            left = decay * left
            k.states[span, :] = state.astype(BF16)
            k.growth[b, span, :] = left.astype(BF16)
        skipped = k.in_skip[...] * k.conv[rows, :].astype(F32)
        k.rows_out[rows, :] = dot(k.c_blocks[rows, :], k.states[...]) + skipped
        return state, left

    begin = (jnp.zeros((NST, WIDTH), F32), jnp.ones((NST, WIDTH), F32))
    state, _ = lax.fori_loop(0, ROWS // 16, scan, begin)
    steps = jnp.sum(k.step[...], axis=0, keepdims=True)
    for i in range(4):
        k.own_end[NST * i : NST * (i + 1), :] = state[:, i * LANES : (i + 1) * LANES].astype(BF16)
    parts = []
    for _ in range(3):
        part = steps.astype(BF16).astype(F32)
        parts += [part[:, i * LANES : (i + 1) * LANES] for i in range(4)]
        steps = steps - part
    k.own_end[64:80, :] = jnp.concatenate(parts + [jnp.zeros((4, LANES), F32)], axis=0).astype(BF16)
    e_copies = []
    for d, place in enumerate(place_g):
        e_copies.append(remote(k.own_end, k.ends.at[grp], k.e_s.at[d], k.e_r.at[grp], place))
    for copy in e_copies:
        copy.start()
    k.ends[grp] = k.own_end[...]

    attend_up_to(4, NG)
    for h in range(2):
        k.out_attn[:, h * HD : (h + 1) * HD] = (k.accum[h, :, 0:HD] / k.accum[h, :, HD:]).astype(BF16)
    stores["attn"].start()
    sums = right[:, 256:384]
    inverse = lax.rsqrt(sums[:, 16:17] / FEATURES + EPS)
    k.out_expert[...] = (k.in_moe[...].astype(F32) * k.in_moe_gain[...] * inverse).astype(BF16)
    logits = (sums * inverse).T
    experts = iota((LANES, ROWS), 0)
    first = jnp.sum(jnp.where(experts == k.in_routing[0:1, :], logits, 0.0), axis=0, keepdims=True)
    second = jnp.sum(jnp.where(experts == k.in_routing[1:2, :], logits, 0.0), axis=0, keepdims=True)
    top = jnp.maximum(first, second)
    first, second = jnp.exp(first - top), jnp.exp(second - top)
    k.out_gate[0:1, :] = first / (first + second)
    k.out_gate[1:2, :] = second / (first + second)
    stores["expert"].start()
    stores["gate"].start()

    for o in others_g:
        remote(k.own_end, k.ends.at[o], k.e_s.at[0], k.e_r.at[o], place_g[0]).wait_recv()
    sums_of = []
    for j in range(NG):
        part = k.ends[j, 64:80, :].astype(F32)
        sums_of.append(part[0:4] + part[4:8] + part[8:12])
    entering = []
    for i in range(4):
        cols = slice(i * LANES, (i + 1) * LANES)
        state = jnp.zeros((NST, LANES), F32)
        mine = state
        for j in range(NG):
            mine = jnp.where(grp == j, state, mine)
            kept = jnp.exp2(sums_of[j][i : i + 1, :] * rate[:, cols])
            state = kept * state + k.ends[j, NST * i : NST * (i + 1), :].astype(F32)
        entering.append(mine)
        for g in range(NG):
            k.own_final[g, 2 * i : 2 * i + 2, :] = state[2 * g : 2 * g + 2, :]
    final_copy = remote(k.own_final.at[grp], k.landed, k.f_s, k.f_r, across)
    final_copy.start()
    entering = jnp.concatenate(entering, axis=1).astype(BF16)

    def finish(b, carry):
        rows = pl.ds(pl.multiple_of(b * 16, 16), 16)
        grown = k.growth[b].reshape(16, NST, WIDTH) * entering[None]
        value = k.rows_out[rows, :] + dot(k.c_blocks[rows, :], grown.reshape(256, WIDTH))
        k.out_mixed[rows, :] = (value * k.silu_z[rows, :]).astype(BF16)
        return carry

    lax.fori_loop(0, ROWS // 16, finish, 0)
    stores["mixed"].start()

    final_copy.wait()
    for i in range(4):
        k.out_final[:, i * LANES : (i + 1) * LANES] = k.landed[2 * i : 2 * i + 2, :]
    stores["final"].start()
    for o in others_q:
        theirs = k.out_pages.at[:, 3 - lax.rem(o, 4)]
        remote(theirs, theirs, k.pf_s.at[0], k.pf_r.at[3 - lax.rem(o, 4)], place_q[0]).wait_recv()
    for copy in list(x_copies.values()) + g_copies + h_copies + page_copies + f_copies + e_copies:
        copy.wait_send()
    for o in range(NZ):
        pl.when(z != o)(z_copies[o].wait_send)
    for i, copy in enumerate(kv_copies):
        pl.when(grp + i // 2 + 1 < NG)(copy.wait_send)
    for store in stores.values():
        store.wait()


def hand_out(*refs):
    count = len(OUTPUTS)
    source, target, stage = refs[:count], refs[count : 2 * count], refs[2 * count : 3 * count]
    read, write = refs[3 * count :]
    inward = [pltpu.make_async_copy(source[i], stage[i], read.at[i]) for i in range(count)]
    outward = [pltpu.make_async_copy(stage[i], target[i], write.at[i]) for i in range(count)]
    for copy in inward:
        copy.start()
    for i in range(count):
        inward[i].wait()
        outward[i].start()
    for copy in outward:
        copy.wait()


def local(
    mamba_x, mamba_z, conv_weight, conv_bias, x_proj, norm_gain, dt_proj, dt_bias, a_log, d_skip,
    segment_ids, queries, keys_values, kv_owner, moe_in, moe_gain, router, routing,
):
    inputs = dict(
        x=mamba_x, seg=segment_ids, conv_w=conv_weight, conv_b=conv_bias.reshape(1, -1), proj=x_proj.T,
        owner=kv_owner.reshape(1, -1), keys_values=keys_values, moe=moe_in, moe_gain=moe_gain.reshape(1, -1), router=router.T, q=queries,
        z=mamba_z, gain=norm_gain.reshape(1, -1), dt=dt_proj, dt_bias=dt_bias.reshape(1, -1), a_log=a_log,
        skip=d_skip.reshape(1, -1), routing=routing.T,
    )
    shapes = tuple(jax.ShapeDtypeStruct(s, t) for _, s, t in OUTPUTS)
    results = pl.pallas_call(
        main_kernel,
        out_shape=shapes,
        in_specs=[ANY] * len(OPERANDS),
        out_specs=tuple([ANY] * len(OUTPUTS)),
        scratch_shapes=[pltpu.VMEM(s, t) for _, s, t in SCRATCH]
        + [pltpu.VMEM(s, t) for _, s, t in INPUTS]
        + [pltpu.VMEM(s, t) for n, s, t in OUTPUTS if n != "pages"]
        + [DMA(s) if s else DMA for _, s in SEMS],
        compiler_params=pltpu.CompilerParams(
            vmem_limit_bytes=62 << 20, collective_id=0, has_side_effects=True
        ),
        name="span",
    )(*[inputs[n] for n in OPERANDS])
    mixed, final, attn, pages, expert, gates = pl.pallas_call(
        hand_out,
        out_shape=shapes,
        in_specs=[ANY] * len(OUTPUTS),
        out_specs=tuple([ANY] * len(OUTPUTS)),
        scratch_shapes=[pltpu.VMEM(s, t) for _, s, t in OUTPUTS] + [DMA((len(OUTPUTS),))] * 2,
        compiler_params=pltpu.CompilerParams(vmem_limit_bytes=62 << 20),
        name="results",
    )(*results)
    return (mixed, final[None], attn, pages.reshape(1, 1, 1, NG * SLOTS, BLK, 2 * HD), expert, gates.T)


def solution(mesh):
    placed = (
        P(("sect", "grp"), "tp"),
        P(("sect", "grp"), "tp"),
        P(None, "tp"),
        P("tp"),
        P("tp", None),
        P(),
        P(None, "tp"),
        P("tp"),
        P(None, "tp"),
        P("tp"),
        P("sect", "grp"),
        P(("sect", "grp"), "tp"),
        P(("sect", "grp"), None, None),
        P("sect", "grp", None),
        P(("sect", "grp"), "tp"),
        P("tp"),
        P("tp", None),
        P(("sect", "grp"), None),
    )
    return jax.shard_map(
        local,
        mesh=mesh,
        in_specs=placed,
        out_specs=(
            P(("sect", "grp"), "tp"),
            P("sect", "grp", "tp"),
            P(("sect", "grp"), "tp"),
            P("sect", "grp", "tp", None, None, None),
            P(("sect", "grp"), "tp"),
            P(("sect", "grp"), None),
        ),
        check_vma=False,
    )
```

```python
import jax
import jax.numpy as jnp
from jax import lax
from jax.experimental import pallas as pl
from jax.experimental.pallas import tpu as pltpu
from jax.sharding import PartitionSpec as P

MESH = pl.DeviceIdType.MESH
F32 = jnp.float32
BF16 = jnp.bfloat16
I32 = jnp.int32

ROWS = 256
WIDTH = 512
RANK = 512
NST = 16
HD = 128
BLK = 16
LANES = 128
NX, NZ, NG = 4, 8, 8
PAY = 768
HALF = PAY // 2
SLOTS = 4
FEATURES = 8192
EPS = 1e-06
LOG2E = 1.4426950408889634
HUGE = 1e30
VMEM = pl.BlockSpec(memory_space=pltpu.VMEM)
ANY = pl.BlockSpec(memory_space=pl.ANY)
DMA = pltpu.SemaphoreType.DMA


def iota(shape, dim):
    return lax.broadcasted_iota(I32, shape, dim)


def dot(a, b, **kw):
    return jnp.dot(a, b, preferred_element_type=F32, **kw)


def dot_t(a, b, **kw):
    return lax.dot_general(a, b, (((1,), (1,)), ((), ())), preferred_element_type=F32, **kw)


def remote(src, dst, send, recv, where):
    return pltpu.make_async_remote_copy(
        src_ref=src, dst_ref=dst, send_sem=send, recv_sem=recv, device_id=where, device_id_type=MESH
    )


INPUTS = (
    ("x", (ROWS, WIDTH), BF16),
    ("seg", (1, ROWS), I32),
    ("conv_w", (4, WIDTH), F32),
    ("conv_b", (1, WIDTH), F32),
    ("proj", (RANK + 2 * NST, WIDTH), BF16),
    ("owner", (1, 16), I32),
    ("page", (ROWS, 2, HD), BF16),
    ("pair", (ROWS, 2, HD), BF16),
    ("moe", (ROWS, 256), BF16),
    ("moe_gain", (1, 256), F32),
    ("router", (16, 256), BF16),
    ("q", (ROWS, 2 * HD), BF16),
    ("z", (ROWS, WIDTH), BF16),
    ("gain", (RANK + 2 * NST,), F32),
    ("dt", (RANK, WIDTH), BF16),
    ("dt_bias", (1, WIDTH), F32),
    ("a_log", (NST, WIDTH), F32),
    ("skip", (1, WIDTH), F32),
    ("routing", (2, ROWS), I32),
)
OUTPUTS = (
    ("mixed", (ROWS, WIDTH), BF16),
    ("final", (2, WIDTH), F32),
    ("attn", (ROWS, 2 * HD), BF16),
    ("pages", (NG, SLOTS, BLK, 2 * HD), BF16),
    ("expert", (ROWS, 256), BF16),
    ("gate", (2, ROWS), F32),
)
OPERANDS = [n for n, _, _ in INPUTS if n not in ("page", "pair")] + ["keys_values"]
SCRATCH = (
    ("page", (ROWS, 2 * HD), BF16),
    ("pair", (ROWS, 2 * HD), BF16),
    ("rim", (16, WIDTH), BF16),
    ("rim_seg", (8, LANES), F32),
    ("seg_send", (8, LANES), F32),
    ("seg_out", (8, ROWS), F32),
    ("seg_all", (NG, 8, ROWS), F32),
    ("kv_all", (NG, ROWS, 2 * HD), BF16),
    ("ext", (8 + ROWS, WIDTH), F32),
    ("ext_seg", (8 + ROWS, LANES), F32),
    ("conv", (ROWS, WIDTH), BF16),
    ("pay", (ROWS, PAY), BF16),
    ("rx", (2, NX, 64, HALF), BF16),
    ("chunk", (NZ, 16, HALF), BF16),
    ("rz", (NZ, 16, HALF), BF16),
    ("low", (NX, NZ, 16, HALF), BF16),
    ("outgoing", (NG, BLK, 2 * HD), BF16),
    ("best", (2, ROWS, LANES), F32),
    ("accum", (2, ROWS, 2 * HD), F32),
    ("silu_z", (ROWS, WIDTH), F32),
    ("rank", (ROWS, RANK), BF16),
    ("bc", (ROWS, 2 * NST), BF16),
    ("step", (ROWS, WIDTH), F32),
    ("driven", (ROWS, WIDTH), F32),
    ("b_cols", (16, NST, LANES), F32),
    ("c_blocks", (ROWS, 256), BF16),
    ("states", (16, 256, WIDTH), BF16),
    ("growth", (16, 256, WIDTH), BF16),
    ("ends", (NG, 80, LANES), BF16),
    ("own_end", (80, LANES), BF16),
    ("own_final", (NG, 8, LANES), F32),
    ("landed", (8, LANES), F32),
)
SEMS = (
    ("load", (len(INPUTS),)), ("store", (len(OUTPUTS),)),
    ("rim_s", ()), ("rim_r", ()), ("rseg_s", ()), ("rseg_r", ()),
    ("kv_s", (NG,)), ("kv_r", (NG,)), ("sg_s", (NG,)), ("sg_r", (NG,)),
    ("sw_s", (NG,)), ("sw_r", (NG,)),
    ("pg_s", (NG,)), ("pg_r", (NG,)), ("pf_s", (4,)), ("pf_r", (4,)),
    ("x_s", (2, NX)), ("x_r", (2, NX)), ("z_s", (NZ,)), ("z_r", (NZ,)),
    ("g_s", (NZ,)), ("g_r", (NZ,)), ("h_s", (NZ, NX)), ("h_r", (NX, NZ)),
    ("e_s", (NG,)), ("e_r", (NG,)), ("f_s", ()), ("f_r", ()),
)


class Refs:
    pass


def main_kernel(*refs):
    k = Refs()
    names = ["hbm_" + n for n in OPERANDS] + ["hbm_out_" + n for n, _, _ in OUTPUTS]
    names += [n for n, _, _ in SCRATCH] + ["in_" + n for n, _, _ in INPUTS]
    names += ["out_" + n for n, _, _ in OUTPUTS if n != "pages"] + [n for n, _ in SEMS]
    for name, ref in zip(names, refs, strict=True):
        setattr(k, name, ref)
    k.out_pages = k.hbm_out_pages
    sect, tp, grp = lax.axis_index("sect"), lax.axis_index("tp"), lax.axis_index("grp")
    x, z = tp // NZ, tp % NZ
    chip, core = grp // 2, grp % 2
    twin = {"grp": grp + 1 - 2 * core}
    half_rows = pl.ds(pl.multiple_of(128 * core, 128), 128)
    heads = {"pair": tp // 4, "page": 2 * x + (NZ - 1 - z) // 4}
    loads = {}
    for i, (n, _, _) in enumerate(INPUTS):
        if n in heads:
            src = k.hbm_keys_values.at[:, :, pl.ds(pl.multiple_of(heads[n] * HD, HD), HD)]
        else:
            src = getattr(k, "hbm_" + n)
        loads[n] = pltpu.make_async_copy(src, getattr(k, "in_" + n), k.load.at[i])
        loads[n].start()
    stores = {}
    for i, (n, _, _) in enumerate(OUTPUTS):
        if n != "pages":
            stores[n] = pltpu.make_async_copy(getattr(k, "out_" + n), getattr(k, "hbm_out_" + n), k.store.at[i])

    quad = z // 4 * 4
    others_x = [lax.rem(x + d, NX) for d in range(1, NX)]
    others_z = [lax.rem(z + d, NZ) for d in range(1, NZ)]
    others_q = [quad + lax.rem(z + d, 4) for d in range(1, 4)]
    others_g = [lax.rem(grp + d, NG) for d in range(1, NG)]
    place_x = [{"tp": o * NZ + z} for o in others_x]
    place_z = [{"tp": x * NZ + o} for o in others_z]
    place_q = [{"tp": x * NZ + o} for o in others_q]
    place_g = [{"grp": o} for o in others_g]
    place_p = [{"sect": 1 - sect, "tp": x * NZ + (NZ - 1 - z), "grp": o} for o in range(NG)]
    across = {"sect": 1 - sect}
    partners = place_x + place_z + place_g + place_p + [across]
    barrier = pltpu.get_barrier_semaphore()
    for place in partners:
        pl.semaphore_signal(barrier, inc=1, device_id=place, device_id_type=MESH)

    loads["seg"].wait()
    seg_row = k.in_seg[...].astype(F32)
    seg_cols = jnp.broadcast_to(seg_row, (LANES, ROWS)).T
    k.ext_seg[8:, :] = seg_cols
    k.ext_seg[0:8, :] = jnp.full((8, LANES), -1.0, F32)
    k.seg_send[...] = seg_cols[ROWS - 8 :, :]
    k.seg_out[...] = jnp.broadcast_to(seg_row, (8, ROWS))
    loads["x"].wait()
    k.ext[8:, :] = k.in_x[...].astype(F32)
    k.ext[0:8, :] = jnp.zeros((8, WIDTH), F32)
    loads["conv_w"].wait()
    loads["conv_b"].wait()

    def convolve(count):
        here = k.ext_seg[8 : 8 + count, :]
        same = [k.ext_seg[5 + i : 5 + i + count, :] == here for i in range(3)]
        for lane in range(0, WIDTH, LANES):
            cols = slice(lane, lane + LANES)
            value = jnp.broadcast_to(k.in_conv_b[:, cols], (count, LANES))
            for i in range(4):
                term = k.ext[5 + i : 5 + i + count, cols] * k.in_conv_w[i : i + 1, cols]
                value = value + (jnp.where(same[i], term, 0.0) if i < 3 else term)
            k.conv[0:count, cols] = (value / (1.0 + jnp.exp(-value))).astype(BF16)

    def project(count):
        rows = k.conv[0:count, :]
        k.pay[0:count, 0:RANK] = dot_t(rows, k.in_proj[0:RANK, :]).astype(BF16)
        k.pay[0:count, RANK : RANK + 2 * NST] = dot_t(rows, k.in_proj[RANK:, :]).astype(BF16)

    convolve(ROWS)
    loads["moe"].wait()
    loads["moe_gain"].wait()
    loads["router"].wait()
    moe_rows = k.in_moe[...].astype(F32)
    spread = (iota((LANES, 16), 0) == iota((LANES, 16), 1)).astype(BF16)
    router = dot(spread, k.in_router[...])
    logits_part = dot_t(moe_rows * k.in_moe_gain[...], router, precision=lax.Precision.HIGHEST)
    squares = jnp.sum(moe_rows * moe_rows, axis=1, keepdims=True)
    tail = jnp.where(iota((ROWS, LANES), 1) == 16, squares, logits_part)
    k.pay[:, 640:768] = tail.astype(BF16)
    k.pay[:, 512:640] = jnp.zeros((ROWS, LANES), BF16)
    loads["proj"].wait()
    project(ROWS)

    loads["owner"].wait()
    loads["page"].wait()
    owners = jnp.broadcast_to(k.in_owner[...].astype(F32), (8, 16)).astype(BF16)
    owner_of = dot(owners, (iota((16, ROWS), 0) == iota((16, ROWS), 1) // BLK).astype(BF16))[0:1, :]
    owner_lanes = dot(owners, (iota((16, LANES), 0) == iota((16, LANES), 1)).astype(BF16))[0:1, :]
    owner_rows = jnp.broadcast_to(owner_lanes, (LANES, LANES)).T[0:16, 0:1]
    before = (owner_rows == owner_of) & (iota((16, ROWS), 0) < iota((16, ROWS), 1) // BLK)
    order = jnp.sum(jnp.where(before, 1.0, 0.0), axis=0, keepdims=True)
    slot = jnp.where(order == lax.rem(z, 4).astype(F32), owner_of, -1.0)
    row, col = iota((NG * BLK, ROWS), 0), iota((NG * BLK, ROWS), 1)
    choose = (slot == (row // BLK).astype(F32)) & (row % BLK == col % BLK)
    k.page[...] = k.in_page[...].reshape(ROWS, 2 * HD)
    chosen = dot(jnp.where(choose, 1.0, 0.0).astype(BF16), k.page[...])
    k.outgoing[...] = chosen.astype(BF16).reshape(NG, BLK, 2 * HD)
    loads["pair"].wait()
    k.pair[...] = k.in_pair[...].reshape(ROWS, 2 * HD)
    pl.semaphore_wait(barrier, len(partners))

    behind = {"grp": lax.rem(grp + 1, NG)}
    rim_copy = remote(k.in_x.at[ROWS - 16 : ROWS], k.rim, k.rim_s, k.rim_r, behind)
    rseg_copy = remote(k.seg_send, k.rim_seg, k.rseg_s, k.rseg_r, behind)
    rim_copy.start()
    rseg_copy.start()

    x_copies = {}
    for h in range(2):
        for d, (o, place) in enumerate(zip(others_x, place_x)):
            src = k.pay.at[pl.ds(pl.multiple_of(o * 64, 64), 64), HALF * h : HALF * (h + 1)]
            x_copies[h, d] = remote(src, k.rx.at[h, x], k.x_s.at[h, d], k.x_r.at[h, x], place)
    for (h, d), copy in x_copies.items():
        pl.when(others_x[d] != 0)(copy.start)

    kv_copies = []
    for d in range(1, NG):
        place = {"grp": lax.rem(grp + d, NG)}
        copy = remote(k.seg_out, k.seg_all.at[grp], k.sg_s.at[d], k.sg_r.at[grp], place)
        kv_copies.append((grp + d < NG, copy))
    for d in range(1, NG // 2):
        for half in range(2):
            rows = slice(128 * half, 128 * half + 128)
            place = {"grp": 2 * lax.rem(chip + d, NG // 2) + half}
            copy = remote(k.pair.at[rows], k.kv_all.at[grp, rows], k.kv_s.at[2 * d + half], k.kv_r.at[grp], place)
            kv_copies.append((chip + d < NG // 2, copy))
    kv_copies.append((core == 0, remote(k.pair, k.kv_all.at[grp], k.kv_s.at[0], k.kv_r.at[grp], twin)))
    for here, copy in kv_copies:
        pl.when(here)(copy.start)

    my_slot, their_slot = lax.rem(z, 4), 3 - lax.rem(z, 4)
    page_copies = []
    for o in range(NG):
        dst = k.out_pages.at[grp, my_slot]
        page_copies.append(remote(k.outgoing.at[o], dst, k.pg_s.at[o], k.pg_r.at[grp], place_p[o]))
    for copy in page_copies:
        copy.start()

    rim_copy.wait()
    rseg_copy.wait()
    k.ext[0:8, :] = k.rim[8:16, :].astype(F32)
    k.ext_seg[0:8, :] = jnp.where(grp == 0, -1.0, k.rim_seg[...])
    convolve(16)
    project(16)
    for (h, d), copy in x_copies.items():
        pl.when(others_x[d] == 0)(copy.start)

    factor = HD**-0.5 * LOG2E

    ones = jnp.ones((ROWS, HD), BF16)

    def attend(key_block, value_block, allowed, first):
        valued = jnp.concatenate([value_block, ones], axis=1)
        for h in range(2):
            scores = dot_t(k.in_q[:, h * HD : (h + 1) * HD], key_block)
            masked = jnp.where(allowed, scores, -HUGE)
            high = jnp.max(masked, axis=1, keepdims=True)
            if first:
                new = high
                weights = jnp.exp2((masked - new) * factor)
                k.accum[h] = dot(weights.astype(BF16), valued)
            else:
                old = k.best[h][:, 0:1]
                new = jnp.maximum(old, high)
                weights = jnp.exp2((masked - new) * factor)
                fade = jnp.exp2((old - new) * factor)
                k.accum[h] = k.accum[h] * fade + dot(weights.astype(BF16), valued)
            k.best[h] = jnp.broadcast_to(new, (ROWS, LANES))

    def attend_block(j):
        remote(k.seg_out, k.seg_all.at[j], k.sg_s.at[0], k.sg_r.at[j], place_g[0]).wait_recv()
        same = k.seg_all[j, 0:1, :] == k.ext_seg[8:, 0:1]
        attend(k.kv_all[j, :, 0:HD], k.kv_all[j, :, HD:], same, False)

    def swap(i):
        block = k.kv_all.at[2 * chip - 1 - i, half_rows]
        return remote(block, block, k.sw_s.at[i], k.sw_r.at[i], twin)

    def swap_start(i, carry):
        block = k.kv_all.at[2 * chip - 1 - i, half_rows]
        remote(block, block, k.sw_s.at[i], k.kv_r.at[2 * chip - 1 - i], twin).wait_recv()
        swap(i).start()
        return carry

    def swap_end(i, carry):
        swap(i).wait_send()
        return carry

    def earlier(i, carry):
        swap(i).wait_recv()
        attend_block(2 * chip - 1 - i)
        return carry

    loads["q"].wait()
    causal = iota((ROWS, ROWS), 1) <= iota((ROWS, ROWS), 0)
    attend(k.pair[:, 0:HD], k.pair[:, HD:], causal & (seg_row == k.ext_seg[8:, 0:1]), True)

    z_copies = [
        remote(k.chunk.at[o], k.rz.at[z], k.z_s.at[o], k.z_r.at[z], {"tp": x * NZ + o}) for o in range(NZ)
    ]
    for h in range(2):
        for o in others_x:
            remote(k.rx.at[h, o], k.rx.at[h, o], k.x_s.at[h, 0], k.x_r.at[h, o], place_x[0]).wait_recv()
        summed = k.pay[pl.ds(pl.multiple_of(x * 64, 64), 64), HALF * h : HALF * (h + 1)].astype(F32)
        for o in others_x:
            summed = summed + k.rx[h, o].astype(F32)
        for r in range(4):
            k.chunk[4 * h + r] = summed[16 * r : 16 * r + 16, :].astype(BF16)
        for r in range(4):
            pl.when(z != 4 * h + r)(z_copies[4 * h + r].start)

    loads["z"].wait()
    gate = k.in_z[...].astype(F32)
    k.silu_z[...] = gate / (1.0 + jnp.exp(-gate))


    @pl.when(core == 1)
    def _():
        remote(k.pair, k.kv_all.at[grp - 1], k.kv_s.at[0], k.kv_r.at[grp - 1], twin).wait_recv()
        attend_block(grp - 1)

    for o in others_z:
        remote(k.chunk.at[0], k.rz.at[o], k.z_s.at[0], k.z_r.at[o], place_z[0]).wait_recv()
    summed = k.chunk[z].astype(F32)
    for o in others_z:
        summed = summed + k.rz[o].astype(F32)
    k.low[x, z] = summed.astype(BF16)
    g_copies = []
    for d, place in enumerate(place_z):
        g_copies.append(remote(k.low.at[x, z], k.low.at[x, z], k.g_s.at[d], k.g_r.at[z], place))
    for copy in g_copies:
        copy.start()
    h_copies = []

    def forward(o):
        for d, place in enumerate(place_x):
            copy = remote(k.low.at[x, o], k.low.at[x, o], k.h_s.at[o, d], k.h_r.at[x, o], place)
            copy.start()
            h_copies.append(copy)

    forward(z)
    for o in others_z:
        remote(k.low.at[x, z], k.low.at[x, o], k.g_s.at[0], k.g_r.at[o], place_z[0]).wait_recv()
        forward(o)

    lax.fori_loop(0, 2 * chip, swap_start, 0)

    for o in range(NG):
        remote(k.outgoing.at[0], k.out_pages.at[o, their_slot], k.pg_s.at[0], k.pg_r.at[o], place_p[0]).wait_recv()
    f_copies = []
    for d, place in enumerate(place_q):
        mine = k.out_pages.at[:, their_slot]
        f_copies.append(remote(mine, mine, k.pf_s.at[d], k.pf_r.at[their_slot], place))
    for copy in f_copies:
        copy.start()

    lax.fori_loop(0, jnp.minimum(2 * chip, 3), earlier, 0)

    for n in ("gain", "dt", "dt_bias", "a_log", "skip", "routing"):
        loads[n].wait()
    for o in others_x:
        for p in range(NZ):
            remote(k.low.at[x, p], k.low.at[o, p], k.h_s.at[0, 0], k.h_r.at[o, p], place_x[0]).wait_recv()
    gain = k.in_gain[...].reshape(1, RANK + 2 * NST)
    left = k.low[:, 0:4].reshape(ROWS, HALF).astype(F32)
    right = k.low[:, 4:8].reshape(ROWS, HALF).astype(F32)
    mean = jnp.sum(left * left, axis=1, keepdims=True) + jnp.sum(right[:, :128] * right[:, :128], axis=1, keepdims=True)
    scale = lax.rsqrt(mean / RANK + EPS)
    k.rank[:, 0:HALF] = (left * scale * gain[:, 0:HALF]).astype(BF16)
    k.rank[:, HALF:RANK] = (right[:, :128] * scale * gain[:, HALF:RANK]).astype(BF16)
    both = right[:, 128 : 128 + 2 * NST]
    is_b = iota((ROWS, 2 * NST), 1) < NST
    power = both * both
    mean_b = jnp.sum(jnp.where(is_b, power, 0.0), axis=1, keepdims=True) / NST
    mean_c = jnp.sum(jnp.where(is_b, 0.0, power), axis=1, keepdims=True) / NST
    scale = jnp.where(is_b, lax.rsqrt(mean_b + EPS), lax.rsqrt(mean_c + EPS))
    k.bc[...] = (both * scale * gain[:, RANK : RANK + 2 * NST]).astype(BF16)

    raw = dot(k.rank[...], k.in_dt[...]) + k.in_dt_bias[...]
    step = jnp.maximum(raw, 0.0) + jnp.log(1.0 + jnp.exp(-jnp.abs(raw)))
    k.driven[...] = step * k.conv[...].astype(F32)
    start = jnp.where(k.ext_seg[7 : 7 + ROWS, :] != k.ext_seg[8:, :], HUGE, 0.0)
    for lane in range(0, WIDTH, LANES):
        k.step[:, lane : lane + LANES] = step[:, lane : lane + LANES] + start
    pick = (iota((NST, 2 * NST), 0) == iota((NST, 2 * NST), 1)).astype(BF16)
    b_all = dot_t(pick, k.bc[...])
    for b in range(16):
        k.b_cols[b, :, 0:16] = b_all[:, 16 * b : 16 * b + 16]
    pick = (iota((2 * NST, 256), 0) == NST + iota((2 * NST, 256), 1) % NST).astype(BF16)
    own = iota((ROWS, 256), 1) // NST == iota((ROWS, 256), 0) % 16
    k.c_blocks[...] = jnp.where(own, dot(k.bc[...], pick), 0.0).astype(BF16)
    rate = jnp.exp(k.in_a_log[...]) * (-LOG2E)

    def scan(b, carry):
        state, left = carry
        rows = pl.ds(pl.multiple_of(b * 16, 16), 16)
        steps, driven, b_cols = k.step[rows, :], k.driven[rows, :], k.b_cols[b]
        for t in range(16):
            span = slice(NST * t, NST * (t + 1))
            decay = jnp.exp2(steps[t : t + 1, :] * rate)
            state = decay * state + b_cols[:, t : t + 1] * driven[t : t + 1, :]
            left = decay * left
            k.states[b, span, :] = state.astype(BF16)
            k.growth[b, span, :] = left.astype(BF16)
        return state, left

    begin = (jnp.zeros((NST, WIDTH), F32), jnp.ones((NST, WIDTH), F32))
    state, _ = lax.fori_loop(0, ROWS // 16, scan, begin)
    steps = jnp.sum(k.step[...], axis=0, keepdims=True)
    for i in range(4):
        k.own_end[NST * i : NST * (i + 1), :] = state[:, i * LANES : (i + 1) * LANES].astype(BF16)
    parts = []
    for _ in range(3):
        part = steps.astype(BF16).astype(F32)
        parts += [part[:, i * LANES : (i + 1) * LANES] for i in range(4)]
        steps = steps - part
    k.own_end[64:80, :] = jnp.concatenate(parts + [jnp.zeros((4, LANES), F32)], axis=0).astype(BF16)
    e_copies = []
    for d, place in enumerate(place_g):
        e_copies.append(remote(k.own_end, k.ends.at[grp], k.e_s.at[d], k.e_r.at[grp], place))
    for copy in e_copies:
        copy.start()
    k.ends[grp] = k.own_end[...]

    lax.fori_loop(jnp.minimum(2 * chip, 3), 2 * chip, earlier, 0)
    for h in range(2):
        k.out_attn[:, h * HD : (h + 1) * HD] = (k.accum[h, :, 0:HD] / k.accum[h, :, HD:]).astype(BF16)
    stores["attn"].start()
    sums = right[:, 256:384]
    inverse = lax.rsqrt(sums[:, 16:17] / FEATURES + EPS)
    k.out_expert[...] = (k.in_moe[...].astype(F32) * k.in_moe_gain[...] * inverse).astype(BF16)
    logits = (sums * inverse).T
    experts = iota((LANES, ROWS), 0)
    first = jnp.sum(jnp.where(experts == k.in_routing[0:1, :], logits, 0.0), axis=0, keepdims=True)
    second = jnp.sum(jnp.where(experts == k.in_routing[1:2, :], logits, 0.0), axis=0, keepdims=True)
    top = jnp.maximum(first, second)
    first, second = jnp.exp(first - top), jnp.exp(second - top)
    k.out_gate[0:1, :] = first / (first + second)
    k.out_gate[1:2, :] = second / (first + second)
    stores["expert"].start()
    stores["gate"].start()

    for o in others_g:
        remote(k.own_end, k.ends.at[o], k.e_s.at[0], k.e_r.at[o], place_g[0]).wait_recv()
    sums_of = []
    for j in range(NG):
        part = k.ends[j, 64:80, :].astype(F32)
        sums_of.append(part[0:4] + part[4:8] + part[8:12])
    entering = []
    for i in range(4):
        cols = slice(i * LANES, (i + 1) * LANES)
        state = jnp.zeros((NST, LANES), F32)
        mine = state
        for j in range(NG):
            mine = jnp.where(grp == j, state, mine)
            kept = jnp.exp2(sums_of[j][i : i + 1, :] * rate[:, cols])
            state = kept * state + k.ends[j, NST * i : NST * (i + 1), :].astype(F32)
        entering.append(mine)
        for g in range(NG):
            k.own_final[g, 2 * i : 2 * i + 2, :] = state[2 * g : 2 * g + 2, :]
    final_copy = remote(k.own_final.at[grp], k.landed, k.f_s, k.f_r, across)
    final_copy.start()
    entering = jnp.concatenate(entering, axis=1).astype(BF16)

    def finish(b, carry):
        rows = pl.ds(pl.multiple_of(b * 16, 16), 16)
        grown = k.growth[b].reshape(16, NST, WIDTH) * entering[None] + k.states[b].reshape(16, NST, WIDTH)
        value = dot(k.c_blocks[rows, :], grown.reshape(256, WIDTH))
        value = value + k.in_skip[...] * k.conv[rows, :].astype(F32)
        k.out_mixed[rows, :] = (value * k.silu_z[rows, :]).astype(BF16)
        return carry

    lax.fori_loop(0, ROWS // 16, finish, 0, unroll=4)
    stores["mixed"].start()

    final_copy.wait()
    for i in range(4):
        k.out_final[:, i * LANES : (i + 1) * LANES] = k.landed[2 * i : 2 * i + 2, :]
    stores["final"].start()
    for o in others_q:
        theirs = k.out_pages.at[:, 3 - lax.rem(o, 4)]
        remote(theirs, theirs, k.pf_s.at[0], k.pf_r.at[3 - lax.rem(o, 4)], place_q[0]).wait_recv()
    for copy in list(x_copies.values()) + g_copies + h_copies + page_copies + f_copies + e_copies:
        copy.wait_send()
    for o in range(NZ):
        pl.when(z != o)(z_copies[o].wait_send)
    lax.fori_loop(0, 2 * chip, swap_end, 0)
    for here, copy in kv_copies:
        pl.when(here)(copy.wait_send)
    for store in stores.values():
        store.wait()


def hand_out(*refs):
    count = len(OUTPUTS)
    source, target, stage = refs[:count], refs[count : 2 * count], refs[2 * count : 3 * count]
    read, write = refs[3 * count :]
    inward = [pltpu.make_async_copy(source[i], stage[i], read.at[i]) for i in range(count)]
    outward = [pltpu.make_async_copy(stage[i], target[i], write.at[i]) for i in range(count)]
    for copy in inward:
        copy.start()
    for i in range(count):
        inward[i].wait()
        outward[i].start()
    for copy in outward:
        copy.wait()


def local(
    mamba_x, mamba_z, conv_weight, conv_bias, x_proj, norm_gain, dt_proj, dt_bias, a_log, d_skip,
    segment_ids, queries, keys_values, kv_owner, moe_in, moe_gain, router, routing,
):
    inputs = dict(
        x=mamba_x, seg=segment_ids, conv_w=conv_weight, conv_b=conv_bias.reshape(1, -1), proj=x_proj.T,
        owner=kv_owner.reshape(1, -1), keys_values=keys_values, moe=moe_in, moe_gain=moe_gain.reshape(1, -1), router=router.T, q=queries,
        z=mamba_z, gain=norm_gain, dt=dt_proj, dt_bias=dt_bias.reshape(1, -1), a_log=a_log,
        skip=d_skip.reshape(1, -1), routing=routing.T,
    )
    shapes = tuple(jax.ShapeDtypeStruct(s, t) for _, s, t in OUTPUTS)
    results = pl.pallas_call(
        main_kernel,
        out_shape=shapes,
        in_specs=[ANY] * len(OPERANDS),
        out_specs=tuple([ANY] * len(OUTPUTS)),
        scratch_shapes=[pltpu.VMEM(s, t) for _, s, t in SCRATCH]
        + [pltpu.VMEM(s, t) for _, s, t in INPUTS]
        + [pltpu.VMEM(s, t) for n, s, t in OUTPUTS if n != "pages"]
        + [DMA(s) if s else DMA for _, s in SEMS],
        compiler_params=pltpu.CompilerParams(
            vmem_limit_bytes=62 << 20, collective_id=0, has_side_effects=True
        ),
        name="span",
    )(*[inputs[n] for n in OPERANDS])
    mixed, final, attn, pages, expert, gates = pl.pallas_call(
        hand_out,
        out_shape=shapes,
        in_specs=[ANY] * len(OUTPUTS),
        out_specs=tuple([ANY] * len(OUTPUTS)),
        scratch_shapes=[pltpu.VMEM(s, t) for _, s, t in OUTPUTS] + [DMA((len(OUTPUTS),))] * 2,
        compiler_params=pltpu.CompilerParams(vmem_limit_bytes=62 << 20),
        name="results",
    )(*results)
    return (mixed, final[None], attn, pages.reshape(1, 1, 1, NG * SLOTS, BLK, 2 * HD), expert, gates.T)


def solution(mesh):
    placed = (
        P(("sect", "grp"), "tp"),
        P(("sect", "grp"), "tp"),
        P(None, "tp"),
        P("tp"),
        P("tp", None),
        P(),
        P(None, "tp"),
        P("tp"),
        P(None, "tp"),
        P("tp"),
        P("sect", "grp"),
        P(("sect", "grp"), "tp"),
        P(("sect", "grp"), None, None),
        P("sect", "grp", None),
        P(("sect", "grp"), "tp"),
        P("tp"),
        P("tp", None),
        P(("sect", "grp"), None),
    )
    return jax.shard_map(
        local,
        mesh=mesh,
        in_specs=placed,
        out_specs=(
            P(("sect", "grp"), "tp"),
            P("sect", "grp", "tp"),
            P(("sect", "grp"), "tp"),
            P("sect", "grp", "tp", None, None, None),
            P(("sect", "grp"), "tp"),
            P(("sect", "grp"), None),
        ),
        check_vma=False,
    )
```

```python
import jax
import jax.numpy as jnp
from jax import lax
from jax.experimental import pallas as pl
from jax.experimental.pallas import tpu as pltpu
from jax.sharding import PartitionSpec as P

MESH = pl.DeviceIdType.MESH
F32 = jnp.float32
BF16 = jnp.bfloat16
I32 = jnp.int32

ROWS = 256
WIDTH = 512
RANK = 512
NST = 16
HD = 128
BLK = 16
LANES = 128
NX, NZ, NG = 4, 8, 8
PAY = 640
CUTS = (0, 384, 640)
WIDE = (384, 256)
SLOTS = 4
FEATURES = 8192
EPS = 1e-06
SQUARES = 2 * NST + 16
LOG2E = 1.4426950408889634
HUGE = 1e30
VMEM = pl.BlockSpec(memory_space=pltpu.VMEM)
ANY = pl.BlockSpec(memory_space=pl.ANY)
DMA = pltpu.SemaphoreType.DMA


def iota(shape, dim):
    return lax.broadcasted_iota(I32, shape, dim)


def dot(a, b, **kw):
    return jnp.dot(a, b, preferred_element_type=F32, **kw)


def dot_t(a, b, **kw):
    return lax.dot_general(a, b, (((1,), (1,)), ((), ())), preferred_element_type=F32, **kw)


def remote(src, dst, send, recv, where):
    return pltpu.make_async_remote_copy(
        src_ref=src, dst_ref=dst, send_sem=send, recv_sem=recv, device_id=where, device_id_type=MESH
    )


INPUTS = (
    ("x", (ROWS, WIDTH), BF16),
    ("seg", (1, ROWS), I32),
    ("conv_w", (4, WIDTH), F32),
    ("conv_b", (1, WIDTH), F32),
    ("proj", (RANK + 2 * NST, WIDTH), BF16),
    ("owner", (1, 16), I32),
    ("page", (ROWS, 2, HD), BF16),
    ("pair", (ROWS, 2, HD), BF16),
    ("moe", (ROWS, 256), BF16),
    ("moe_gain", (1, 256), F32),
    ("router", (16, 256), BF16),
    ("q", (ROWS, 2 * HD), BF16),
    ("z", (ROWS, WIDTH), BF16),
    ("gain", (RANK + 2 * NST,), F32),
    ("dt", (RANK, WIDTH), BF16),
    ("dt_bias", (1, WIDTH), F32),
    ("a_log", (NST, WIDTH), F32),
    ("skip", (1, WIDTH), F32),
    ("routing", (2, ROWS), I32),
)
OUTPUTS = (
    ("mixed", (ROWS, WIDTH), BF16),
    ("final", (2, WIDTH), F32),
    ("attn", (ROWS, 2 * HD), BF16),
    ("pages", (NG, SLOTS, BLK, 2 * HD), BF16),
    ("expert", (ROWS, 256), BF16),
    ("gate", (2, ROWS), F32),
)
OPERANDS = [n for n, _, _ in INPUTS if n not in ("page", "pair")] + ["keys_values"]
SCRATCH = (
    ("page", (ROWS, 2 * HD), BF16),
    ("pair", (ROWS, 2 * HD), BF16),
    ("rim", (16, WIDTH), BF16),
    ("rim_seg", (8, LANES), F32),
    ("seg_send", (8, LANES), F32),
    ("seg_out", (8, ROWS), F32),
    ("seg_all", (NG, 8, ROWS), F32),
    ("kv_all", (NG, ROWS, 2 * HD), BF16),
    ("ext", (8 + ROWS, WIDTH), F32),
    ("ext_seg", (8 + ROWS, LANES), F32),
    ("conv", (ROWS, WIDTH), BF16),
    ("pay", (ROWS, PAY), BF16),
    ("rx0", (NX, 64, WIDE[0]), BF16),
    ("rx1", (NX, 64, WIDE[1]), BF16),
    ("chunk0", (4, 16, WIDE[0]), BF16),
    ("chunk1", (4, 16, WIDE[1]), BF16),
    ("rz0", (NZ, 16, WIDE[0]), BF16),
    ("rz1", (NZ, 16, WIDE[1]), BF16),
    ("low0", (NX, 4, 16, WIDE[0]), BF16),
    ("low1", (NX, 4, 16, WIDE[1]), BF16),
    ("outgoing", (NG, BLK, 2 * HD), BF16),
    ("best", (2, ROWS, LANES), F32),
    ("accum", (2, ROWS, 2 * HD), F32),
    ("silu_z", (ROWS, WIDTH), F32),
    ("rank", (ROWS, RANK), BF16),
    ("bc", (ROWS, 2 * NST), BF16),
    ("step", (ROWS, WIDTH), F32),
    ("driven", (ROWS, WIDTH), F32),
    ("b_cols", (16, NST, LANES), F32),
    ("c_blocks", (ROWS, 256), BF16),
    ("states", (16, 256, WIDTH), BF16),
    ("growth", (16, 256, WIDTH), BF16),
    ("ends", (NG, 80, LANES), BF16),
    ("own_end", (80, LANES), BF16),
    ("own_final", (NG, 8, LANES), F32),
    ("landed", (8, LANES), F32),
)
SEMS = (
    ("load", (len(INPUTS),)), ("store", (len(OUTPUTS),)),
    ("rim_s", ()), ("rim_r", ()), ("rseg_s", ()), ("rseg_r", ()),
    ("kv_s", (NG,)), ("kv_r", (NG,)), ("sg_s", (NG,)), ("sg_r", (NG,)),
    ("sw_s", (NG,)), ("sw_r", (NG,)),
    ("pg_s", (NG,)), ("pg_r", (NG,)), ("pf_s", (4,)), ("pf_r", (4,)),
    ("x_s", (2, NX)), ("x_r", (2, NX)), ("z_s", (NZ,)), ("z_r", (NZ,)),
    ("g_s", (NZ,)), ("g_r", (NZ,)), ("h_s", (NZ, NX)), ("h_r", (NX, NZ)),
    ("e_s", (NG,)), ("e_r", (NG,)), ("f_s", ()), ("f_r", ()),
)


class Refs:
    pass


def main_kernel(*refs):
    k = Refs()
    names = ["hbm_" + n for n in OPERANDS] + ["hbm_out_" + n for n, _, _ in OUTPUTS]
    names += [n for n, _, _ in SCRATCH] + ["in_" + n for n, _, _ in INPUTS]
    names += ["out_" + n for n, _, _ in OUTPUTS if n != "pages"] + [n for n, _ in SEMS]
    for name, ref in zip(names, refs, strict=True):
        setattr(k, name, ref)
    k.out_pages = k.hbm_out_pages
    sect, tp, grp = lax.axis_index("sect"), lax.axis_index("tp"), lax.axis_index("grp")
    x, z = tp // NZ, tp % NZ
    chip, core = grp // 2, grp % 2
    twin = {"grp": grp + 1 - 2 * core}
    half_rows = pl.ds(pl.multiple_of(128 * core, 128), 128)
    heads = {"pair": tp // 4, "page": 2 * x + (NZ - 1 - z) // 4}
    loads = {}
    for i, (n, _, _) in enumerate(INPUTS):
        if n in heads:
            src = k.hbm_keys_values.at[:, :, pl.ds(pl.multiple_of(heads[n] * HD, HD), HD)]
        else:
            src = getattr(k, "hbm_" + n)
        loads[n] = pltpu.make_async_copy(src, getattr(k, "in_" + n), k.load.at[i])
        loads[n].start()
    stores = {}
    for i, (n, _, _) in enumerate(OUTPUTS):
        if n != "pages":
            stores[n] = pltpu.make_async_copy(getattr(k, "out_" + n), getattr(k, "hbm_out_" + n), k.store.at[i])

    quad = z // 4 * 4
    others_x = [lax.rem(x + d, NX) for d in range(1, NX)]
    others_z = [lax.rem(z + d, NZ) for d in range(1, NZ)]
    others_q = [quad + lax.rem(z + d, 4) for d in range(1, 4)]
    others_g = [lax.rem(grp + d, NG) for d in range(1, NG)]
    place_x = [{"tp": o * NZ + z} for o in others_x]
    place_z = [{"tp": x * NZ + o} for o in others_z]
    place_q = [{"tp": x * NZ + o} for o in others_q]
    place_g = [{"grp": o} for o in others_g]
    place_p = [{"sect": 1 - sect, "tp": x * NZ + (NZ - 1 - z), "grp": o} for o in range(NG)]
    across = {"sect": 1 - sect}
    partners = place_x + place_z + place_g + place_p + [across]
    barrier = pltpu.get_barrier_semaphore()
    for place in partners:
        pl.semaphore_signal(barrier, inc=1, device_id=place, device_id_type=MESH)

    loads["x"].wait()
    loads["seg"].wait()
    seg_row = k.in_seg[...].astype(F32)
    seg_cols = jnp.broadcast_to(seg_row, (LANES, ROWS)).T
    k.ext_seg[8:, :] = seg_cols
    k.seg_send[...] = seg_cols[ROWS - 8 :, :]
    k.seg_out[...] = jnp.broadcast_to(seg_row, (8, ROWS))
    pl.semaphore_wait(barrier, len(partners))

    behind = {"grp": lax.rem(grp + 1, NG)}
    rim_copy = remote(k.in_x.at[ROWS - 16 : ROWS], k.rim, k.rim_s, k.rim_r, behind)
    rseg_copy = remote(k.seg_send, k.rim_seg, k.rseg_s, k.rseg_r, behind)
    rim_copy.start()
    rseg_copy.start()

    loads["pair"].wait()
    k.pair[...] = k.in_pair[...].reshape(ROWS, 2 * HD)
    kv_copies = []
    for d in range(1, NG):
        place = {"grp": lax.rem(grp + d, NG)}
        copy = remote(k.seg_out, k.seg_all.at[grp], k.sg_s.at[d], k.sg_r.at[grp], place)
        kv_copies.append((grp + d < NG, copy))
    for d in range(1, NG // 2):
        for half in range(2):
            rows = slice(128 * half, 128 * half + 128)
            place = {"grp": 2 * lax.rem(chip + d, NG // 2) + half}
            copy = remote(k.pair.at[rows], k.kv_all.at[grp, rows], k.kv_s.at[2 * d + half], k.kv_r.at[grp], place)
            kv_copies.append((chip + d < NG // 2, copy))
    kv_copies.append((core == 0, remote(k.pair, k.kv_all.at[grp], k.kv_s.at[0], k.kv_r.at[grp], twin)))
    for here, copy in kv_copies:
        pl.when(here)(copy.start)

    loads["owner"].wait()
    loads["page"].wait()
    owners = jnp.broadcast_to(k.in_owner[...].astype(F32), (8, 16)).astype(BF16)
    owner_of = dot(owners, (iota((16, ROWS), 0) == iota((16, ROWS), 1) // BLK).astype(BF16))[0:1, :]
    owner_lanes = dot(owners, (iota((16, LANES), 0) == iota((16, LANES), 1)).astype(BF16))[0:1, :]
    owner_rows = jnp.broadcast_to(owner_lanes, (LANES, LANES)).T[0:16, 0:1]
    before = (owner_rows == owner_of) & (iota((16, ROWS), 0) < iota((16, ROWS), 1) // BLK)
    order = jnp.sum(jnp.where(before, 1.0, 0.0), axis=0, keepdims=True)
    slot = jnp.where(order == lax.rem(z, 4).astype(F32), owner_of, -1.0)
    row, col = iota((NG * BLK, ROWS), 0), iota((NG * BLK, ROWS), 1)
    choose = (slot == (row // BLK).astype(F32)) & (row % BLK == col % BLK)
    k.page[...] = k.in_page[...].reshape(ROWS, 2 * HD)
    chosen = dot(jnp.where(choose, 1.0, 0.0).astype(BF16), k.page[...])
    k.outgoing[...] = chosen.astype(BF16).reshape(NG, BLK, 2 * HD)
    my_slot, their_slot = lax.rem(z, 4), 3 - lax.rem(z, 4)
    page_copies = []
    for o in range(NG):
        dst = k.out_pages.at[grp, my_slot]
        page_copies.append(remote(k.outgoing.at[o], dst, k.pg_s.at[o], k.pg_r.at[grp], place_p[o]))
    for copy in page_copies:
        copy.start()

    loads["moe"].wait()
    loads["moe_gain"].wait()
    loads["router"].wait()
    moe_rows = k.in_moe[...].astype(F32)
    spread = (iota((LANES, 16), 0) == iota((LANES, 16), 1) + 2 * NST).astype(BF16)
    router = dot(spread, k.in_router[...])
    logits_part = dot_t(moe_rows * k.in_moe_gain[...], router, precision=lax.Precision.HIGHEST)
    squares = jnp.sum(moe_rows * moe_rows, axis=1, keepdims=True)
    tail = jnp.where(iota((ROWS, LANES), 1) == SQUARES, squares, logits_part)

    k.ext[8:, :] = k.in_x[...].astype(F32)
    loads["conv_w"].wait()
    loads["conv_b"].wait()
    loads["proj"].wait()
    rim_copy.wait()
    rseg_copy.wait()
    k.ext[0:8, :] = k.rim[8:16, :].astype(F32)
    k.ext_seg[0:8, :] = jnp.where(grp == 0, -1.0, k.rim_seg[...])
    here = k.ext_seg[8:, :]
    same = [k.ext_seg[5 + i : 5 + i + ROWS, :] == here for i in range(3)]
    for lane in range(0, WIDTH, LANES):
        cols = slice(lane, lane + LANES)
        value = jnp.broadcast_to(k.in_conv_b[:, cols], (ROWS, LANES))
        for i in range(4):
            term = k.ext[5 + i : 5 + i + ROWS, cols] * k.in_conv_w[i : i + 1, cols]
            value = value + (jnp.where(same[i], term, 0.0) if i < 3 else term)
        k.conv[:, cols] = (value / (1.0 + jnp.exp(-value))).astype(BF16)
    conv = k.conv[...]

    rx, chunk, rz, low = (k.rx0, k.rx1), (k.chunk0, k.chunk1), (k.rz0, k.rz1), (k.low0, k.low1)
    x_copies = []
    for h in range(2):
        if h == 0:
            k.pay[:, 0:384] = dot_t(conv, k.in_proj[0:384, :]).astype(BF16)
        else:
            k.pay[:, 384:RANK] = dot_t(conv, k.in_proj[384:RANK, :]).astype(BF16)
            spread = (iota((LANES, 2 * NST), 0) == iota((LANES, 2 * NST), 1)).astype(BF16)
            last = dot(spread, k.in_proj[RANK:, :]).astype(BF16)
            k.pay[:, RANK:PAY] = (dot_t(conv, last) + tail).astype(BF16)
        for d, (o, place) in enumerate(zip(others_x, place_x)):
            src = k.pay.at[pl.ds(pl.multiple_of(o * 64, 64), 64), CUTS[h] : CUTS[h + 1]]
            copy = remote(src, rx[h].at[x], k.x_s.at[h, d], k.x_r.at[h, x], place)
            copy.start()
            x_copies.append(copy)

    factor = HD**-0.5 * LOG2E

    ones = jnp.ones((ROWS, HD), BF16)

    def attend(key_block, value_block, allowed, first):
        valued = jnp.concatenate([value_block, ones], axis=1)
        for h in range(2):
            scores = dot_t(k.in_q[:, h * HD : (h + 1) * HD], key_block)
            masked = jnp.where(allowed, scores, -HUGE)
            high = jnp.max(masked, axis=1, keepdims=True)
            if first:
                new = high
                weights = jnp.exp2((masked - new) * factor)
                k.accum[h] = dot(weights.astype(BF16), valued)
            else:
                old = k.best[h][:, 0:1]
                new = jnp.maximum(old, high)
                weights = jnp.exp2((masked - new) * factor)
                fade = jnp.exp2((old - new) * factor)
                k.accum[h] = k.accum[h] * fade + dot(weights.astype(BF16), valued)
            k.best[h] = jnp.broadcast_to(new, (ROWS, LANES))

    def attend_block(j):
        remote(k.seg_out, k.seg_all.at[j], k.sg_s.at[0], k.sg_r.at[j], place_g[0]).wait_recv()
        same = k.seg_all[j, 0:1, :] == k.ext_seg[8:, 0:1]
        attend(k.kv_all[j, :, 0:HD], k.kv_all[j, :, HD:], same, False)

    def swap(i):
        block = k.kv_all.at[2 * chip - 1 - i, half_rows]
        return remote(block, block, k.sw_s.at[i], k.sw_r.at[i], twin)

    def swap_start(i, carry):
        block = k.kv_all.at[2 * chip - 1 - i, half_rows]
        remote(block, block, k.sw_s.at[i], k.kv_r.at[2 * chip - 1 - i], twin).wait_recv()
        swap(i).start()
        return carry

    def swap_end(i, carry):
        swap(i).wait_send()
        return carry

    def earlier(i, carry):
        swap(i).wait_recv()
        attend_block(2 * chip - 1 - i)
        return carry

    loads["q"].wait()
    causal = iota((ROWS, ROWS), 1) <= iota((ROWS, ROWS), 0)
    attend(k.pair[:, 0:HD], k.pair[:, HD:], causal & (seg_row == k.ext_seg[8:, 0:1]), True)

    z_copies = []
    for h in range(2):
        for o in others_x:
            remote(rx[h].at[o], rx[h].at[o], k.x_s.at[h, 0], k.x_r.at[h, o], place_x[0]).wait_recv()
        summed = k.pay[pl.ds(pl.multiple_of(x * 64, 64), 64), CUTS[h] : CUTS[h + 1]].astype(F32)
        for o in others_x:
            summed = summed + rx[h][o].astype(F32)
        for r in range(4):
            chunk[h][r] = summed[16 * r : 16 * r + 16, :].astype(BF16)
        for r in range(4):
            o = 4 * h + r
            copy = remote(chunk[h].at[r], rz[h].at[z], k.z_s.at[o], k.z_r.at[z], {"tp": x * NZ + o})
            z_copies.append((z != o, copy))
            pl.when(z != o)(copy.start)

    loads["z"].wait()
    gate = k.in_z[...].astype(F32)
    k.silu_z[...] = gate / (1.0 + jnp.exp(-gate))


    @pl.when(core == 1)
    def _():
        remote(k.pair, k.kv_all.at[grp - 1], k.kv_s.at[0], k.kv_r.at[grp - 1], twin).wait_recv()
        attend_block(grp - 1)

    quarter = lax.rem(z, 4)

    def gathering(h, r, source):
        piece = low[h].at[x, r]
        return [remote(piece, piece, k.g_s.at[d], k.g_r.at[source], place) for d, place in enumerate(place_z)]

    def forwards(h, r, source):
        piece = low[h].at[x, r]
        return [
            remote(piece, piece, k.h_s.at[source, d], k.h_r.at[x, source], place)
            for d, place in enumerate(place_x)
        ]

    for h in range(2):

        @pl.when(z // 4 == h)
        def _(h=h):
            for o in others_z:
                remote(chunk[h].at[0], rz[h].at[o], k.z_s.at[0], k.z_r.at[o], place_z[0]).wait_recv()
            summed = chunk[h][quarter].astype(F32)
            for o in others_z:
                summed = summed + rz[h][o].astype(F32)
            low[h][x, quarter] = summed.astype(BF16)
            for copy in gathering(h, quarter, z) + forwards(h, quarter, z):
                copy.start()

    for near in range(2):

        @pl.when(z // 4 == near)
        def _(near=near):
            for h in (near, 1 - near):
                for r in range(4):

                    @pl.when(z != 4 * h + r)
                    def _(h=h, r=r):
                        piece = low[h].at[x, r]
                        remote(piece, piece, k.g_s.at[0], k.g_r.at[4 * h + r], place_z[0]).wait_recv()
                        for copy in forwards(h, r, 4 * h + r):
                            copy.start()

    lax.fori_loop(0, 2 * chip, swap_start, 0)

    for o in range(NG):
        remote(k.outgoing.at[0], k.out_pages.at[o, their_slot], k.pg_s.at[0], k.pg_r.at[o], place_p[0]).wait_recv()
    f_copies = []
    for d, place in enumerate(place_q):
        mine = k.out_pages.at[:, their_slot]
        f_copies.append(remote(mine, mine, k.pf_s.at[d], k.pf_r.at[their_slot], place))
    for copy in f_copies:
        copy.start()

    lax.fori_loop(0, jnp.minimum(2 * chip, 3), earlier, 0)

    for n in ("gain", "dt", "dt_bias", "a_log", "skip", "routing"):
        loads[n].wait()
    for o in others_x:
        for p in range(NZ):
            piece = low[p // 4].at[o, p % 4]
            remote(piece, piece, k.h_s.at[0, 0], k.h_r.at[o, p], place_x[0]).wait_recv()
    gain = k.in_gain[...].reshape(1, RANK + 2 * NST)
    left = k.low0[...].reshape(ROWS, WIDE[0]).astype(F32)
    right = k.low1[...].reshape(ROWS, WIDE[1]).astype(F32)
    mean = jnp.sum(left * left, axis=1, keepdims=True) + jnp.sum(right[:, :128] * right[:, :128], axis=1, keepdims=True)
    scale = lax.rsqrt(mean / RANK + EPS)
    k.rank[:, 0:384] = (left * scale * gain[:, 0:384]).astype(BF16)
    k.rank[:, 384:RANK] = (right[:, :128] * scale * gain[:, 384:RANK]).astype(BF16)
    both = right[:, 128 : 128 + 2 * NST]
    is_b = iota((ROWS, 2 * NST), 1) < NST
    power = both * both
    mean_b = jnp.sum(jnp.where(is_b, power, 0.0), axis=1, keepdims=True) / NST
    mean_c = jnp.sum(jnp.where(is_b, 0.0, power), axis=1, keepdims=True) / NST
    scale = jnp.where(is_b, lax.rsqrt(mean_b + EPS), lax.rsqrt(mean_c + EPS))
    k.bc[...] = (both * scale * gain[:, RANK : RANK + 2 * NST]).astype(BF16)

    raw = dot(k.rank[...], k.in_dt[...]) + k.in_dt_bias[...]
    step = jnp.maximum(raw, 0.0) + jnp.log(1.0 + jnp.exp(-jnp.abs(raw)))
    k.driven[...] = step * k.conv[...].astype(F32)
    start = jnp.where(k.ext_seg[7 : 7 + ROWS, :] != k.ext_seg[8:, :], HUGE, 0.0)
    for lane in range(0, WIDTH, LANES):
        k.step[:, lane : lane + LANES] = step[:, lane : lane + LANES] + start
    pick = (iota((NST, 2 * NST), 0) == iota((NST, 2 * NST), 1)).astype(BF16)
    b_all = dot_t(pick, k.bc[...])
    for b in range(16):
        k.b_cols[b, :, 0:16] = b_all[:, 16 * b : 16 * b + 16]
    pick = (iota((2 * NST, 256), 0) == NST + iota((2 * NST, 256), 1) % NST).astype(BF16)
    own = iota((ROWS, 256), 1) // NST == iota((ROWS, 256), 0) % 16
    k.c_blocks[...] = jnp.where(own, dot(k.bc[...], pick), 0.0).astype(BF16)
    rate = jnp.exp(k.in_a_log[...]) * (-LOG2E)

    def scan(b, carry):
        state, left = carry
        rows = pl.ds(pl.multiple_of(b * 16, 16), 16)
        steps, driven, b_cols = k.step[rows, :], k.driven[rows, :], k.b_cols[b]
        for t in range(16):
            span = slice(NST * t, NST * (t + 1))
            decay = jnp.exp2(steps[t : t + 1, :] * rate)
            state = decay * state + b_cols[:, t : t + 1] * driven[t : t + 1, :]
            left = decay * left
            k.states[b, span, :] = state.astype(BF16)
            k.growth[b, span, :] = left.astype(BF16)
        return state, left

    begin = (jnp.zeros((NST, WIDTH), F32), jnp.ones((NST, WIDTH), F32))
    state, _ = lax.fori_loop(0, ROWS // 16, scan, begin)
    steps = jnp.sum(k.step[...], axis=0, keepdims=True)
    for i in range(4):
        k.own_end[NST * i : NST * (i + 1), :] = state[:, i * LANES : (i + 1) * LANES].astype(BF16)
    parts = []
    for _ in range(3):
        part = steps.astype(BF16).astype(F32)
        parts += [part[:, i * LANES : (i + 1) * LANES] for i in range(4)]
        steps = steps - part
    k.own_end[64:80, :] = jnp.concatenate(parts + [jnp.zeros((4, LANES), F32)], axis=0).astype(BF16)
    e_copies = []
    for d, place in enumerate(place_g):
        e_copies.append(remote(k.own_end, k.ends.at[grp], k.e_s.at[d], k.e_r.at[grp], place))
    for copy in e_copies:
        copy.start()
    k.ends[grp] = k.own_end[...]

    lax.fori_loop(jnp.minimum(2 * chip, 3), 2 * chip, earlier, 0)
    for h in range(2):
        k.out_attn[:, h * HD : (h + 1) * HD] = (k.accum[h, :, 0:HD] / k.accum[h, :, HD:]).astype(BF16)
    stores["attn"].start()
    sums = right[:, 128:256]
    inverse = lax.rsqrt(sums[:, SQUARES : SQUARES + 1] / FEATURES + EPS)
    k.out_expert[...] = (k.in_moe[...].astype(F32) * k.in_moe_gain[...] * inverse).astype(BF16)
    logits = (sums * inverse).T
    experts = iota((LANES, ROWS), 0) - 2 * NST
    first = jnp.sum(jnp.where(experts == k.in_routing[0:1, :], logits, 0.0), axis=0, keepdims=True)
    second = jnp.sum(jnp.where(experts == k.in_routing[1:2, :], logits, 0.0), axis=0, keepdims=True)
    top = jnp.maximum(first, second)
    first, second = jnp.exp(first - top), jnp.exp(second - top)
    k.out_gate[0:1, :] = first / (first + second)
    k.out_gate[1:2, :] = second / (first + second)
    stores["expert"].start()
    stores["gate"].start()

    for o in others_g:
        remote(k.own_end, k.ends.at[o], k.e_s.at[0], k.e_r.at[o], place_g[0]).wait_recv()
    sums_of = []
    for j in range(NG):
        part = k.ends[j, 64:80, :].astype(F32)
        sums_of.append(part[0:4] + part[4:8] + part[8:12])
    entering = []
    for i in range(4):
        cols = slice(i * LANES, (i + 1) * LANES)
        state = jnp.zeros((NST, LANES), F32)
        mine = state
        for j in range(NG):
            mine = jnp.where(grp == j, state, mine)
            kept = jnp.exp2(sums_of[j][i : i + 1, :] * rate[:, cols])
            state = kept * state + k.ends[j, NST * i : NST * (i + 1), :].astype(F32)
        entering.append(mine)
        for g in range(NG):
            k.own_final[g, 2 * i : 2 * i + 2, :] = state[2 * g : 2 * g + 2, :]
    final_copy = remote(k.own_final.at[grp], k.landed, k.f_s, k.f_r, across)
    final_copy.start()
    entering = jnp.concatenate(entering, axis=1).astype(BF16)

    def finish(b, carry):
        rows = pl.ds(pl.multiple_of(b * 16, 16), 16)
        grown = k.growth[b].reshape(16, NST, WIDTH) * entering[None] + k.states[b].reshape(16, NST, WIDTH)
        value = dot(k.c_blocks[rows, :], grown.reshape(256, WIDTH))
        value = value + k.in_skip[...] * k.conv[rows, :].astype(F32)
        k.out_mixed[rows, :] = (value * k.silu_z[rows, :]).astype(BF16)
        return carry

    lax.fori_loop(0, ROWS // 16, finish, 0, unroll=4)
    stores["mixed"].start()

    final_copy.wait()
    for i in range(4):
        k.out_final[:, i * LANES : (i + 1) * LANES] = k.landed[2 * i : 2 * i + 2, :]
    stores["final"].start()
    for o in others_q:
        theirs = k.out_pages.at[:, 3 - lax.rem(o, 4)]
        remote(theirs, theirs, k.pf_s.at[0], k.pf_r.at[3 - lax.rem(o, 4)], place_q[0]).wait_recv()
    for copy in x_copies + page_copies + f_copies + e_copies:
        copy.wait_send()
    for here, copy in z_copies:
        pl.when(here)(copy.wait_send)
    for h in range(2):

        @pl.when(z // 4 == h)
        def _(h=h):
            for copy in gathering(h, quarter, z):
                copy.wait_send()

    for p in range(NZ):
        for copy in forwards(p // 4, p % 4, p):
            copy.wait_send()
    lax.fori_loop(0, 2 * chip, swap_end, 0)
    for here, copy in kv_copies:
        pl.when(here)(copy.wait_send)
    for store in stores.values():
        store.wait()


def hand_out(*refs):
    count = len(OUTPUTS)
    source, target, stage = refs[:count], refs[count : 2 * count], refs[2 * count : 3 * count]
    read, write = refs[3 * count :]
    inward = [pltpu.make_async_copy(source[i], stage[i], read.at[i]) for i in range(count)]
    outward = [pltpu.make_async_copy(stage[i], target[i], write.at[i]) for i in range(count)]
    for copy in inward:
        copy.start()
    for i in range(count):
        inward[i].wait()
        outward[i].start()
    for copy in outward:
        copy.wait()


def local(
    mamba_x, mamba_z, conv_weight, conv_bias, x_proj, norm_gain, dt_proj, dt_bias, a_log, d_skip,
    segment_ids, queries, keys_values, kv_owner, moe_in, moe_gain, router, routing,
):
    inputs = dict(
        x=mamba_x, seg=segment_ids, conv_w=conv_weight, conv_b=conv_bias.reshape(1, -1), proj=x_proj.T,
        owner=kv_owner.reshape(1, -1), keys_values=keys_values, moe=moe_in, moe_gain=moe_gain.reshape(1, -1), router=router.T, q=queries,
        z=mamba_z, gain=norm_gain, dt=dt_proj, dt_bias=dt_bias.reshape(1, -1), a_log=a_log,
        skip=d_skip.reshape(1, -1), routing=routing.T,
    )
    shapes = tuple(jax.ShapeDtypeStruct(s, t) for _, s, t in OUTPUTS)
    results = pl.pallas_call(
        main_kernel,
        out_shape=shapes,
        in_specs=[ANY] * len(OPERANDS),
        out_specs=tuple([ANY] * len(OUTPUTS)),
        scratch_shapes=[pltpu.VMEM(s, t) for _, s, t in SCRATCH]
        + [pltpu.VMEM(s, t) for _, s, t in INPUTS]
        + [pltpu.VMEM(s, t) for n, s, t in OUTPUTS if n != "pages"]
        + [DMA(s) if s else DMA for _, s in SEMS],
        compiler_params=pltpu.CompilerParams(
            vmem_limit_bytes=62 << 20, collective_id=0, has_side_effects=True
        ),
        name="span",
    )(*[inputs[n] for n in OPERANDS])
    mixed, final, attn, pages, expert, gates = pl.pallas_call(
        hand_out,
        out_shape=shapes,
        in_specs=[ANY] * len(OUTPUTS),
        out_specs=tuple([ANY] * len(OUTPUTS)),
        scratch_shapes=[pltpu.VMEM(s, t) for _, s, t in OUTPUTS] + [DMA((len(OUTPUTS),))] * 2,
        compiler_params=pltpu.CompilerParams(vmem_limit_bytes=62 << 20),
        name="results",
    )(*results)
    return (mixed, final[None], attn, pages.reshape(1, 1, 1, NG * SLOTS, BLK, 2 * HD), expert, gates.T)


def solution(mesh):
    placed = (
        P(("sect", "grp"), "tp"),
        P(("sect", "grp"), "tp"),
        P(None, "tp"),
        P("tp"),
        P("tp", None),
        P(),
        P(None, "tp"),
        P("tp"),
        P(None, "tp"),
        P("tp"),
        P("sect", "grp"),
        P(("sect", "grp"), "tp"),
        P(("sect", "grp"), None, None),
        P("sect", "grp", None),
        P(("sect", "grp"), "tp"),
        P("tp"),
        P("tp", None),
        P(("sect", "grp"), None),
    )
    return jax.shard_map(
        local,
        mesh=mesh,
        in_specs=placed,
        out_specs=(
            P(("sect", "grp"), "tp"),
            P("sect", "grp", "tp"),
            P(("sect", "grp"), "tp"),
            P("sect", "grp", "tp", None, None, None),
            P(("sect", "grp"), "tp"),
            P(("sect", "grp"), None),
        ),
        check_vma=False,
    )
```

```python
import jax
import jax.numpy as jnp
from jax import lax
from jax.experimental import pallas as pl
from jax.experimental.pallas import tpu as pltpu
from jax.sharding import PartitionSpec as P

MESH = pl.DeviceIdType.MESH
F32 = jnp.float32
BF16 = jnp.bfloat16
I32 = jnp.int32

ROWS = 256
WIDTH = 512
RANK = 512
NST = 16
HD = 128
BLK = 16
LANES = 128
NX, NZ, NG = 4, 8, 8
PAY = 640
CUTS = (0, 384, 640)
WIDE = (384, 256)
SLOTS = 4
FEATURES = 8192
EPS = 1e-06
SQUARES = 2 * NST + 16
LOG2E = 1.4426950408889634
HUGE = 1e30
VMEM = pl.BlockSpec(memory_space=pltpu.VMEM)
ANY = pl.BlockSpec(memory_space=pl.ANY)
DMA = pltpu.SemaphoreType.DMA


def iota(shape, dim):
    return lax.broadcasted_iota(I32, shape, dim)


def dot(a, b, **kw):
    return jnp.dot(a, b, preferred_element_type=F32, **kw)


def dot_t(a, b, **kw):
    return lax.dot_general(a, b, (((1,), (1,)), ((), ())), preferred_element_type=F32, **kw)


def remote(src, dst, send, recv, where):
    return pltpu.make_async_remote_copy(
        src_ref=src, dst_ref=dst, send_sem=send, recv_sem=recv, device_id=where, device_id_type=MESH
    )


INPUTS = (
    ("x", (ROWS, WIDTH), BF16),
    ("seg", (1, ROWS), I32),
    ("conv_w", (4, WIDTH), F32),
    ("conv_b", (1, WIDTH), F32),
    ("proj", (RANK + 2 * NST, WIDTH), BF16),
    ("owner", (1, 16), I32),
    ("pair", (ROWS, 2, HD), BF16),
    ("moe", (ROWS, 256), BF16),
    ("moe_gain", (1, 256), F32),
    ("router", (16, 256), BF16),
    ("q", (ROWS, 2 * HD), BF16),
    ("z", (ROWS, WIDTH), BF16),
    ("gain", (RANK + 2 * NST,), F32),
    ("dt", (RANK, WIDTH), BF16),
    ("dt_bias", (1, WIDTH), F32),
    ("a_log", (NST, WIDTH), F32),
    ("skip", (1, WIDTH), F32),
    ("routing", (2, ROWS), I32),
)
OUTPUTS = (
    ("mixed", (ROWS, WIDTH), BF16),
    ("final", (2, WIDTH), F32),
    ("attn", (ROWS, 2 * HD), BF16),
    ("pages", (NG, SLOTS, BLK, 2 * HD), BF16),
    ("expert", (ROWS, 256), BF16),
    ("gate", (2, ROWS), F32),
)
OPERANDS = [n for n, _, _ in INPUTS if n != "pair"] + ["keys_values"]
SCRATCH = (
    ("pair", (ROWS, 2 * HD), BF16),
    ("rim", (16, WIDTH), BF16),
    ("rim_seg", (8, LANES), F32),
    ("seg_send", (8, LANES), F32),
    ("seg_out", (8, ROWS), F32),
    ("seg_all", (NG, 8, ROWS), F32),
    ("kv_all", (NG, ROWS, 2 * HD), BF16),
    ("ext", (8 + ROWS, WIDTH), F32),
    ("ext_seg", (8 + ROWS, LANES), F32),
    ("conv", (ROWS, WIDTH), BF16),
    ("pay", (ROWS, PAY), BF16),
    ("rx0", (NX, 64, WIDE[0]), BF16),
    ("rx1", (NX, 64, WIDE[1]), BF16),
    ("chunk0", (4, 16, WIDE[0]), BF16),
    ("chunk1", (4, 16, WIDE[1]), BF16),
    ("rz0", (NZ, 16, WIDE[0]), BF16),
    ("rz1", (NZ, 16, WIDE[1]), BF16),
    ("low0", (NX, 4, 16, WIDE[0]), BF16),
    ("low1", (NX, 4, 16, WIDE[1]), BF16),
    ("outgoing", (NG, BLK, 2 * HD), BF16),
    ("best", (2, ROWS, LANES), F32),
    ("accum", (2, ROWS, 2 * HD), F32),
    ("silu_z", (ROWS, WIDTH), F32),
    ("rank", (ROWS, RANK), BF16),
    ("bc", (ROWS, 2 * NST), BF16),
    ("step", (ROWS, WIDTH), F32),
    ("driven", (ROWS, WIDTH), F32),
    ("b_cols", (16, NST, LANES), F32),
    ("c_blocks", (ROWS, 256), BF16),
    ("states", (16, 256, WIDTH), BF16),
    ("growth", (16, 256, WIDTH), BF16),
    ("ends", (NG, 80, LANES), BF16),
    ("own_end", (80, LANES), BF16),
    ("own_final", (NG, 8, LANES), F32),
    ("landed", (8, LANES), F32),
)
SEMS = (
    ("load", (len(INPUTS),)), ("store", (len(OUTPUTS),)),
    ("rim_s", ()), ("rim_r", ()), ("rseg_s", ()), ("rseg_r", ()),
    ("kv_s", (NG,)), ("kv_r", (NG,)), ("sg_s", (NG,)), ("sg_r", (NG,)),
    ("sw_s", (NG,)), ("sw_r", (NG,)),
    ("pg_s", ()), ("pg_r", ()), ("pf_s", ()), ("pf_r", ()),
    ("x_s", (2,)), ("x_r", (2,)), ("z_s", (2,)), ("z_r", ()),
    ("g_s", ()), ("g_r", (2,)), ("h_s", (2,)), ("h_r", (2,)),
    ("e_s", ()), ("e_r", ()), ("f_s", ()), ("f_r", ()),
)


class Refs:
    pass


def main_kernel(*refs):
    k = Refs()
    names = ["hbm_" + n for n in OPERANDS] + ["hbm_out_" + n for n, _, _ in OUTPUTS]
    names += [n for n, _, _ in SCRATCH] + ["in_" + n for n, _, _ in INPUTS]
    names += ["out_" + n for n, _, _ in OUTPUTS if n != "pages"] + [n for n, _ in SEMS]
    for name, ref in zip(names, refs, strict=True):
        setattr(k, name, ref)
    k.out_pages = k.hbm_out_pages
    sect, tp, grp = lax.axis_index("sect"), lax.axis_index("tp"), lax.axis_index("grp")
    x, z = tp // NZ, tp % NZ
    chip, core = grp // 2, grp % 2
    twin = {"grp": grp + 1 - 2 * core}
    half_rows = pl.ds(pl.multiple_of(128 * core, 128), 128)
    loads = {}
    for i, (n, _, _) in enumerate(INPUTS):
        if n == "pair":
            src = k.hbm_keys_values.at[:, :, pl.ds(pl.multiple_of(tp // 4 * HD, HD), HD)]
        else:
            src = getattr(k, "hbm_" + n)
        loads[n] = pltpu.make_async_copy(src, getattr(k, "in_" + n), k.load.at[i])
        loads[n].start()
    stores = {}
    for i, (n, _, _) in enumerate(OUTPUTS):
        if n != "pages":
            stores[n] = pltpu.make_async_copy(getattr(k, "out_" + n), getattr(k, "hbm_out_" + n), k.store.at[i])

    quad = z // 4 * 4
    others_x = [lax.rem(x + d, NX) for d in range(1, NX)]
    others_z = [lax.rem(z + d, NZ) for d in range(1, NZ)]
    others_q = [quad + lax.rem(z + d, 4) for d in range(1, 4)]
    others_g = [lax.rem(grp + d, NG) for d in range(1, NG)]
    place_x = [{"tp": o * NZ + z} for o in others_x]
    place_z = [{"tp": x * NZ + o} for o in others_z]
    place_q = [{"tp": x * NZ + o} for o in others_q]
    place_g = [{"grp": o} for o in others_g]
    place_p = [{"sect": 1 - sect, "grp": o} for o in range(NG)]
    across = {"sect": 1 - sect}
    partners = place_x + place_z + place_g + place_p
    barrier = pltpu.get_barrier_semaphore()
    for place in partners:
        pl.semaphore_signal(barrier, inc=1, device_id=place, device_id_type=MESH)

    loads["x"].wait()
    loads["seg"].wait()
    seg_row = k.in_seg[...].astype(F32)
    seg_cols = jnp.broadcast_to(seg_row, (LANES, ROWS)).T
    k.ext_seg[8:, :] = seg_cols
    k.seg_send[...] = seg_cols[ROWS - 8 :, :]
    k.seg_out[...] = jnp.broadcast_to(seg_row, (8, ROWS))
    pl.semaphore_wait(barrier, len(partners))

    behind = {"grp": lax.rem(grp + 1, NG)}
    rim_copy = remote(k.in_x.at[ROWS - 16 : ROWS], k.rim, k.rim_s, k.rim_r, behind)
    rseg_copy = remote(k.seg_send, k.rim_seg, k.rseg_s, k.rseg_r, behind)
    rim_copy.start()
    rseg_copy.start()

    loads["pair"].wait()
    k.pair[...] = k.in_pair[...].reshape(ROWS, 2 * HD)
    kv_copies = []
    for d in range(1, NG):
        place = {"grp": lax.rem(grp + d, NG)}
        copy = remote(k.seg_out, k.seg_all.at[grp], k.sg_s.at[d], k.sg_r.at[grp], place)
        kv_copies.append((grp + d < NG, copy))
    for d in range(1, NG // 2):
        for half in range(2):
            rows = slice(128 * half, 128 * half + 128)
            place = {"grp": 2 * lax.rem(chip + d, NG // 2) + half}
            copy = remote(k.pair.at[rows], k.kv_all.at[grp, rows], k.kv_s.at[2 * d + half], k.kv_r.at[grp], place)
            kv_copies.append((chip + d < NG // 2, copy))
    kv_copies.append((core == 0, remote(k.pair, k.kv_all.at[grp], k.kv_s.at[0], k.kv_r.at[grp], twin)))
    for here, copy in kv_copies:
        pl.when(here)(copy.start)

    loads["owner"].wait()
    owners = jnp.broadcast_to(k.in_owner[...].astype(F32), (8, 16)).astype(BF16)
    owner_of = dot(owners, (iota((16, ROWS), 0) == iota((16, ROWS), 1) // BLK).astype(BF16))[0:1, :]
    owner_lanes = dot(owners, (iota((16, LANES), 0) == iota((16, LANES), 1)).astype(BF16))[0:1, :]
    owner_rows = jnp.broadcast_to(owner_lanes, (LANES, LANES)).T[0:16, 0:1]
    before = (owner_rows == owner_of) & (iota((16, ROWS), 0) < iota((16, ROWS), 1) // BLK)
    order = jnp.sum(jnp.where(before, 1.0, 0.0), axis=0, keepdims=True)
    slot = jnp.where(order == lax.rem(z, 4).astype(F32), owner_of, -1.0)
    row, col = iota((NG * BLK, ROWS), 0), iota((NG * BLK, ROWS), 1)
    choose = (slot == (row // BLK).astype(F32)) & (row % BLK == col % BLK)
    chosen = dot(jnp.where(choose, 1.0, 0.0).astype(BF16), k.pair[...])
    k.outgoing[...] = chosen.astype(BF16).reshape(NG, BLK, 2 * HD)
    my_slot = lax.rem(z, 4)
    page_copies = []
    for o in range(NG):
        dst = k.out_pages.at[grp, my_slot]
        page_copies.append(remote(k.outgoing.at[o], dst, k.pg_s, k.pg_r, place_p[o]))
    for copy in page_copies:
        copy.start()

    loads["moe"].wait()
    loads["moe_gain"].wait()
    loads["router"].wait()
    moe_rows = k.in_moe[...].astype(F32)
    spread = (iota((LANES, 16), 0) == iota((LANES, 16), 1) + 2 * NST).astype(BF16)
    router = dot(spread, k.in_router[...])
    logits_part = dot_t(moe_rows * k.in_moe_gain[...], router, precision=lax.Precision.HIGHEST)
    squares = jnp.sum(moe_rows * moe_rows, axis=1, keepdims=True)
    tail = jnp.where(iota((ROWS, LANES), 1) == SQUARES, squares, logits_part)

    k.ext[8:, :] = k.in_x[...].astype(F32)
    loads["conv_w"].wait()
    loads["conv_b"].wait()
    loads["proj"].wait()
    rim_copy.wait()
    rseg_copy.wait()
    k.ext[0:8, :] = k.rim[8:16, :].astype(F32)
    k.ext_seg[0:8, :] = jnp.where(grp == 0, -1.0, k.rim_seg[...])
    here = k.ext_seg[8:, :]
    same = [k.ext_seg[5 + i : 5 + i + ROWS, :] == here for i in range(3)]
    for lane in range(0, WIDTH, LANES):
        cols = slice(lane, lane + LANES)
        value = jnp.broadcast_to(k.in_conv_b[:, cols], (ROWS, LANES))
        for i in range(4):
            term = k.ext[5 + i : 5 + i + ROWS, cols] * k.in_conv_w[i : i + 1, cols]
            value = value + (jnp.where(same[i], term, 0.0) if i < 3 else term)
        k.conv[:, cols] = (value / (1.0 + jnp.exp(-value))).astype(BF16)
    conv = k.conv[...]

    rx, chunk, rz, low = (k.rx0, k.rx1), (k.chunk0, k.chunk1), (k.rz0, k.rz1), (k.low0, k.low1)
    for h in range(2):
        if h == 0:
            k.pay[:, 0:384] = dot_t(conv, k.in_proj[0:384, :]).astype(BF16)
        else:
            k.pay[:, 384:RANK] = dot_t(conv, k.in_proj[384:RANK, :]).astype(BF16)
            spread = (iota((LANES, 2 * NST), 0) == iota((LANES, 2 * NST), 1)).astype(BF16)
            last = dot(spread, k.in_proj[RANK:, :]).astype(BF16)
            k.pay[:, RANK:PAY] = (dot_t(conv, last) + tail).astype(BF16)
        for o, place in zip(others_x, place_x):
            src = k.pay.at[pl.ds(pl.multiple_of(o * 64, 64), 64), CUTS[h] : CUTS[h + 1]]
            remote(src, rx[h].at[x], k.x_s.at[h], k.x_r.at[h], place).start()

    factor = HD**-0.5 * LOG2E

    ones = jnp.ones((ROWS, HD), BF16)

    def attend(key_block, value_block, allowed, first):
        valued = jnp.concatenate([value_block, ones], axis=1)
        for h in range(2):
            scores = dot_t(k.in_q[:, h * HD : (h + 1) * HD], key_block)
            masked = jnp.where(allowed, scores, -HUGE)
            high = jnp.max(masked, axis=1, keepdims=True)
            if first:
                new = high
                weights = jnp.exp2((masked - new) * factor)
                k.accum[h] = dot(weights.astype(BF16), valued)
            else:
                old = k.best[h][:, 0:1]
                new = jnp.maximum(old, high)
                weights = jnp.exp2((masked - new) * factor)
                fade = jnp.exp2((old - new) * factor)
                k.accum[h] = k.accum[h] * fade + dot(weights.astype(BF16), valued)
            k.best[h] = jnp.broadcast_to(new, (ROWS, LANES))

    def attend_block(j):
        remote(k.seg_out, k.seg_all.at[j], k.sg_s.at[0], k.sg_r.at[j], place_g[0]).wait_recv()
        same = k.seg_all[j, 0:1, :] == k.ext_seg[8:, 0:1]
        attend(k.kv_all[j, :, 0:HD], k.kv_all[j, :, HD:], same, False)

    def swap(i):
        block = k.kv_all.at[2 * chip - 1 - i, half_rows]
        return remote(block, block, k.sw_s.at[i], k.sw_r.at[i], twin)

    def swap_start(i, carry):
        block = k.kv_all.at[2 * chip - 1 - i, half_rows]
        remote(block, block, k.sw_s.at[i], k.kv_r.at[2 * chip - 1 - i], twin).wait_recv()
        swap(i).start()
        return carry

    def swap_end(i, carry):
        swap(i).wait_send()
        return carry

    def earlier(i, carry):
        swap(i).wait_recv()
        attend_block(2 * chip - 1 - i)
        return carry

    loads["q"].wait()
    causal = iota((ROWS, ROWS), 1) <= iota((ROWS, ROWS), 0)
    attend(k.pair[:, 0:HD], k.pair[:, HD:], causal & (seg_row == k.ext_seg[8:, 0:1]), True)

    for h in range(2):
        remote(rx[h].at[0:3], rx[h].at[0:3], k.x_s.at[h], k.x_r.at[h], place_x[0]).wait_recv()
        summed = k.pay[pl.ds(pl.multiple_of(x * 64, 64), 64), CUTS[h] : CUTS[h + 1]].astype(F32)
        for o in others_x:
            summed = summed + rx[h][o].astype(F32)
        for r in range(4):
            chunk[h][r] = summed[16 * r : 16 * r + 16, :].astype(BF16)
        for r in range(4):
            o = 4 * h + r
            copy = remote(chunk[h].at[r], rz[h].at[z], k.z_s.at[h], k.z_r, {"tp": x * NZ + o})
            pl.when(z != o)(copy.start)

    loads["z"].wait()
    gate = k.in_z[...].astype(F32)
    k.silu_z[...] = gate / (1.0 + jnp.exp(-gate))


    @pl.when(core == 1)
    def _():
        remote(k.pair, k.kv_all.at[grp - 1], k.kv_s.at[0], k.kv_r.at[grp - 1], twin).wait_recv()
        attend_block(grp - 1)

    quarter = lax.rem(z, 4)
    for h in range(2):

        @pl.when(z // 4 == h)
        def _(h=h):
            remote(rz[h].at[0:7], rz[h].at[0:7], k.g_s, k.z_r, place_z[0]).wait_recv()
            summed = chunk[h][quarter].astype(F32)
            for o in others_z:
                summed = summed + rz[h][o].astype(F32)
            low[h][x, quarter] = summed.astype(BF16)
            piece = low[h].at[x, quarter]
            for place in place_z:
                remote(piece, piece, k.g_s, k.g_r.at[h], place).start()
            for part in (h, 1 - h):
                whole = low[part].at[x]
                landing = low[part].at[x, 0:3] if part == h else whole
                remote(landing, landing, k.g_s, k.g_r.at[part], place_z[0]).wait_recv()
                for place in place_x:
                    remote(whole, whole, k.h_s.at[part], k.h_r.at[part], place).start()

    lax.fori_loop(0, 2 * chip, swap_start, 0)

    remote(k.outgoing, k.outgoing, k.pg_s, k.pg_r, place_p[0]).wait_recv()
    f_copies = []
    for d, place in enumerate(place_q):
        mine = k.out_pages.at[:, my_slot]
        f_copies.append(remote(mine, mine, k.pf_s, k.pf_r, place))
    for copy in f_copies:
        copy.start()

    lax.fori_loop(0, jnp.minimum(2 * chip, 3), earlier, 0)

    for n in ("gain", "dt", "dt_bias", "a_log", "skip", "routing"):
        loads[n].wait()
    for h in range(2):
        remote(low[h].at[0:3], low[h].at[0:3], k.h_s.at[h], k.h_r.at[h], place_x[0]).wait_recv()
    gain = k.in_gain[...].reshape(1, RANK + 2 * NST)
    left = k.low0[...].reshape(ROWS, WIDE[0]).astype(F32)
    right = k.low1[...].reshape(ROWS, WIDE[1]).astype(F32)
    mean = jnp.sum(left * left, axis=1, keepdims=True) + jnp.sum(right[:, :128] * right[:, :128], axis=1, keepdims=True)
    scale = lax.rsqrt(mean / RANK + EPS)
    k.rank[:, 0:384] = (left * scale * gain[:, 0:384]).astype(BF16)
    k.rank[:, 384:RANK] = (right[:, :128] * scale * gain[:, 384:RANK]).astype(BF16)
    both = right[:, 128 : 128 + 2 * NST]
    is_b = iota((ROWS, 2 * NST), 1) < NST
    power = both * both
    mean_b = jnp.sum(jnp.where(is_b, power, 0.0), axis=1, keepdims=True) / NST
    mean_c = jnp.sum(jnp.where(is_b, 0.0, power), axis=1, keepdims=True) / NST
    scale = jnp.where(is_b, lax.rsqrt(mean_b + EPS), lax.rsqrt(mean_c + EPS))
    k.bc[...] = (both * scale * gain[:, RANK : RANK + 2 * NST]).astype(BF16)

    raw = dot(k.rank[...], k.in_dt[...]) + k.in_dt_bias[...]
    step = jnp.maximum(raw, 0.0) + jnp.log(1.0 + jnp.exp(-jnp.abs(raw)))
    k.driven[...] = step * k.conv[...].astype(F32)
    start = jnp.where(k.ext_seg[7 : 7 + ROWS, :] != k.ext_seg[8:, :], HUGE, 0.0)
    for lane in range(0, WIDTH, LANES):
        k.step[:, lane : lane + LANES] = step[:, lane : lane + LANES] + start
    pick = (iota((NST, 2 * NST), 0) == iota((NST, 2 * NST), 1)).astype(BF16)
    b_all = dot_t(pick, k.bc[...])
    for b in range(16):
        k.b_cols[b, :, 0:16] = b_all[:, 16 * b : 16 * b + 16]
    pick = (iota((2 * NST, 256), 0) == NST + iota((2 * NST, 256), 1) % NST).astype(BF16)
    own = iota((ROWS, 256), 1) // NST == iota((ROWS, 256), 0) % 16
    k.c_blocks[...] = jnp.where(own, dot(k.bc[...], pick), 0.0).astype(BF16)
    rate = jnp.exp(k.in_a_log[...]) * (-LOG2E)

    def scan(b, carry):
        state, left = carry
        rows = pl.ds(pl.multiple_of(b * 16, 16), 16)
        steps, driven, b_cols = k.step[rows, :], k.driven[rows, :], k.b_cols[b]
        for t in range(16):
            span = slice(NST * t, NST * (t + 1))
            decay = jnp.exp2(steps[t : t + 1, :] * rate)
            state = decay * state + b_cols[:, t : t + 1] * driven[t : t + 1, :]
            left = decay * left
            k.states[b, span, :] = state.astype(BF16)
            k.growth[b, span, :] = left.astype(BF16)
        return state, left

    begin = (jnp.zeros((NST, WIDTH), F32), jnp.ones((NST, WIDTH), F32))
    state, _ = lax.fori_loop(0, ROWS // 16, scan, begin)
    steps = jnp.sum(k.step[...], axis=0, keepdims=True)
    for i in range(4):
        k.own_end[NST * i : NST * (i + 1), :] = state[:, i * LANES : (i + 1) * LANES].astype(BF16)
    parts = []
    for _ in range(3):
        part = steps.astype(BF16).astype(F32)
        parts += [part[:, i * LANES : (i + 1) * LANES] for i in range(4)]
        steps = steps - part
    k.own_end[64:80, :] = jnp.concatenate(parts + [jnp.zeros((4, LANES), F32)], axis=0).astype(BF16)
    for place in place_g:
        remote(k.own_end, k.ends.at[grp], k.e_s, k.e_r, place).start()
    k.ends[grp] = k.own_end[...]

    lax.fori_loop(jnp.minimum(2 * chip, 3), 2 * chip, earlier, 0)
    for h in range(2):
        k.out_attn[:, h * HD : (h + 1) * HD] = (k.accum[h, :, 0:HD] / k.accum[h, :, HD:]).astype(BF16)
    stores["attn"].start()
    sums = right[:, 128:256]
    inverse = lax.rsqrt(sums[:, SQUARES : SQUARES + 1] / FEATURES + EPS)
    k.out_expert[...] = (k.in_moe[...].astype(F32) * k.in_moe_gain[...] * inverse).astype(BF16)
    logits = (sums * inverse).T
    experts = iota((LANES, ROWS), 0) - 2 * NST
    first = jnp.sum(jnp.where(experts == k.in_routing[0:1, :], logits, 0.0), axis=0, keepdims=True)
    second = jnp.sum(jnp.where(experts == k.in_routing[1:2, :], logits, 0.0), axis=0, keepdims=True)
    top = jnp.maximum(first, second)
    first, second = jnp.exp(first - top), jnp.exp(second - top)
    k.out_gate[0:1, :] = first / (first + second)
    k.out_gate[1:2, :] = second / (first + second)
    stores["expert"].start()
    stores["gate"].start()

    remote(k.ends.at[0:7], k.ends.at[0:7], k.e_s, k.e_r, place_g[0]).wait_recv()
    sums_of = []
    for j in range(NG):
        part = k.ends[j, 64:80, :].astype(F32)
        sums_of.append(part[0:4] + part[4:8] + part[8:12])
    entering = []
    for i in range(4):
        cols = slice(i * LANES, (i + 1) * LANES)
        state = jnp.zeros((NST, LANES), F32)
        mine = state
        for j in range(NG):
            mine = jnp.where(grp == j, state, mine)
            kept = jnp.exp2(sums_of[j][i : i + 1, :] * rate[:, cols])
            state = kept * state + k.ends[j, NST * i : NST * (i + 1), :].astype(F32)
        entering.append(mine)
        for g in range(NG):
            k.own_final[g, 2 * i : 2 * i + 2, :] = state[2 * g : 2 * g + 2, :]
    final_copy = remote(k.own_final.at[grp], k.landed, k.f_s, k.f_r, across)
    final_copy.start()
    entering = jnp.concatenate(entering, axis=1).astype(BF16)

    def finish(b, carry):
        rows = pl.ds(pl.multiple_of(b * 16, 16), 16)
        grown = k.growth[b].reshape(16, NST, WIDTH) * entering[None] + k.states[b].reshape(16, NST, WIDTH)
        value = dot(k.c_blocks[rows, :], grown.reshape(256, WIDTH))
        value = value + k.in_skip[...] * k.conv[rows, :].astype(F32)
        k.out_mixed[rows, :] = (value * k.silu_z[rows, :]).astype(BF16)
        return carry

    lax.fori_loop(0, ROWS // 16, finish, 0, unroll=4)
    stores["mixed"].start()

    final_copy.wait()
    for i in range(4):
        k.out_final[:, i * LANES : (i + 1) * LANES] = k.landed[2 * i : 2 * i + 2, :]
    stores["final"].start()
    rest = k.out_pages.at[:, 0:3]
    remote(rest, rest, k.pf_s, k.pf_r, place_q[0]).wait()
    remote(k.outgoing, k.outgoing, k.pg_s, k.pg_r, place_p[0]).wait_send()
    remote(k.ends.at[0:7], k.ends.at[0:7], k.e_s, k.e_r, place_g[0]).wait_send()
    for h in range(2):
        remote(rx[h].at[0:3], rx[h].at[0:3], k.x_s.at[h], k.x_r.at[h], place_x[0]).wait_send()
        remote(low[h].at[0:3], low[h].at[0:3], k.h_s.at[h], k.h_r.at[h], place_x[0]).wait_send()

        @pl.when(z // 4 == h)
        def _(h=h):
            remote(rz[h].at[0:7], rz[h].at[0:7], k.g_s, k.g_r.at[h], place_z[0]).wait_send()
            remote(rz[h].at[0:3], rz[h].at[0:3], k.z_s.at[h], k.z_r, place_z[0]).wait_send()

        @pl.when(z // 4 != h)
        def _(h=h):
            remote(rz[h].at[0:4], rz[h].at[0:4], k.z_s.at[h], k.z_r, place_z[0]).wait_send()

    lax.fori_loop(0, 2 * chip, swap_end, 0)
    for here, copy in kv_copies:
        pl.when(here)(copy.wait_send)
    for store in stores.values():
        store.wait()


def hand_out(*refs):
    count = len(OUTPUTS)
    source, target, stage = refs[:count], refs[count : 2 * count], refs[2 * count : 3 * count]
    read, write = refs[3 * count :]
    inward = [pltpu.make_async_copy(source[i], stage[i], read.at[i]) for i in range(count)]
    outward = [pltpu.make_async_copy(stage[i], target[i], write.at[i]) for i in range(count)]
    for copy in inward:
        copy.start()
    for i in range(count):
        inward[i].wait()
        outward[i].start()
    for copy in outward:
        copy.wait()


def local(
    mamba_x, mamba_z, conv_weight, conv_bias, x_proj, norm_gain, dt_proj, dt_bias, a_log, d_skip,
    segment_ids, queries, keys_values, kv_owner, moe_in, moe_gain, router, routing,
):
    inputs = dict(
        x=mamba_x, seg=segment_ids, conv_w=conv_weight, conv_b=conv_bias.reshape(1, -1), proj=x_proj.T,
        owner=kv_owner.reshape(1, -1), keys_values=keys_values, moe=moe_in, moe_gain=moe_gain.reshape(1, -1), router=router.T, q=queries,
        z=mamba_z, gain=norm_gain, dt=dt_proj, dt_bias=dt_bias.reshape(1, -1), a_log=a_log,
        skip=d_skip.reshape(1, -1), routing=routing.T,
    )
    shapes = tuple(jax.ShapeDtypeStruct(s, t) for _, s, t in OUTPUTS)
    results = pl.pallas_call(
        main_kernel,
        out_shape=shapes,
        in_specs=[ANY] * len(OPERANDS),
        out_specs=tuple([ANY] * len(OUTPUTS)),
        scratch_shapes=[pltpu.VMEM(s, t) for _, s, t in SCRATCH]
        + [pltpu.VMEM(s, t) for _, s, t in INPUTS]
        + [pltpu.VMEM(s, t) for n, s, t in OUTPUTS if n != "pages"]
        + [DMA(s) if s else DMA for _, s in SEMS],
        compiler_params=pltpu.CompilerParams(
            vmem_limit_bytes=62 << 20, collective_id=0, has_side_effects=True
        ),
        name="span",
    )(*[inputs[n] for n in OPERANDS])
    mixed, final, attn, pages, expert, gates = pl.pallas_call(
        hand_out,
        out_shape=shapes,
        in_specs=[ANY] * len(OUTPUTS),
        out_specs=tuple([ANY] * len(OUTPUTS)),
        scratch_shapes=[pltpu.VMEM(s, t) for _, s, t in OUTPUTS] + [DMA((len(OUTPUTS),))] * 2,
        compiler_params=pltpu.CompilerParams(vmem_limit_bytes=62 << 20),
        name="results",
    )(*results)
    return (mixed, final[None], attn, pages.reshape(1, 1, 1, NG * SLOTS, BLK, 2 * HD), expert, gates.T)


def solution(mesh):
    placed = (
        P(("sect", "grp"), "tp"),
        P(("sect", "grp"), "tp"),
        P(None, "tp"),
        P("tp"),
        P("tp", None),
        P(),
        P(None, "tp"),
        P("tp"),
        P(None, "tp"),
        P("tp"),
        P("sect", "grp"),
        P(("sect", "grp"), "tp"),
        P(("sect", "grp"), None, None),
        P("sect", "grp", None),
        P(("sect", "grp"), "tp"),
        P("tp"),
        P("tp", None),
        P(("sect", "grp"), None),
    )
    return jax.shard_map(
        local,
        mesh=mesh,
        in_specs=placed,
        out_specs=(
            P(("sect", "grp"), "tp"),
            P("sect", "grp", "tp"),
            P(("sect", "grp"), "tp"),
            P("sect", "grp", "tp", None, None, None),
            P(("sect", "grp"), "tp"),
            P(("sect", "grp"), None),
        ),
        check_vma=False,
    )
```

```python
import jax
import jax.numpy as jnp
from jax import lax
from jax.experimental import pallas as pl
from jax.experimental.pallas import tpu as pltpu
from jax.sharding import PartitionSpec as P

MESH = pl.DeviceIdType.MESH
F32 = jnp.float32
BF16 = jnp.bfloat16
I32 = jnp.int32

ROWS = 256
WIDTH = 512
RANK = 512
NST = 16
HD = 128
BLK = 16
LANES = 128
NX, NZ, NG = 4, 8, 8
PAY = 640
CUTS = (0, 384, 640)
WIDE = (384, 256)
SLOTS = 4
FEATURES = 8192
EPS = 1e-06
SQUARES = 2 * NST + 16
FIRST = 2
LOG2E = 1.4426950408889634
HUGE = 1e30
VMEM = pl.BlockSpec(memory_space=pltpu.VMEM)
ANY = pl.BlockSpec(memory_space=pl.ANY)
DMA = pltpu.SemaphoreType.DMA


def iota(shape, dim):
    return lax.broadcasted_iota(I32, shape, dim)


def dot(a, b, **kw):
    return jnp.dot(a, b, preferred_element_type=F32, **kw)


def dot_t(a, b, **kw):
    return lax.dot_general(a, b, (((1,), (1,)), ((), ())), preferred_element_type=F32, **kw)


def remote(src, dst, send, recv, where):
    return pltpu.make_async_remote_copy(
        src_ref=src, dst_ref=dst, send_sem=send, recv_sem=recv, device_id=where, device_id_type=MESH
    )


INPUTS = (
    ("x", (ROWS, WIDTH), BF16),
    ("seg", (1, ROWS), I32),
    ("conv_w", (4, WIDTH), F32),
    ("conv_b", (1, WIDTH), F32),
    ("proj", (RANK + 2 * NST, WIDTH), BF16),
    ("owner", (1, 16), I32),
    ("pair", (ROWS, 2, HD), BF16),
    ("moe", (ROWS, 256), BF16),
    ("moe_gain", (1, 256), F32),
    ("router", (16, 256), BF16),
    ("q", (ROWS, 2 * HD), BF16),
    ("z", (ROWS, WIDTH), BF16),
    ("gain", (RANK + 2 * NST,), F32),
    ("dt", (RANK, WIDTH), BF16),
    ("dt_bias", (1, WIDTH), F32),
    ("a_log", (NST, WIDTH), F32),
    ("skip", (1, WIDTH), F32),
    ("routing", (2, ROWS), I32),
)
OUTPUTS = (
    ("mixed", (ROWS, WIDTH), BF16),
    ("final", (2, WIDTH), F32),
    ("attn", (ROWS, 2 * HD), BF16),
    ("pages", (NG, SLOTS, BLK, 2 * HD), BF16),
    ("expert", (ROWS, 256), BF16),
    ("gate", (2, ROWS), F32),
)
OPERANDS = [n for n, _, _ in INPUTS if n != "pair"] + ["keys_values"]
SCRATCH = (
    ("pair", (ROWS, 2 * HD), BF16),
    ("rim", (16, WIDTH), BF16),
    ("rim_seg", (8, LANES), F32),
    ("seg_send", (8, LANES), F32),
    ("seg_out", (8, ROWS), F32),
    ("seg_all", (NG, 8, ROWS), F32),
    ("kv_all", (NG, ROWS, 2 * HD), BF16),
    ("ext", (8 + ROWS, WIDTH), F32),
    ("ext_seg", (8 + ROWS, LANES), F32),
    ("conv", (ROWS, WIDTH), BF16),
    ("pay", (ROWS, PAY), BF16),
    ("rx0", (NX, 64, WIDE[0]), BF16),
    ("rx1", (NX, 64, WIDE[1]), BF16),
    ("chunk0", (4, 16, WIDE[0]), BF16),
    ("chunk1", (4, 16, WIDE[1]), BF16),
    ("rz0", (NZ, 16, WIDE[0]), BF16),
    ("rz1", (NZ, 16, WIDE[1]), BF16),
    ("low", (NX, 4, 16, PAY), BF16),
    ("outgoing", (NG, BLK, 2 * HD), BF16),
    ("best", (2, ROWS, LANES), F32),
    ("accum", (2, ROWS, 2 * HD), F32),
    ("silu_z", (ROWS, WIDTH), F32),
    ("rank", (ROWS, RANK), BF16),
    ("bc", (ROWS, 2 * NST), BF16),
    ("step", (ROWS, WIDTH), F32),
    ("driven", (ROWS, WIDTH), F32),
    ("b_cols", (16, NST, LANES), F32),
    ("c_blocks", (ROWS, 256), BF16),
    ("states", (16, 256, WIDTH), BF16),
    ("growth", (16, 256, WIDTH), BF16),
    ("ends", (NG, 80, LANES), BF16),
    ("own_end", (80, LANES), BF16),
    ("own_final", (NG, 8, LANES), F32),
    ("landed", (8, LANES), F32),
)
SEMS = (
    ("load", (len(INPUTS),)), ("store", (len(OUTPUTS),)),
    ("rim_s", ()), ("rim_r", ()), ("rseg_s", ()), ("rseg_r", ()),
    ("kv_s", (NG,)), ("kv_r", (NG,)), ("sg_s", (NG,)), ("sg_r", (NG,)),
    ("sw_s", (NG,)), ("sw_r", (NG,)),
    ("pg_s", ()), ("pg_r", ()), ("pf_s", ()), ("pf_r", ()),
    ("x_s", (2,)), ("x_r", (2,)), ("z_s", (2,)), ("z_r", (2,)),
    ("g_s", (NZ,)), ("g_r", (4,)), ("h_s", ()), ("h_r", ()),
    ("e_s", ()), ("e_r", ()), ("f_s", ()), ("f_r", ()),
)


class Refs:
    pass


def main_kernel(*refs):
    k = Refs()
    names = ["hbm_" + n for n in OPERANDS] + ["hbm_out_" + n for n, _, _ in OUTPUTS]
    names += [n for n, _, _ in SCRATCH] + ["in_" + n for n, _, _ in INPUTS]
    names += ["out_" + n for n, _, _ in OUTPUTS if n != "pages"] + [n for n, _ in SEMS]
    for name, ref in zip(names, refs, strict=True):
        setattr(k, name, ref)
    k.out_pages = k.hbm_out_pages
    sect, tp, grp = lax.axis_index("sect"), lax.axis_index("tp"), lax.axis_index("grp")
    x, z = tp // NZ, tp % NZ
    chip, core = grp // 2, grp % 2
    twin = {"grp": grp + 1 - 2 * core}
    half_rows = pl.ds(pl.multiple_of(128 * core, 128), 128)
    loads = {}
    for i, (n, _, _) in enumerate(INPUTS):
        if n == "pair":
            src = k.hbm_keys_values.at[:, :, pl.ds(pl.multiple_of(tp // 4 * HD, HD), HD)]
        else:
            src = getattr(k, "hbm_" + n)
        loads[n] = pltpu.make_async_copy(src, getattr(k, "in_" + n), k.load.at[i])
        loads[n].start()
    stores = {}
    for i, (n, _, _) in enumerate(OUTPUTS):
        if n != "pages":
            stores[n] = pltpu.make_async_copy(getattr(k, "out_" + n), getattr(k, "hbm_out_" + n), k.store.at[i])

    quad = z // 4 * 4
    others_x = [lax.rem(x + d, NX) for d in range(1, NX)]
    others_z = [lax.rem(z + d, NZ) for d in range(1, NZ)]
    others_q = [quad + lax.rem(z + d, 4) for d in range(1, 4)]
    others_g = [lax.rem(grp + d, NG) for d in range(1, NG)]
    place_x = [{"tp": o * NZ + z} for o in others_x]
    place_z = [{"tp": x * NZ + o} for o in others_z]
    place_q = [{"tp": x * NZ + o} for o in others_q]
    place_g = [{"grp": o} for o in others_g]
    place_p = [{"sect": 1 - sect, "grp": o} for o in range(NG)]
    across = {"sect": 1 - sect}
    partners = place_x + place_z + place_g + place_p
    barrier = pltpu.get_barrier_semaphore()
    for place in partners:
        pl.semaphore_signal(barrier, inc=1, device_id=place, device_id_type=MESH)

    loads["x"].wait()
    loads["seg"].wait()
    seg_row = k.in_seg[...].astype(F32)
    seg_cols = jnp.broadcast_to(seg_row, (LANES, ROWS)).T
    k.ext_seg[8:, :] = seg_cols
    k.seg_send[...] = seg_cols[ROWS - 8 :, :]
    k.seg_out[...] = jnp.broadcast_to(seg_row, (8, ROWS))
    pl.semaphore_wait(barrier, len(partners))

    behind = {"grp": lax.rem(grp + 1, NG)}
    rim_copy = remote(k.in_x.at[ROWS - 16 : ROWS], k.rim, k.rim_s, k.rim_r, behind)
    rseg_copy = remote(k.seg_send, k.rim_seg, k.rseg_s, k.rseg_r, behind)
    rim_copy.start()
    rseg_copy.start()

    loads["pair"].wait()
    k.pair[...] = k.in_pair[...].reshape(ROWS, 2 * HD)
    kv_copies = []
    for d in range(1, NG):
        place = {"grp": lax.rem(grp + d, NG)}
        copy = remote(k.seg_out, k.seg_all.at[grp], k.sg_s.at[d], k.sg_r.at[grp], place)
        kv_copies.append((grp + d < NG, copy))
    for d in range(1, NG // 2):
        for half in range(2):
            rows = slice(128 * half, 128 * half + 128)
            place = {"grp": 2 * lax.rem(chip + d, NG // 2) + half}
            copy = remote(k.pair.at[rows], k.kv_all.at[grp, rows], k.kv_s.at[2 * d + half], k.kv_r.at[grp], place)
            kv_copies.append((chip + d < NG // 2, copy))
    kv_copies.append((core == 0, remote(k.pair, k.kv_all.at[grp], k.kv_s.at[0], k.kv_r.at[grp], twin)))
    for here, copy in kv_copies:
        pl.when(here)(copy.start)

    loads["owner"].wait()
    owners = jnp.broadcast_to(k.in_owner[...].astype(F32), (8, 16)).astype(BF16)
    owner_of = dot(owners, (iota((16, ROWS), 0) == iota((16, ROWS), 1) // BLK).astype(BF16))[0:1, :]
    owner_lanes = dot(owners, (iota((16, LANES), 0) == iota((16, LANES), 1)).astype(BF16))[0:1, :]
    owner_rows = jnp.broadcast_to(owner_lanes, (LANES, LANES)).T[0:16, 0:1]
    before = (owner_rows == owner_of) & (iota((16, ROWS), 0) < iota((16, ROWS), 1) // BLK)
    order = jnp.sum(jnp.where(before, 1.0, 0.0), axis=0, keepdims=True)
    slot = jnp.where(order == lax.rem(z, 4).astype(F32), owner_of, -1.0)
    row, col = iota((NG * BLK, ROWS), 0), iota((NG * BLK, ROWS), 1)
    choose = (slot == (row // BLK).astype(F32)) & (row % BLK == col % BLK)
    chosen = dot(jnp.where(choose, 1.0, 0.0).astype(BF16), k.pair[...])
    k.outgoing[...] = chosen.astype(BF16).reshape(NG, BLK, 2 * HD)
    my_slot = lax.rem(z, 4)
    page_copies = []
    for o in range(NG):
        dst = k.out_pages.at[grp, my_slot]
        page_copies.append(remote(k.outgoing.at[o], dst, k.pg_s, k.pg_r, place_p[o]))
    for copy in page_copies:
        copy.start()

    loads["moe"].wait()
    loads["moe_gain"].wait()
    loads["router"].wait()
    moe_rows = k.in_moe[...].astype(F32)
    spread = (iota((LANES, 16), 0) == iota((LANES, 16), 1) + 2 * NST).astype(BF16)
    router = dot(spread, k.in_router[...])
    logits_part = dot_t(moe_rows * k.in_moe_gain[...], router, precision=lax.Precision.HIGHEST)
    squares = jnp.sum(moe_rows * moe_rows, axis=1, keepdims=True)
    tail = jnp.where(iota((ROWS, LANES), 1) == SQUARES, squares, logits_part)

    k.ext[8:, :] = k.in_x[...].astype(F32)
    loads["conv_w"].wait()
    loads["conv_b"].wait()
    loads["proj"].wait()
    rim_copy.wait()
    rseg_copy.wait()
    k.ext[0:8, :] = k.rim[8:16, :].astype(F32)
    k.ext_seg[0:8, :] = jnp.where(grp == 0, -1.0, k.rim_seg[...])
    here = k.ext_seg[8:, :]
    same = [k.ext_seg[5 + i : 5 + i + ROWS, :] == here for i in range(3)]
    for lane in range(0, WIDTH, LANES):
        cols = slice(lane, lane + LANES)
        value = jnp.broadcast_to(k.in_conv_b[:, cols], (ROWS, LANES))
        for i in range(4):
            term = k.ext[5 + i : 5 + i + ROWS, cols] * k.in_conv_w[i : i + 1, cols]
            value = value + (jnp.where(same[i], term, 0.0) if i < 3 else term)
        k.conv[:, cols] = (value / (1.0 + jnp.exp(-value))).astype(BF16)
    conv = k.conv[...]

    rx, chunk, rz, low = (k.rx0, k.rx1), (k.chunk0, k.chunk1), (k.rz0, k.rz1), k.low
    for h in range(2):
        if h == 0:
            k.pay[:, 0:384] = dot_t(conv, k.in_proj[0:384, :]).astype(BF16)
        else:
            k.pay[:, 384:RANK] = dot_t(conv, k.in_proj[384:RANK, :]).astype(BF16)
            spread = (iota((LANES, 2 * NST), 0) == iota((LANES, 2 * NST), 1)).astype(BF16)
            last = dot(spread, k.in_proj[RANK:, :]).astype(BF16)
            k.pay[:, RANK:PAY] = (dot_t(conv, last) + tail).astype(BF16)
        for o, place in zip(others_x, place_x):
            src = k.pay.at[pl.ds(pl.multiple_of(o * 64, 64), 64), CUTS[h] : CUTS[h + 1]]
            remote(src, rx[h].at[x], k.x_s.at[h], k.x_r.at[h], place).start()

    factor = HD**-0.5 * LOG2E

    def attend(key_block, value_block, allowed, first):
        valued = jnp.concatenate([value_block, jnp.ones_like(value_block)], axis=1)
        for h in range(2):
            scores = dot_t(k.in_q[:, h * HD : (h + 1) * HD], key_block)
            masked = jnp.where(allowed, scores, -HUGE)
            high = jnp.max(masked, axis=1, keepdims=True)
            if first:
                new = high
                weights = jnp.exp2((masked - new) * factor)
                k.accum[h] = dot(weights.astype(BF16), valued)
            else:
                old = k.best[h][:, 0:1]
                new = jnp.maximum(old, high)
                weights = jnp.exp2((masked - new) * factor)
                fade = jnp.exp2((old - new) * factor)
                k.accum[h] = k.accum[h] * fade + dot(weights.astype(BF16), valued)
            k.best[h] = jnp.broadcast_to(new, (ROWS, LANES))

    def ids_of(j):
        remote(k.seg_out, k.seg_all.at[j], k.sg_s.at[0], k.sg_r.at[j], place_g[0]).wait_recv()
        return k.seg_all[j, 0:1, :]

    def swap(i):
        block = k.kv_all.at[2 * chip - 1 - i, half_rows]
        return remote(block, block, k.sw_s.at[i], k.sw_r.at[i], twin)

    def swap_start(i, carry):
        block = k.kv_all.at[2 * chip - 1 - i, half_rows]
        remote(block, block, k.sw_s.at[i], k.kv_r.at[2 * chip - 1 - i], twin).wait_recv()
        swap(i).start()
        return carry

    def swap_end(i, carry):
        swap(i).wait_send()
        return carry

    def earlier(i, carry):
        pair = 2 * (chip - 1 - i)
        swap(2 * i).wait_recv()
        swap(2 * i + 1).wait_recv()
        same = jnp.concatenate([ids_of(pair), ids_of(pair + 1)], axis=1) == k.ext_seg[8:, 0:1]
        block = k.kv_all[pl.ds(pair, 2)].reshape(2 * ROWS, 2 * HD)
        attend(block[:, 0:HD], block[:, HD:], same, False)
        return carry

    loads["q"].wait()
    causal = iota((ROWS, ROWS), 1) <= iota((ROWS, ROWS), 0)
    attend(k.pair[:, 0:HD], k.pair[:, HD:], causal & (seg_row == k.ext_seg[8:, 0:1]), True)

    for h in range(2):
        remote(rx[h].at[0:3], rx[h].at[0:3], k.x_s.at[h], k.x_r.at[h], place_x[0]).wait_recv()
        summed = k.pay[pl.ds(pl.multiple_of(x * 64, 64), 64), CUTS[h] : CUTS[h + 1]].astype(F32)
        for o in others_x:
            summed = summed + rx[h][o].astype(F32)
        for r in range(4):
            chunk[h][r] = summed[16 * r : 16 * r + 16, :].astype(BF16)
        for r in range(4):
            copy = remote(chunk[h].at[r], rz[h].at[z], k.z_s.at[h], k.z_r.at[h], {"tp": x * NZ + FIRST + r})
            pl.when(z != FIRST + r)(copy.start)

    loads["z"].wait()
    gate = k.in_z[...].astype(F32)
    k.silu_z[...] = gate / (1.0 + jnp.exp(-gate))


    @pl.when(core == 1)
    def _():
        remote(k.pair, k.kv_all.at[grp - 1], k.kv_s.at[0], k.kv_r.at[grp - 1], twin).wait_recv()
        same = ids_of(grp - 1) == k.ext_seg[8:, 0:1]
        attend(k.kv_all[grp - 1, :, 0:HD], k.kv_all[grp - 1, :, HD:], same, False)

    is_owner = (z >= FIRST) & (z < FIRST + 4)
    quarter = jnp.clip(z - FIRST, 0, 3)

    def forward(r):
        piece = low.at[x, r]
        for place in place_x:
            remote(piece, piece, k.h_s, k.h_r, place).start()

    loads["gain"].wait()

    @pl.when(is_owner)
    def _():
        sums = []
        for h in range(2):
            remote(rz[h].at[0:7], rz[h].at[0:7], k.z_s.at[h], k.z_r.at[h], place_z[0]).wait_recv()
            summed = chunk[h][quarter].astype(F32)
            for o in others_z:
                summed = summed + rz[h][o].astype(F32)
            sums.append(summed)
        left, right = sums
        rank, last = right[:, 0:128], right[:, 128:256]
        gain = k.in_gain[...].reshape(1, RANK + 2 * NST)
        mean = jnp.sum(left * left, axis=1, keepdims=True) + jnp.sum(rank * rank, axis=1, keepdims=True)
        scale = lax.rsqrt(mean / RANK + EPS)
        low[x, quarter, :, 0:384] = (left * scale * gain[:, 0:384]).astype(BF16)
        low[x, quarter, :, 384:RANK] = (rank * scale * gain[:, 384:RANK]).astype(BF16)
        lanes = iota((16, LANES), 1)
        power = last * last
        mean_b = jnp.sum(jnp.where(lanes < NST, power, 0.0), axis=1, keepdims=True) / NST
        mean_c = jnp.sum(jnp.where((lanes >= NST) & (lanes < 2 * NST), power, 0.0), axis=1, keepdims=True) / NST
        inverse = lax.rsqrt(last[:, SQUARES : SQUARES + 1] / FEATURES + EPS)
        coarse = inverse.astype(BF16).astype(F32)
        scale = jnp.where(lanes < NST, lax.rsqrt(mean_b + EPS), lax.rsqrt(mean_c + EPS))
        last = last * jnp.where(lanes < 2 * NST, scale, inverse)
        last = jnp.where(lanes == SQUARES, coarse, jnp.where(lanes == SQUARES + 1, inverse - coarse, last))
        low[x, quarter, :, RANK:PAY] = last.astype(BF16)
        low[x, quarter, :, RANK : RANK + 2 * NST] = (last[:, 0 : 2 * NST] * gain[:, RANK:]).astype(BF16)
        piece = low.at[x, quarter]
        for d, place in enumerate(place_z):
            remote(piece, piece, k.g_s.at[d], k.g_r.at[quarter], place).start()
        forward(quarter)

    for r in range(4):

        @pl.when(z != FIRST + r)
        def _(r=r):
            piece = low.at[x, r]
            remote(piece, piece, k.g_s.at[0], k.g_r.at[r], place_z[0]).wait_recv()
            forward(r)

    lax.fori_loop(0, 2 * chip, swap_start, 0)

    remote(k.outgoing, k.outgoing, k.pg_s, k.pg_r, place_p[0]).wait_recv()
    f_copies = []
    for d, place in enumerate(place_q):
        mine = k.out_pages.at[:, my_slot]
        f_copies.append(remote(mine, mine, k.pf_s, k.pf_r, place))
    for copy in f_copies:
        copy.start()


    for n in ("dt", "dt_bias", "a_log", "skip", "routing"):
        loads[n].wait()
    remote(low.at[0:3], low.at[0:3], k.h_s, k.h_r, place_x[0]).wait_recv()
    k.rank[...] = low[...].reshape(ROWS, PAY)[:, 0:RANK]
    shared = low[...].reshape(ROWS, PAY)[:, RANK:PAY]
    k.bc[...] = shared[:, 0 : 2 * NST]

    raw = dot(k.rank[...], k.in_dt[...]) + k.in_dt_bias[...]
    step = jnp.maximum(raw, 0.0) + jnp.log(1.0 + jnp.exp(-jnp.abs(raw)))
    k.driven[...] = step * k.conv[...].astype(F32)
    start = jnp.where(k.ext_seg[7 : 7 + ROWS, :] != k.ext_seg[8:, :], HUGE, 0.0)
    for lane in range(0, WIDTH, LANES):
        k.step[:, lane : lane + LANES] = step[:, lane : lane + LANES] + start
    pick = (iota((NST, 2 * NST), 0) == iota((NST, 2 * NST), 1)).astype(BF16)
    b_all = dot_t(pick, k.bc[...])
    for b in range(16):
        k.b_cols[b, :, 0:16] = b_all[:, 16 * b : 16 * b + 16]
    pick = (iota((2 * NST, 256), 0) == NST + iota((2 * NST, 256), 1) % NST).astype(BF16)
    own = iota((ROWS, 256), 1) // NST == iota((ROWS, 256), 0) % 16
    k.c_blocks[...] = jnp.where(own, dot(k.bc[...], pick), 0.0).astype(BF16)
    rate = jnp.exp(k.in_a_log[...]) * (-LOG2E)

    def scan(b, carry):
        state, left = carry
        rows = pl.ds(pl.multiple_of(b * 16, 16), 16)
        steps, driven, b_cols = k.step[rows, :], k.driven[rows, :], k.b_cols[b]
        for t in range(16):
            span = slice(NST * t, NST * (t + 1))
            decay = jnp.exp2(steps[t : t + 1, :] * rate)
            state = decay * state + b_cols[:, t : t + 1] * driven[t : t + 1, :]
            left = decay * left
            k.states[b, span, :] = state.astype(BF16)
            k.growth[b, span, :] = left.astype(BF16)
        return state, left

    begin = (jnp.zeros((NST, WIDTH), F32), jnp.ones((NST, WIDTH), F32))
    state, _ = lax.fori_loop(0, ROWS // 16, scan, begin)
    steps = jnp.sum(k.step[...], axis=0, keepdims=True)
    for i in range(4):
        k.own_end[NST * i : NST * (i + 1), :] = state[:, i * LANES : (i + 1) * LANES].astype(BF16)
    parts = []
    for _ in range(3):
        part = steps.astype(BF16).astype(F32)
        parts += [part[:, i * LANES : (i + 1) * LANES] for i in range(4)]
        steps = steps - part
    k.own_end[64:80, :] = jnp.concatenate(parts + [jnp.zeros((4, LANES), F32)], axis=0).astype(BF16)
    for place in place_g:
        remote(k.own_end, k.ends.at[grp], k.e_s, k.e_r, place).start()
    k.ends[grp] = k.own_end[...]

    lax.fori_loop(0, chip, earlier, 0)
    for h in range(2):
        k.out_attn[:, h * HD : (h + 1) * HD] = (k.accum[h, :, 0:HD] / k.accum[h, :, HD:]).astype(BF16)
    stores["attn"].start()
    shared = shared.astype(F32)
    inverse = shared[:, SQUARES : SQUARES + 1] + shared[:, SQUARES + 1 : SQUARES + 2]
    k.out_expert[...] = (k.in_moe[...].astype(F32) * k.in_moe_gain[...] * inverse).astype(BF16)
    logits = shared.T
    experts = iota((LANES, ROWS), 0) - 2 * NST
    first = jnp.sum(jnp.where(experts == k.in_routing[0:1, :], logits, 0.0), axis=0, keepdims=True)
    second = jnp.sum(jnp.where(experts == k.in_routing[1:2, :], logits, 0.0), axis=0, keepdims=True)
    top = jnp.maximum(first, second)
    first, second = jnp.exp(first - top), jnp.exp(second - top)
    k.out_gate[0:1, :] = first / (first + second)
    k.out_gate[1:2, :] = second / (first + second)
    stores["expert"].start()
    stores["gate"].start()

    remote(k.ends.at[0:7], k.ends.at[0:7], k.e_s, k.e_r, place_g[0]).wait_recv()
    sums_of = []
    for j in range(NG):
        part = k.ends[j, 64:80, :].astype(F32)
        sums_of.append(part[0:4] + part[4:8] + part[8:12])
    entering = []
    for i in range(4):
        cols = slice(i * LANES, (i + 1) * LANES)
        state = jnp.zeros((NST, LANES), F32)
        mine = state
        for j in range(NG):
            mine = jnp.where(grp == j, state, mine)
            kept = jnp.exp2(sums_of[j][i : i + 1, :] * rate[:, cols])
            state = kept * state + k.ends[j, NST * i : NST * (i + 1), :].astype(F32)
        entering.append(mine)
        for g in range(NG):
            k.own_final[g, 2 * i : 2 * i + 2, :] = state[2 * g : 2 * g + 2, :]
    final_copy = remote(k.own_final.at[grp], k.landed, k.f_s, k.f_r, across)
    final_copy.start()
    entering = jnp.concatenate(entering, axis=1).astype(BF16)

    def finish(b, carry):
        rows = pl.ds(pl.multiple_of(b * 16, 16), 16)
        grown = k.growth[b].reshape(16, NST, WIDTH) * entering[None] + k.states[b].reshape(16, NST, WIDTH)
        value = dot(k.c_blocks[rows, :], grown.reshape(256, WIDTH))
        value = value + k.in_skip[...] * k.conv[rows, :].astype(F32)
        k.out_mixed[rows, :] = (value * k.silu_z[rows, :]).astype(BF16)
        return carry

    lax.fori_loop(0, ROWS // 16, finish, 0, unroll=4)
    stores["mixed"].start()

    final_copy.wait()
    for i in range(4):
        k.out_final[:, i * LANES : (i + 1) * LANES] = k.landed[2 * i : 2 * i + 2, :]
    stores["final"].start()
    rest = k.out_pages.at[:, 0:3]
    remote(rest, rest, k.pf_s, k.pf_r, place_q[0]).wait()
    remote(k.outgoing, k.outgoing, k.pg_s, k.pg_r, place_p[0]).wait_send()
    remote(k.ends.at[0:7], k.ends.at[0:7], k.e_s, k.e_r, place_g[0]).wait_send()
    for h in range(2):
        remote(rx[h].at[0:3], rx[h].at[0:3], k.x_s.at[h], k.x_r.at[h], place_x[0]).wait_send()

        @pl.when(is_owner)
        def _(h=h):
            remote(rz[h].at[0:3], rz[h].at[0:3], k.z_s.at[h], k.z_r.at[h], place_z[0]).wait_send()

        @pl.when(jnp.logical_not(is_owner))
        def _(h=h):
            remote(rz[h].at[0:4], rz[h].at[0:4], k.z_s.at[h], k.z_r.at[h], place_z[0]).wait_send()

    remote(low.at[0:3], low.at[0:3], k.h_s, k.h_r, place_x[0]).wait_send()

    @pl.when(is_owner)
    def _():
        for d in range(NZ - 1):
            remote(low.at[x, 0], low.at[x, 0], k.g_s.at[d], k.g_r.at[0], place_z[0]).wait_send()

    lax.fori_loop(0, 2 * chip, swap_end, 0)
    for here, copy in kv_copies:
        pl.when(here)(copy.wait_send)
    for store in stores.values():
        store.wait()


def hand_out(*refs):
    count = len(OUTPUTS)
    source, target, stage = refs[:count], refs[count : 2 * count], refs[2 * count : 3 * count]
    read, write = refs[3 * count :]
    inward = [pltpu.make_async_copy(source[i], stage[i], read.at[i]) for i in range(count)]
    outward = [pltpu.make_async_copy(stage[i], target[i], write.at[i]) for i in range(count)]
    for copy in inward:
        copy.start()
    for i in range(count):
        inward[i].wait()
        outward[i].start()
    for copy in outward:
        copy.wait()


def local(
    mamba_x, mamba_z, conv_weight, conv_bias, x_proj, norm_gain, dt_proj, dt_bias, a_log, d_skip,
    segment_ids, queries, keys_values, kv_owner, moe_in, moe_gain, router, routing,
):
    inputs = dict(
        x=mamba_x, seg=segment_ids, conv_w=conv_weight, conv_b=conv_bias.reshape(1, -1), proj=x_proj.T,
        owner=kv_owner.reshape(1, -1), keys_values=keys_values, moe=moe_in, moe_gain=moe_gain.reshape(1, -1), router=router.T, q=queries,
        z=mamba_z, gain=norm_gain, dt=dt_proj, dt_bias=dt_bias.reshape(1, -1), a_log=a_log,
        skip=d_skip.reshape(1, -1), routing=routing.T,
    )
    shapes = tuple(jax.ShapeDtypeStruct(s, t) for _, s, t in OUTPUTS)
    results = pl.pallas_call(
        main_kernel,
        out_shape=shapes,
        in_specs=[ANY] * len(OPERANDS),
        out_specs=tuple([ANY] * len(OUTPUTS)),
        scratch_shapes=[pltpu.VMEM(s, t) for _, s, t in SCRATCH]
        + [pltpu.VMEM(s, t) for _, s, t in INPUTS]
        + [pltpu.VMEM(s, t) for n, s, t in OUTPUTS if n != "pages"]
        + [DMA(s) if s else DMA for _, s in SEMS],
        compiler_params=pltpu.CompilerParams(
            vmem_limit_bytes=62 << 20, collective_id=0, has_side_effects=True
        ),
        name="span",
    )(*[inputs[n] for n in OPERANDS])
    mixed, final, attn, pages, expert, gates = pl.pallas_call(
        hand_out,
        out_shape=shapes,
        in_specs=[ANY] * len(OUTPUTS),
        out_specs=tuple([ANY] * len(OUTPUTS)),
        scratch_shapes=[pltpu.VMEM(s, t) for _, s, t in OUTPUTS] + [DMA((len(OUTPUTS),))] * 2,
        compiler_params=pltpu.CompilerParams(vmem_limit_bytes=62 << 20),
        name="results",
    )(*results)
    return (mixed, final[None], attn, pages.reshape(1, 1, 1, NG * SLOTS, BLK, 2 * HD), expert, gates.T)


def solution(mesh):
    placed = (
        P(("sect", "grp"), "tp"),
        P(("sect", "grp"), "tp"),
        P(None, "tp"),
        P("tp"),
        P("tp", None),
        P(),
        P(None, "tp"),
        P("tp"),
        P(None, "tp"),
        P("tp"),
        P("sect", "grp"),
        P(("sect", "grp"), "tp"),
        P(("sect", "grp"), None, None),
        P("sect", "grp", None),
        P(("sect", "grp"), "tp"),
        P("tp"),
        P("tp", None),
        P(("sect", "grp"), None),
    )
    return jax.shard_map(
        local,
        mesh=mesh,
        in_specs=placed,
        out_specs=(
            P(("sect", "grp"), "tp"),
            P("sect", "grp", "tp"),
            P(("sect", "grp"), "tp"),
            P("sect", "grp", "tp", None, None, None),
            P(("sect", "grp"), "tp"),
            P(("sect", "grp"), None),
        ),
        check_vma=False,
    )
```

```python
import jax
import jax.numpy as jnp
from jax import lax
from jax.experimental import pallas as pl
from jax.experimental.pallas import tpu as pltpu
from jax.sharding import PartitionSpec as P

MESH = pl.DeviceIdType.MESH
F32 = jnp.float32
BF16 = jnp.bfloat16
I32 = jnp.int32

ROWS = 256
WIDTH = 512
RANK = 512
NST = 16
HD = 128
BLK = 16
LANES = 128
NX, NZ, NG = 4, 8, 8
PAY = 640
CUTS = (0, 384, 640)
WIDE = (384, 256)
SLOTS = 4
FEATURES = 8192
EPS = 1e-06
SQUARES = 2 * NST + 16
FIRST = 2
LOG2E = 1.4426950408889634
HUGE = 1e30
VMEM = pl.BlockSpec(memory_space=pltpu.VMEM)
ANY = pl.BlockSpec(memory_space=pl.ANY)
DMA = pltpu.SemaphoreType.DMA


def iota(shape, dim):
    return lax.broadcasted_iota(I32, shape, dim)


def dot(a, b, **kw):
    return jnp.dot(a, b, preferred_element_type=F32, **kw)


def dot_t(a, b, **kw):
    return lax.dot_general(a, b, (((1,), (1,)), ((), ())), preferred_element_type=F32, **kw)


def remote(src, dst, send, recv, where):
    return pltpu.make_async_remote_copy(
        src_ref=src, dst_ref=dst, send_sem=send, recv_sem=recv, device_id=where, device_id_type=MESH
    )


INPUTS = (
    ("x", (ROWS, WIDTH), BF16),
    ("seg", (1, ROWS), I32),
    ("conv_w", (4, WIDTH), F32),
    ("conv_b", (1, WIDTH), F32),
    ("proj", (RANK + 2 * NST, WIDTH), BF16),
    ("owner", (1, 16), I32),
    ("pair", (ROWS, 2, HD), BF16),
    ("moe", (ROWS, 256), BF16),
    ("moe_gain", (1, 256), F32),
    ("router", (16, 256), BF16),
    ("q", (ROWS, 2 * HD), BF16),
    ("z", (ROWS, WIDTH), BF16),
    ("gain", (RANK + 2 * NST,), F32),
    ("dt", (RANK, WIDTH), BF16),
    ("dt_bias", (1, WIDTH), F32),
    ("a_log", (NST, WIDTH), F32),
    ("skip", (1, WIDTH), F32),
    ("routing", (2, ROWS), I32),
)
OUTPUTS = (
    ("mixed", (ROWS, WIDTH), BF16),
    ("final", (2, WIDTH), F32),
    ("attn", (ROWS, 2 * HD), BF16),
    ("pages", (NG, SLOTS, BLK, 2 * HD), BF16),
    ("expert", (ROWS, 256), BF16),
    ("gate", (2, ROWS), F32),
)
OPERANDS = [n for n, _, _ in INPUTS if n != "pair"] + ["keys_values"]
SCRATCH = (
    ("pair", (ROWS, 2 * HD), BF16),
    ("rim", (16, WIDTH), BF16),
    ("rim_seg", (8, LANES), F32),
    ("seg_send", (8, LANES), F32),
    ("seg_out", (8, ROWS), F32),
    ("seg_all", (NG, 8, ROWS), F32),
    ("kv_all", (NG, ROWS, 2 * HD), BF16),
    ("ext", (8 + ROWS, WIDTH), F32),
    ("ext_seg", (8 + ROWS, LANES), F32),
    ("conv", (ROWS, WIDTH), BF16),
    ("pay", (ROWS, PAY), BF16),
    ("rx0", (NX, 64, WIDE[0]), BF16),
    ("rx1", (NX, 64, WIDE[1]), BF16),
    ("chunk0", (4, 16, WIDE[0]), BF16),
    ("chunk1", (4, 16, WIDE[1]), BF16),
    ("rz0", (NZ, 16, WIDE[0]), BF16),
    ("rz1", (NZ, 16, WIDE[1]), BF16),
    ("low", (NX, 4, 16, PAY), BF16),
    ("outgoing", (NG, BLK, 2 * HD), BF16),
    ("best", (2, ROWS, LANES), F32),
    ("accum", (2, ROWS, 2 * HD), F32),
    ("silu_z", (ROWS, WIDTH), F32),
    ("rank", (ROWS, RANK), BF16),
    ("bc", (ROWS, 2 * NST), BF16),
    ("step", (ROWS, WIDTH), F32),
    ("driven", (ROWS, WIDTH), F32),
    ("b_cols", (16, NST, LANES), F32),
    ("c_blocks", (ROWS, 256), BF16),
    ("states", (16, 256, WIDTH), BF16),
    ("growth", (16, 256, WIDTH), BF16),
    ("ends", (NG, 80, LANES), BF16),
    ("own_end", (80, LANES), BF16),
    ("own_final", (NG, 8, LANES), F32),
    ("landed", (8, LANES), F32),
)
SEMS = (
    ("load", (len(INPUTS),)), ("store", (len(OUTPUTS),)),
    ("rim_s", ()), ("rim_r", ()), ("rseg_s", ()), ("rseg_r", ()),
    ("kv_s", (NG,)), ("kv_r", (NG,)), ("sg_s", (NG,)), ("sg_r", (NG,)),
    ("sw_s", (NG,)), ("sw_r", (NG,)),
    ("pg_s", ()), ("pg_r", ()), ("pf_s", ()), ("pf_r", ()),
    ("x_s", (2,)), ("x_r", (2,)), ("z_s", (2,)), ("z_r", (2,)),
    ("g_s", (NZ,)), ("g_r", (4,)), ("h_s", ()), ("h_r", ()),
    ("e_s", ()), ("e_r", ()), ("f_s", ()), ("f_r", ()),
)


class Refs:
    pass


def main_kernel(*refs):
    k = Refs()
    names = ["hbm_" + n for n in OPERANDS] + ["hbm_out_" + n for n, _, _ in OUTPUTS]
    names += [n for n, _, _ in SCRATCH] + ["in_" + n for n, _, _ in INPUTS]
    names += ["out_" + n for n, _, _ in OUTPUTS if n != "pages"] + [n for n, _ in SEMS]
    for name, ref in zip(names, refs, strict=True):
        setattr(k, name, ref)
    k.out_pages = k.hbm_out_pages
    sect, tp, grp = lax.axis_index("sect"), lax.axis_index("tp"), lax.axis_index("grp")
    x, z = tp // NZ, tp % NZ
    chip, core = grp // 2, grp % 2
    twin = {"grp": grp + 1 - 2 * core}
    half_rows = pl.ds(pl.multiple_of(128 * core, 128), 128)
    loads = {}
    for i, (n, _, _) in enumerate(INPUTS):
        if n == "pair":
            src = k.hbm_keys_values.at[:, :, pl.ds(pl.multiple_of(tp // 4 * HD, HD), HD)]
        else:
            src = getattr(k, "hbm_" + n)
        loads[n] = pltpu.make_async_copy(src, getattr(k, "in_" + n), k.load.at[i])
        loads[n].start()
    stores = {}
    for i, (n, _, _) in enumerate(OUTPUTS):
        if n != "pages":
            stores[n] = pltpu.make_async_copy(getattr(k, "out_" + n), getattr(k, "hbm_out_" + n), k.store.at[i])

    quad = z // 4 * 4
    others_x = [lax.rem(x + d, NX) for d in range(1, NX)]
    others_z = [lax.rem(z + d, NZ) for d in range(1, NZ)]
    others_q = [quad + lax.rem(z + d, 4) for d in range(1, 4)]
    others_g = [lax.rem(grp + d, NG) for d in range(1, NG)]
    place_x = [{"tp": o * NZ + z} for o in others_x]
    place_z = [{"tp": x * NZ + o} for o in others_z]
    place_q = [{"tp": x * NZ + o} for o in others_q]
    place_g = [{"grp": o} for o in others_g]
    place_p = [{"sect": 1 - sect, "grp": o} for o in range(NG)]
    across = {"sect": 1 - sect}
    partners = place_x + place_z + place_g + place_p
    barrier = pltpu.get_barrier_semaphore()
    for place in partners:
        pl.semaphore_signal(barrier, inc=1, device_id=place, device_id_type=MESH)

    loads["x"].wait()
    loads["seg"].wait()
    seg_row = k.in_seg[...].astype(F32)
    seg_cols = jnp.broadcast_to(seg_row, (LANES, ROWS)).T
    k.ext_seg[8:, :] = seg_cols
    k.seg_send[...] = seg_cols[ROWS - 8 :, :]
    k.seg_out[...] = jnp.broadcast_to(seg_row, (8, ROWS))
    pl.semaphore_wait(barrier, len(partners))

    behind = {"grp": lax.rem(grp + 1, NG)}
    rim_copy = remote(k.in_x.at[ROWS - 16 : ROWS], k.rim, k.rim_s, k.rim_r, behind)
    rseg_copy = remote(k.seg_send, k.rim_seg, k.rseg_s, k.rseg_r, behind)
    rim_copy.start()
    rseg_copy.start()

    loads["pair"].wait()
    k.pair[...] = k.in_pair[...].reshape(ROWS, 2 * HD)

    loads["owner"].wait()
    owners = jnp.broadcast_to(k.in_owner[...].astype(F32), (8, 16)).astype(BF16)
    owner_of = dot(owners, (iota((16, ROWS), 0) == iota((16, ROWS), 1) // BLK).astype(BF16))[0:1, :]
    owner_lanes = dot(owners, (iota((16, LANES), 0) == iota((16, LANES), 1)).astype(BF16))[0:1, :]
    owner_rows = jnp.broadcast_to(owner_lanes, (LANES, LANES)).T[0:16, 0:1]
    before = (owner_rows == owner_of) & (iota((16, ROWS), 0) < iota((16, ROWS), 1) // BLK)
    order = jnp.sum(jnp.where(before, 1.0, 0.0), axis=0, keepdims=True)
    slot = jnp.where(order == lax.rem(z, 4).astype(F32), owner_of, -1.0)
    row, col = iota((NG * BLK, ROWS), 0), iota((NG * BLK, ROWS), 1)
    choose = (slot == (row // BLK).astype(F32)) & (row % BLK == col % BLK)
    chosen = dot(jnp.where(choose, 1.0, 0.0).astype(BF16), k.pair[...])
    k.outgoing[...] = chosen.astype(BF16).reshape(NG, BLK, 2 * HD)
    my_slot = lax.rem(z, 4)
    page_copies = []
    for o in range(NG):
        dst = k.out_pages.at[grp, my_slot]
        page_copies.append(remote(k.outgoing.at[o], dst, k.pg_s, k.pg_r, place_p[o]))

    loads["moe"].wait()
    loads["moe_gain"].wait()
    loads["router"].wait()
    moe_rows = k.in_moe[...].astype(F32)
    spread = (iota((LANES, 16), 0) == iota((LANES, 16), 1) + 2 * NST).astype(BF16)
    router = dot(spread, k.in_router[...])
    logits_part = dot_t(moe_rows * k.in_moe_gain[...], router, precision=lax.Precision.HIGHEST)
    squares = jnp.sum(moe_rows * moe_rows, axis=1, keepdims=True)
    tail = jnp.where(iota((ROWS, LANES), 1) == SQUARES, squares, logits_part)

    k.ext[8:, :] = k.in_x[...].astype(F32)
    loads["conv_w"].wait()
    loads["conv_b"].wait()
    loads["proj"].wait()
    rim_copy.wait()
    rseg_copy.wait()
    k.ext[0:8, :] = k.rim[8:16, :].astype(F32)
    k.ext_seg[0:8, :] = jnp.where(grp == 0, -1.0, k.rim_seg[...])
    here = k.ext_seg[8:, :]
    same = [k.ext_seg[5 + i : 5 + i + ROWS, :] == here for i in range(3)]
    for lane in range(0, WIDTH, LANES):
        cols = slice(lane, lane + LANES)
        value = jnp.broadcast_to(k.in_conv_b[:, cols], (ROWS, LANES))
        for i in range(4):
            term = k.ext[5 + i : 5 + i + ROWS, cols] * k.in_conv_w[i : i + 1, cols]
            value = value + (jnp.where(same[i], term, 0.0) if i < 3 else term)
        k.conv[:, cols] = (value / (1.0 + jnp.exp(-value))).astype(BF16)
    conv = k.conv[...]

    rx, chunk, rz, low = (k.rx0, k.rx1), (k.chunk0, k.chunk1), (k.rz0, k.rz1), k.low
    for h in range(2):
        if h == 0:
            k.pay[:, 0:384] = dot_t(conv, k.in_proj[0:384, :]).astype(BF16)
        else:
            k.pay[:, 384:RANK] = dot_t(conv, k.in_proj[384:RANK, :]).astype(BF16)
            spread = (iota((LANES, 2 * NST), 0) == iota((LANES, 2 * NST), 1)).astype(BF16)
            last = dot(spread, k.in_proj[RANK:, :]).astype(BF16)
            k.pay[:, RANK:PAY] = (dot_t(conv, last) + tail).astype(BF16)
        for o, place in zip(others_x, place_x):
            src = k.pay.at[pl.ds(pl.multiple_of(o * 64, 64), 64), CUTS[h] : CUTS[h + 1]]
            remote(src, rx[h].at[x], k.x_s.at[h], k.x_r.at[h], place).start()

    for copy in page_copies:
        copy.start()

    factor = HD**-0.5 * LOG2E

    def attend(key_block, value_block, allowed, first):
        valued = jnp.concatenate([value_block, jnp.ones_like(value_block)], axis=1)
        for h in range(2):
            scores = dot_t(k.in_q[:, h * HD : (h + 1) * HD], key_block)
            masked = jnp.where(allowed, scores, -HUGE)
            high = jnp.max(masked, axis=1, keepdims=True)
            if first:
                new = high
                weights = jnp.exp2((masked - new) * factor)
                k.accum[h] = dot(weights.astype(BF16), valued)
            else:
                old = k.best[h][:, 0:1]
                new = jnp.maximum(old, high)
                weights = jnp.exp2((masked - new) * factor)
                fade = jnp.exp2((old - new) * factor)
                k.accum[h] = k.accum[h] * fade + dot(weights.astype(BF16), valued)
            k.best[h] = jnp.broadcast_to(new, (ROWS, LANES))

    def ids_of(j):
        remote(k.seg_out, k.seg_all.at[j], k.sg_s.at[0], k.sg_r.at[j], place_g[0]).wait_recv()
        return k.seg_all[j, 0:1, :]

    def swap(i):
        block = k.kv_all.at[2 * chip - 1 - i, half_rows]
        return remote(block, block, k.sw_s.at[i], k.sw_r.at[i], twin)

    def swap_start(i, carry):
        block = k.kv_all.at[2 * chip - 1 - i, half_rows]
        remote(block, block, k.sw_s.at[i], k.kv_r.at[2 * chip - 1 - i], twin).wait_recv()
        swap(i).start()
        return carry

    def swap_end(i, carry):
        swap(i).wait_send()
        return carry

    def earlier(i, carry):
        pair = 2 * (chip - 1 - i)
        swap(2 * i).wait_recv()
        swap(2 * i + 1).wait_recv()
        same = jnp.concatenate([ids_of(pair), ids_of(pair + 1)], axis=1) == k.ext_seg[8:, 0:1]
        block = k.kv_all[pl.ds(pair, 2)].reshape(2 * ROWS, 2 * HD)
        attend(block[:, 0:HD], block[:, HD:], same, False)
        return carry

    loads["q"].wait()
    causal = iota((ROWS, ROWS), 1) <= iota((ROWS, ROWS), 0)
    attend(k.pair[:, 0:HD], k.pair[:, HD:], causal & (seg_row == k.ext_seg[8:, 0:1]), True)

    for h in range(2):
        remote(rx[h].at[0:3], rx[h].at[0:3], k.x_s.at[h], k.x_r.at[h], place_x[0]).wait_recv()
        summed = k.pay[pl.ds(pl.multiple_of(x * 64, 64), 64), CUTS[h] : CUTS[h + 1]].astype(F32)
        for o in others_x:
            summed = summed + rx[h][o].astype(F32)
        for r in range(4):
            chunk[h][r] = summed[16 * r : 16 * r + 16, :].astype(BF16)
        for r in range(4):
            copy = remote(chunk[h].at[r], rz[h].at[z], k.z_s.at[h], k.z_r.at[h], {"tp": x * NZ + FIRST + r})
            pl.when(z != FIRST + r)(copy.start)

    kv_copies = []
    for d in range(1, NG):
        place = {"grp": lax.rem(grp + d, NG)}
        copy = remote(k.seg_out, k.seg_all.at[grp], k.sg_s.at[d], k.sg_r.at[grp], place)
        kv_copies.append((grp + d < NG, copy))
    for d in range(1, NG // 2):
        for half in range(2):
            rows = slice(128 * half, 128 * half + 128)
            place = {"grp": 2 * lax.rem(chip + d, NG // 2) + half}
            copy = remote(k.pair.at[rows], k.kv_all.at[grp, rows], k.kv_s.at[2 * d + half], k.kv_r.at[grp], place)
            kv_copies.append((chip + d < NG // 2, copy))
    kv_copies.append((core == 0, remote(k.pair, k.kv_all.at[grp], k.kv_s.at[0], k.kv_r.at[grp], twin)))
    for here, copy in kv_copies:
        pl.when(here)(copy.start)

    loads["z"].wait()
    gate = k.in_z[...].astype(F32)
    k.silu_z[...] = gate / (1.0 + jnp.exp(-gate))


    is_owner = (z >= FIRST) & (z < FIRST + 4)
    quarter = jnp.clip(z - FIRST, 0, 3)

    def forward(r):
        piece = low.at[x, r]
        for place in place_x:
            remote(piece, piece, k.h_s, k.h_r, place).start()

    loads["gain"].wait()

    @pl.when(is_owner)
    def _():
        sums = []
        for h in range(2):
            remote(rz[h].at[0:7], rz[h].at[0:7], k.z_s.at[h], k.z_r.at[h], place_z[0]).wait_recv()
            summed = chunk[h][quarter].astype(F32)
            for o in others_z:
                summed = summed + rz[h][o].astype(F32)
            sums.append(summed)
        left, right = sums
        rank, last = right[:, 0:128], right[:, 128:256]
        gain = k.in_gain[...].reshape(1, RANK + 2 * NST)
        mean = jnp.sum(left * left, axis=1, keepdims=True) + jnp.sum(rank * rank, axis=1, keepdims=True)
        scale = lax.rsqrt(mean / RANK + EPS)
        low[x, quarter, :, 0:384] = (left * scale * gain[:, 0:384]).astype(BF16)
        low[x, quarter, :, 384:RANK] = (rank * scale * gain[:, 384:RANK]).astype(BF16)
        lanes = iota((16, LANES), 1)
        power = last * last
        mean_b = jnp.sum(jnp.where(lanes < NST, power, 0.0), axis=1, keepdims=True) / NST
        mean_c = jnp.sum(jnp.where((lanes >= NST) & (lanes < 2 * NST), power, 0.0), axis=1, keepdims=True) / NST
        inverse = lax.rsqrt(last[:, SQUARES : SQUARES + 1] / FEATURES + EPS)
        coarse = inverse.astype(BF16).astype(F32)
        scale = jnp.where(lanes < NST, lax.rsqrt(mean_b + EPS), lax.rsqrt(mean_c + EPS))
        last = last * jnp.where(lanes < 2 * NST, scale, inverse)
        last = jnp.where(lanes == SQUARES, coarse, jnp.where(lanes == SQUARES + 1, inverse - coarse, last))
        low[x, quarter, :, RANK:PAY] = last.astype(BF16)
        low[x, quarter, :, RANK : RANK + 2 * NST] = (last[:, 0 : 2 * NST] * gain[:, RANK:]).astype(BF16)
        piece = low.at[x, quarter]
        for d, place in enumerate(place_z):
            remote(piece, piece, k.g_s.at[d], k.g_r.at[quarter], place).start()
        forward(quarter)

    for r in range(4):

        @pl.when(z != FIRST + r)
        def _(r=r):
            piece = low.at[x, r]
            remote(piece, piece, k.g_s.at[0], k.g_r.at[r], place_z[0]).wait_recv()
            forward(r)

    remote(k.outgoing, k.outgoing, k.pg_s, k.pg_r, place_p[0]).wait_recv()
    f_copies = []
    for d, place in enumerate(place_q):
        mine = k.out_pages.at[:, my_slot]
        f_copies.append(remote(mine, mine, k.pf_s, k.pf_r, place))
    for copy in f_copies:
        copy.start()


    for n in ("dt", "dt_bias", "a_log", "skip", "routing"):
        loads[n].wait()
    remote(low.at[0:3], low.at[0:3], k.h_s, k.h_r, place_x[0]).wait_recv()
    k.rank[...] = low[...].reshape(ROWS, PAY)[:, 0:RANK]
    shared = low[...].reshape(ROWS, PAY)[:, RANK:PAY]
    k.bc[...] = shared[:, 0 : 2 * NST]

    raw = dot(k.rank[...], k.in_dt[...]) + k.in_dt_bias[...]
    step = jnp.maximum(raw, 0.0) + jnp.log(1.0 + jnp.exp(-jnp.abs(raw)))
    k.driven[...] = step * k.conv[...].astype(F32)
    start = jnp.where(k.ext_seg[7 : 7 + ROWS, :] != k.ext_seg[8:, :], HUGE, 0.0)
    for lane in range(0, WIDTH, LANES):
        k.step[:, lane : lane + LANES] = step[:, lane : lane + LANES] + start
    pick = (iota((NST, 2 * NST), 0) == iota((NST, 2 * NST), 1)).astype(BF16)
    b_all = dot_t(pick, k.bc[...])
    for b in range(16):
        k.b_cols[b, :, 0:16] = b_all[:, 16 * b : 16 * b + 16]
    pick = (iota((2 * NST, 256), 0) == NST + iota((2 * NST, 256), 1) % NST).astype(BF16)
    own = iota((ROWS, 256), 1) // NST == iota((ROWS, 256), 0) % 16
    k.c_blocks[...] = jnp.where(own, dot(k.bc[...], pick), 0.0).astype(BF16)
    rate = jnp.exp(k.in_a_log[...]) * (-LOG2E)

    def scan(b, carry):
        state, left = carry
        rows = pl.ds(pl.multiple_of(b * 16, 16), 16)
        steps, driven, b_cols = k.step[rows, :], k.driven[rows, :], k.b_cols[b]
        for t in range(16):
            span = slice(NST * t, NST * (t + 1))
            decay = jnp.exp2(steps[t : t + 1, :] * rate)
            state = decay * state + b_cols[:, t : t + 1] * driven[t : t + 1, :]
            left = decay * left
            k.states[b, span, :] = state.astype(BF16)
            k.growth[b, span, :] = left.astype(BF16)
        return state, left

    begin = (jnp.zeros((NST, WIDTH), F32), jnp.ones((NST, WIDTH), F32))
    state, _ = lax.fori_loop(0, ROWS // 16, scan, begin)
    steps = jnp.sum(k.step[...], axis=0, keepdims=True)
    for i in range(4):
        k.own_end[NST * i : NST * (i + 1), :] = state[:, i * LANES : (i + 1) * LANES].astype(BF16)
    parts = []
    for _ in range(3):
        part = steps.astype(BF16).astype(F32)
        parts += [part[:, i * LANES : (i + 1) * LANES] for i in range(4)]
        steps = steps - part
    k.own_end[64:80, :] = jnp.concatenate(parts + [jnp.zeros((4, LANES), F32)], axis=0).astype(BF16)
    for place in place_g:
        remote(k.own_end, k.ends.at[grp], k.e_s, k.e_r, place).start()
    k.ends[grp] = k.own_end[...]

    lax.fori_loop(0, 2 * chip, swap_start, 0)
    @pl.when(core == 1)
    def _():
        remote(k.pair, k.kv_all.at[grp - 1], k.kv_s.at[0], k.kv_r.at[grp - 1], twin).wait_recv()
        same = ids_of(grp - 1) == k.ext_seg[8:, 0:1]
        attend(k.kv_all[grp - 1, :, 0:HD], k.kv_all[grp - 1, :, HD:], same, False)

    shared = shared.astype(F32)
    inverse = shared[:, SQUARES : SQUARES + 1] + shared[:, SQUARES + 1 : SQUARES + 2]
    k.out_expert[...] = (k.in_moe[...].astype(F32) * k.in_moe_gain[...] * inverse).astype(BF16)
    logits = shared.T
    experts = iota((LANES, ROWS), 0) - 2 * NST
    first = jnp.sum(jnp.where(experts == k.in_routing[0:1, :], logits, 0.0), axis=0, keepdims=True)
    second = jnp.sum(jnp.where(experts == k.in_routing[1:2, :], logits, 0.0), axis=0, keepdims=True)
    top = jnp.maximum(first, second)
    first, second = jnp.exp(first - top), jnp.exp(second - top)
    k.out_gate[0:1, :] = first / (first + second)
    k.out_gate[1:2, :] = second / (first + second)
    stores["expert"].start()
    stores["gate"].start()
    lax.fori_loop(0, chip, earlier, 0)
    for h in range(2):
        k.out_attn[:, h * HD : (h + 1) * HD] = (k.accum[h, :, 0:HD] / k.accum[h, :, HD:]).astype(BF16)
    stores["attn"].start()

    remote(k.ends.at[0:7], k.ends.at[0:7], k.e_s, k.e_r, place_g[0]).wait_recv()
    sums_of = []
    for j in range(NG):
        part = k.ends[j, 64:80, :].astype(F32)
        sums_of.append(part[0:4] + part[4:8] + part[8:12])
    entering = []
    for i in range(4):
        cols = slice(i * LANES, (i + 1) * LANES)
        state = jnp.zeros((NST, LANES), F32)
        mine = state
        for j in range(NG):
            mine = jnp.where(grp == j, state, mine)
            kept = jnp.exp2(sums_of[j][i : i + 1, :] * rate[:, cols])
            state = kept * state + k.ends[j, NST * i : NST * (i + 1), :].astype(F32)
        entering.append(mine)
        for g in range(NG):
            k.own_final[g, 2 * i : 2 * i + 2, :] = state[2 * g : 2 * g + 2, :]
    final_copy = remote(k.own_final.at[grp], k.landed, k.f_s, k.f_r, across)
    final_copy.start()
    entering = jnp.concatenate(entering, axis=1).astype(BF16)

    def finish(b, carry):
        rows = pl.ds(pl.multiple_of(b * 16, 16), 16)
        grown = k.growth[b].reshape(16, NST, WIDTH) * entering[None] + k.states[b].reshape(16, NST, WIDTH)
        value = dot(k.c_blocks[rows, :], grown.reshape(256, WIDTH))
        value = value + k.in_skip[...] * k.conv[rows, :].astype(F32)
        k.out_mixed[rows, :] = (value * k.silu_z[rows, :]).astype(BF16)
        return carry

    lax.fori_loop(0, ROWS // 16, finish, 0, unroll=4)
    stores["mixed"].start()

    final_copy.wait()
    for i in range(4):
        k.out_final[:, i * LANES : (i + 1) * LANES] = k.landed[2 * i : 2 * i + 2, :]
    stores["final"].start()
    rest = k.out_pages.at[:, 0:3]
    remote(rest, rest, k.pf_s, k.pf_r, place_q[0]).wait()
    remote(k.outgoing, k.outgoing, k.pg_s, k.pg_r, place_p[0]).wait_send()
    remote(k.ends.at[0:7], k.ends.at[0:7], k.e_s, k.e_r, place_g[0]).wait_send()
    for h in range(2):
        remote(rx[h].at[0:3], rx[h].at[0:3], k.x_s.at[h], k.x_r.at[h], place_x[0]).wait_send()

        @pl.when(is_owner)
        def _(h=h):
            remote(rz[h].at[0:3], rz[h].at[0:3], k.z_s.at[h], k.z_r.at[h], place_z[0]).wait_send()

        @pl.when(jnp.logical_not(is_owner))
        def _(h=h):
            remote(rz[h].at[0:4], rz[h].at[0:4], k.z_s.at[h], k.z_r.at[h], place_z[0]).wait_send()

    remote(low.at[0:3], low.at[0:3], k.h_s, k.h_r, place_x[0]).wait_send()

    @pl.when(is_owner)
    def _():
        for d in range(NZ - 1):
            remote(low.at[x, 0], low.at[x, 0], k.g_s.at[d], k.g_r.at[0], place_z[0]).wait_send()

    lax.fori_loop(0, 2 * chip, swap_end, 0)
    for here, copy in kv_copies:
        pl.when(here)(copy.wait_send)
    for store in stores.values():
        store.wait()


def hand_out(*refs):
    count = len(OUTPUTS)
    source, target, stage = refs[:count], refs[count : 2 * count], refs[2 * count : 3 * count]
    read, write = refs[3 * count :]
    inward = [pltpu.make_async_copy(source[i], stage[i], read.at[i]) for i in range(count)]
    outward = [pltpu.make_async_copy(stage[i], target[i], write.at[i]) for i in range(count)]
    for copy in inward:
        copy.start()
    for i in range(count):
        inward[i].wait()
        outward[i].start()
    for copy in outward:
        copy.wait()


def local(
    mamba_x, mamba_z, conv_weight, conv_bias, x_proj, norm_gain, dt_proj, dt_bias, a_log, d_skip,
    segment_ids, queries, keys_values, kv_owner, moe_in, moe_gain, router, routing,
):
    inputs = dict(
        x=mamba_x, seg=segment_ids, conv_w=conv_weight, conv_b=conv_bias.reshape(1, -1), proj=x_proj.T,
        owner=kv_owner.reshape(1, -1), keys_values=keys_values, moe=moe_in, moe_gain=moe_gain.reshape(1, -1), router=router.T, q=queries,
        z=mamba_z, gain=norm_gain, dt=dt_proj, dt_bias=dt_bias.reshape(1, -1), a_log=a_log,
        skip=d_skip.reshape(1, -1), routing=routing.T,
    )
    shapes = tuple(jax.ShapeDtypeStruct(s, t) for _, s, t in OUTPUTS)
    results = pl.pallas_call(
        main_kernel,
        out_shape=shapes,
        in_specs=[ANY] * len(OPERANDS),
        out_specs=tuple([ANY] * len(OUTPUTS)),
        scratch_shapes=[pltpu.VMEM(s, t) for _, s, t in SCRATCH]
        + [pltpu.VMEM(s, t) for _, s, t in INPUTS]
        + [pltpu.VMEM(s, t) for n, s, t in OUTPUTS if n != "pages"]
        + [DMA(s) if s else DMA for _, s in SEMS],
        compiler_params=pltpu.CompilerParams(
            vmem_limit_bytes=62 << 20, collective_id=0, has_side_effects=True
        ),
        name="span",
    )(*[inputs[n] for n in OPERANDS])
    mixed, final, attn, pages, expert, gates = pl.pallas_call(
        hand_out,
        out_shape=shapes,
        in_specs=[ANY] * len(OUTPUTS),
        out_specs=tuple([ANY] * len(OUTPUTS)),
        scratch_shapes=[pltpu.VMEM(s, t) for _, s, t in OUTPUTS] + [DMA((len(OUTPUTS),))] * 2,
        compiler_params=pltpu.CompilerParams(vmem_limit_bytes=62 << 20),
        name="results",
    )(*results)
    return (mixed, final[None], attn, pages.reshape(1, 1, 1, NG * SLOTS, BLK, 2 * HD), expert, gates.T)


def solution(mesh):
    placed = (
        P(("sect", "grp"), "tp"),
        P(("sect", "grp"), "tp"),
        P(None, "tp"),
        P("tp"),
        P("tp", None),
        P(),
        P(None, "tp"),
        P("tp"),
        P(None, "tp"),
        P("tp"),
        P("sect", "grp"),
        P(("sect", "grp"), "tp"),
        P(("sect", "grp"), None, None),
        P("sect", "grp", None),
        P(("sect", "grp"), "tp"),
        P("tp"),
        P("tp", None),
        P(("sect", "grp"), None),
    )
    return jax.shard_map(
        local,
        mesh=mesh,
        in_specs=placed,
        out_specs=(
            P(("sect", "grp"), "tp"),
            P("sect", "grp", "tp"),
            P(("sect", "grp"), "tp"),
            P("sect", "grp", "tp", None, None, None),
            P(("sect", "grp"), "tp"),
            P(("sect", "grp"), None),
        ),
        check_vma=False,
    )
```

```python
import jax
import jax.numpy as jnp
from jax import lax
from jax.experimental import pallas as pl
from jax.experimental.pallas import tpu as pltpu
from jax.sharding import PartitionSpec as P

MESH = pl.DeviceIdType.MESH
F32 = jnp.float32
BF16 = jnp.bfloat16
I32 = jnp.int32

ROWS = 256
WIDTH = 512
RANK = 512
NST = 16
HD = 128
BLK = 16
LANES = 128
NX, NZ, NG = 4, 8, 8
PAY = 640
CUTS = (0, 384, 640)
WIDE = (384, 256)
SLOTS = 4
FEATURES = 8192
EPS = 1e-06
SQUARES = 2 * NST + 16
FIRST = 2
LOG2E = 1.4426950408889634
HUGE = 1e30
VMEM = pl.BlockSpec(memory_space=pltpu.VMEM)
ANY = pl.BlockSpec(memory_space=pl.ANY)
DMA = pltpu.SemaphoreType.DMA


def iota(shape, dim):
    return lax.broadcasted_iota(I32, shape, dim)


def dot(a, b, **kw):
    return jnp.dot(a, b, preferred_element_type=F32, **kw)


def dot_t(a, b, **kw):
    return lax.dot_general(a, b, (((1,), (1,)), ((), ())), preferred_element_type=F32, **kw)


def remote(src, dst, send, recv, where):
    return pltpu.make_async_remote_copy(
        src_ref=src, dst_ref=dst, send_sem=send, recv_sem=recv, device_id=where, device_id_type=MESH
    )


INPUTS = (
    ("x", (ROWS, WIDTH), BF16),
    ("seg", (1, ROWS), I32),
    ("conv_w", (4, WIDTH), F32),
    ("conv_b", (1, WIDTH), F32),
    ("proj", (RANK + 2 * NST, WIDTH), BF16),
    ("owner", (1, 16), I32),
    ("pair", (ROWS, 2, HD), BF16),
    ("moe", (ROWS, 256), BF16),
    ("moe_gain", (1, 256), F32),
    ("router", (16, 256), BF16),
    ("q", (ROWS, 2 * HD), BF16),
    ("z", (ROWS, WIDTH), BF16),
    ("gain", (RANK + 2 * NST,), F32),
    ("dt", (RANK, WIDTH), BF16),
    ("dt_bias", (1, WIDTH), F32),
    ("a_log", (NST, WIDTH), F32),
    ("skip", (1, WIDTH), F32),
    ("routing", (2, ROWS), I32),
)
OUTPUTS = (
    ("mixed", (ROWS, WIDTH), BF16),
    ("final", (2, WIDTH), F32),
    ("attn", (ROWS, 2 * HD), BF16),
    ("pages", (NG, SLOTS, BLK, 2 * HD), BF16),
    ("expert", (ROWS, 256), BF16),
    ("gate", (2, ROWS), F32),
)
OPERANDS = [n for n, _, _ in INPUTS if n != "pair"] + ["keys_values"]
SCRATCH = (
    ("pair", (ROWS, 2 * HD), BF16),
    ("rim", (16, WIDTH), BF16),
    ("rim_seg", (8, LANES), F32),
    ("seg_send", (8, LANES), F32),
    ("seg_out", (8, ROWS), F32),
    ("seg_all", (NG, 8, ROWS), F32),
    ("kv_all", (NG, ROWS, 2 * HD), BF16),
    ("ext", (8 + ROWS, WIDTH), F32),
    ("ext_seg", (8 + ROWS, LANES), F32),
    ("conv", (ROWS, WIDTH), BF16),
    ("pay", (ROWS, PAY), BF16),
    ("rx0", (NX, 64, WIDE[0]), BF16),
    ("rx1", (NX, 64, WIDE[1]), BF16),
    ("chunk0", (4, 16, WIDE[0]), BF16),
    ("chunk1", (4, 16, WIDE[1]), BF16),
    ("rz0", (NZ, 16, WIDE[0]), BF16),
    ("rz1", (NZ, 16, WIDE[1]), BF16),
    ("low", (NX, 4, 16, PAY), BF16),
    ("outgoing", (NG, BLK, 2 * HD), BF16),
    ("best", (2, ROWS, LANES), F32),
    ("accum", (2, ROWS, 2 * HD), F32),
    ("silu_z", (ROWS, WIDTH), F32),
    ("rank", (ROWS, RANK), BF16),
    ("bc", (ROWS, 2 * NST), BF16),
    ("step", (ROWS, WIDTH), F32),
    ("driven", (ROWS, WIDTH), F32),
    ("b_cols", (16, NST, LANES), F32),
    ("c_blocks", (ROWS, 256), BF16),
    ("states", (16, 256, WIDTH), BF16),
    ("growth", (16, 256, WIDTH), BF16),
    ("ends", (NG, 80, LANES), BF16),
    ("own_end", (80, LANES), BF16),
    ("own_final", (NG, 8, LANES), F32),
    ("landed", (8, LANES), F32),
)
SEMS = (
    ("load", (len(INPUTS),)), ("store", (len(OUTPUTS),)),
    ("rim_s", ()), ("rim_r", ()), ("rseg_s", ()), ("rseg_r", ()),
    ("kv_s", (NG,)), ("kv_r", (NG,)), ("sg_s", (NG,)), ("sg_r", (NG,)),
    ("sw_s", (NG,)), ("sw_r", (NG,)),
    ("pg_s", ()), ("pg_r", ()), ("pf_s", ()), ("pf_r", ()),
    ("x_s", (2,)), ("x_r", (2,)), ("z_s", (2,)), ("z_r", (2,)),
    ("g_s", (NZ,)), ("g_r", (4,)), ("h_s", ()), ("h_r", ()),
    ("e_s", ()), ("e_r", ()), ("f_s", ()), ("f_r", ()),
)


class Refs:
    pass


def main_kernel(*refs):
    k = Refs()
    names = ["hbm_" + n for n in OPERANDS] + ["hbm_out_" + n for n, _, _ in OUTPUTS]
    names += [n for n, _, _ in SCRATCH] + ["in_" + n for n, _, _ in INPUTS]
    names += ["out_" + n for n, _, _ in OUTPUTS if n != "pages"] + [n for n, _ in SEMS]
    for name, ref in zip(names, refs, strict=True):
        setattr(k, name, ref)
    k.out_pages = k.hbm_out_pages
    sect, tp, grp = lax.axis_index("sect"), lax.axis_index("tp"), lax.axis_index("grp")
    x, z = tp // NZ, tp % NZ
    chip, core = grp // 2, grp % 2
    twin = {"grp": grp + 1 - 2 * core}
    half_rows = pl.ds(pl.multiple_of(128 * core, 128), 128)
    loads = {}
    for i, (n, _, _) in enumerate(INPUTS):
        if n == "pair":
            src = k.hbm_keys_values.at[:, :, pl.ds(pl.multiple_of(tp // 4 * HD, HD), HD)]
        else:
            src = getattr(k, "hbm_" + n)
        loads[n] = pltpu.make_async_copy(src, getattr(k, "in_" + n), k.load.at[i])
        loads[n].start()
    stores = {}
    for i, (n, _, _) in enumerate(OUTPUTS):
        if n != "pages":
            stores[n] = pltpu.make_async_copy(getattr(k, "out_" + n), getattr(k, "hbm_out_" + n), k.store.at[i])

    quad = z // 4 * 4
    others_x = [lax.rem(x + d, NX) for d in range(1, NX)]
    others_z = [lax.rem(z + d, NZ) for d in range(1, NZ)]
    others_q = [quad + lax.rem(z + d, 4) for d in range(1, 4)]
    others_g = [lax.rem(grp + d, NG) for d in range(1, NG)]
    place_x = [{"tp": o * NZ + z} for o in others_x]
    place_z = [{"tp": x * NZ + o} for o in others_z]
    place_q = [{"tp": x * NZ + o} for o in others_q]
    place_g = [{"grp": o} for o in others_g]
    place_p = [{"sect": 1 - sect, "grp": o} for o in range(NG)]
    across = {"sect": 1 - sect}
    partners = place_x + place_z + place_g + place_p
    barrier = pltpu.get_barrier_semaphore()
    for place in partners:
        pl.semaphore_signal(barrier, inc=1, device_id=place, device_id_type=MESH)

    loads["x"].wait()
    loads["seg"].wait()
    seg_row = k.in_seg[...].astype(F32)
    seg_cols = jnp.broadcast_to(seg_row, (LANES, ROWS)).T
    k.ext_seg[8:, :] = seg_cols
    k.seg_send[...] = seg_cols[ROWS - 8 :, :]
    k.seg_out[...] = jnp.broadcast_to(seg_row, (8, ROWS))
    pl.semaphore_wait(barrier, len(partners))

    behind = {"grp": lax.rem(grp + 1, NG)}
    rim_copy = remote(k.in_x.at[ROWS - 16 : ROWS], k.rim, k.rim_s, k.rim_r, behind)
    rseg_copy = remote(k.seg_send, k.rim_seg, k.rseg_s, k.rseg_r, behind)
    rim_copy.start()
    rseg_copy.start()

    loads["moe"].wait()
    loads["moe_gain"].wait()
    loads["router"].wait()
    moe_rows = k.in_moe[...].astype(F32)
    spread = (iota((LANES, 16), 0) == iota((LANES, 16), 1) + 2 * NST).astype(BF16)
    router = dot(spread, k.in_router[...])
    logits_part = dot_t(moe_rows * k.in_moe_gain[...], router, precision=lax.Precision.HIGHEST)
    squares = jnp.sum(moe_rows * moe_rows, axis=1, keepdims=True)
    tail = jnp.where(iota((ROWS, LANES), 1) == SQUARES, squares, logits_part)

    k.ext[8:, :] = k.in_x[...].astype(F32)
    loads["conv_w"].wait()
    loads["conv_b"].wait()
    loads["proj"].wait()
    rim_copy.wait()
    rseg_copy.wait()
    k.ext[0:8, :] = k.rim[8:16, :].astype(F32)
    k.ext_seg[0:8, :] = jnp.where(grp == 0, -1.0, k.rim_seg[...])
    here = k.ext_seg[8:, :]
    same = [k.ext_seg[5 + i : 5 + i + ROWS, :] == here for i in range(3)]
    for lane in range(0, WIDTH, LANES):
        cols = slice(lane, lane + LANES)
        value = jnp.broadcast_to(k.in_conv_b[:, cols], (ROWS, LANES))
        for i in range(4):
            term = k.ext[5 + i : 5 + i + ROWS, cols] * k.in_conv_w[i : i + 1, cols]
            value = value + (jnp.where(same[i], term, 0.0) if i < 3 else term)
        k.conv[:, cols] = (value / (1.0 + jnp.exp(-value))).astype(BF16)
    conv = k.conv[...]

    rx, chunk, rz, low = (k.rx0, k.rx1), (k.chunk0, k.chunk1), (k.rz0, k.rz1), k.low
    for h in range(2):
        if h == 0:
            k.pay[:, 0:384] = dot_t(conv, k.in_proj[0:384, :]).astype(BF16)
        else:
            k.pay[:, 384:RANK] = dot_t(conv, k.in_proj[384:RANK, :]).astype(BF16)
            spread = (iota((LANES, 2 * NST), 0) == iota((LANES, 2 * NST), 1)).astype(BF16)
            last = dot(spread, k.in_proj[RANK:, :]).astype(BF16)
            k.pay[:, RANK:PAY] = (dot_t(conv, last) + tail).astype(BF16)
        for o, place in zip(others_x, place_x):
            src = k.pay.at[pl.ds(pl.multiple_of(o * 64, 64), 64), CUTS[h] : CUTS[h + 1]]
            remote(src, rx[h].at[x], k.x_s.at[h], k.x_r.at[h], place).start()

    loads["pair"].wait()
    k.pair[...] = k.in_pair[...].reshape(ROWS, 2 * HD)

    loads["owner"].wait()
    owners = jnp.broadcast_to(k.in_owner[...].astype(F32), (8, 16)).astype(BF16)
    owner_of = dot(owners, (iota((16, ROWS), 0) == iota((16, ROWS), 1) // BLK).astype(BF16))[0:1, :]
    owner_lanes = dot(owners, (iota((16, LANES), 0) == iota((16, LANES), 1)).astype(BF16))[0:1, :]
    owner_rows = jnp.broadcast_to(owner_lanes, (LANES, LANES)).T[0:16, 0:1]
    before = (owner_rows == owner_of) & (iota((16, ROWS), 0) < iota((16, ROWS), 1) // BLK)
    order = jnp.sum(jnp.where(before, 1.0, 0.0), axis=0, keepdims=True)
    slot = jnp.where(order == lax.rem(z, 4).astype(F32), owner_of, -1.0)
    row, col = iota((NG * BLK, ROWS), 0), iota((NG * BLK, ROWS), 1)
    choose = (slot == (row // BLK).astype(F32)) & (row % BLK == col % BLK)
    chosen = dot(jnp.where(choose, 1.0, 0.0).astype(BF16), k.pair[...])
    k.outgoing[...] = chosen.astype(BF16).reshape(NG, BLK, 2 * HD)
    my_slot = lax.rem(z, 4)
    page_copies = []
    for o in range(NG):
        dst = k.out_pages.at[grp, my_slot]
        page_copies.append(remote(k.outgoing.at[o], dst, k.pg_s, k.pg_r, place_p[o]))
    for copy in page_copies:
        copy.start()

    factor = HD**-0.5 * LOG2E

    def attend(key_block, value_block, allowed, first):
        valued = jnp.concatenate([value_block, jnp.ones_like(value_block)], axis=1)
        for h in range(2):
            scores = dot_t(k.in_q[:, h * HD : (h + 1) * HD], key_block)
            masked = jnp.where(allowed, scores, -HUGE)
            high = jnp.max(masked, axis=1, keepdims=True)
            if first:
                new = high
                weights = jnp.exp2((masked - new) * factor)
                k.accum[h] = dot(weights.astype(BF16), valued)
            else:
                old = k.best[h][:, 0:1]
                new = jnp.maximum(old, high)
                weights = jnp.exp2((masked - new) * factor)
                fade = jnp.exp2((old - new) * factor)
                k.accum[h] = k.accum[h] * fade + dot(weights.astype(BF16), valued)
            k.best[h] = jnp.broadcast_to(new, (ROWS, LANES))

    def ids_of(j):
        remote(k.seg_out, k.seg_all.at[j], k.sg_s.at[0], k.sg_r.at[j], place_g[0]).wait_recv()
        return k.seg_all[j, 0:1, :]

    def swap(i):
        block = k.kv_all.at[2 * chip - 1 - i, half_rows]
        return remote(block, block, k.sw_s.at[i], k.sw_r.at[i], twin)

    def swap_start(i, carry):
        block = k.kv_all.at[2 * chip - 1 - i, half_rows]
        remote(block, block, k.sw_s.at[i], k.kv_r.at[2 * chip - 1 - i], twin).wait_recv()
        swap(i).start()
        return carry

    def swap_end(i, carry):
        swap(i).wait_send()
        return carry

    def earlier(i, carry):
        pair = 2 * (chip - 1 - i)
        swap(2 * i).wait_recv()
        swap(2 * i + 1).wait_recv()
        same = jnp.concatenate([ids_of(pair), ids_of(pair + 1)], axis=1) == k.ext_seg[8:, 0:1]
        block = k.kv_all[pl.ds(pair, 2)].reshape(2 * ROWS, 2 * HD)
        attend(block[:, 0:HD], block[:, HD:], same, False)
        return carry

    loads["q"].wait()
    causal = iota((ROWS, ROWS), 1) <= iota((ROWS, ROWS), 0)
    attend(k.pair[:, 0:HD], k.pair[:, HD:], causal & (seg_row == k.ext_seg[8:, 0:1]), True)

    for h in range(2):
        remote(rx[h].at[0:3], rx[h].at[0:3], k.x_s.at[h], k.x_r.at[h], place_x[0]).wait_recv()
        summed = k.pay[pl.ds(pl.multiple_of(x * 64, 64), 64), CUTS[h] : CUTS[h + 1]].astype(F32)
        for o in others_x:
            summed = summed + rx[h][o].astype(F32)
        for r in range(4):
            chunk[h][r] = summed[16 * r : 16 * r + 16, :].astype(BF16)
        for r in range(4):
            copy = remote(chunk[h].at[r], rz[h].at[z], k.z_s.at[h], k.z_r.at[h], {"tp": x * NZ + FIRST + r})
            pl.when(z != FIRST + r)(copy.start)

    kv_copies = []
    for d in range(1, NG):
        place = {"grp": lax.rem(grp + d, NG)}
        copy = remote(k.seg_out, k.seg_all.at[grp], k.sg_s.at[d], k.sg_r.at[grp], place)
        kv_copies.append((grp + d < NG, copy))
    for d in range(1, NG // 2):
        for half in range(2):
            rows = slice(128 * half, 128 * half + 128)
            place = {"grp": 2 * lax.rem(chip + d, NG // 2) + half}
            copy = remote(k.pair.at[rows], k.kv_all.at[grp, rows], k.kv_s.at[2 * d + half], k.kv_r.at[grp], place)
            kv_copies.append((chip + d < NG // 2, copy))
    kv_copies.append((core == 0, remote(k.pair, k.kv_all.at[grp], k.kv_s.at[0], k.kv_r.at[grp], twin)))
    for here, copy in kv_copies:
        pl.when(here)(copy.start)

    loads["z"].wait()
    gate = k.in_z[...].astype(F32)
    k.silu_z[...] = gate / (1.0 + jnp.exp(-gate))


    is_owner = (z >= FIRST) & (z < FIRST + 4)
    quarter = jnp.clip(z - FIRST, 0, 3)

    def forward(r):
        piece = low.at[x, r]
        for place in place_x:
            remote(piece, piece, k.h_s, k.h_r, place).start()

    loads["gain"].wait()

    @pl.when(is_owner)
    def _():
        sums = []
        for h in range(2):
            remote(rz[h].at[0:7], rz[h].at[0:7], k.z_s.at[h], k.z_r.at[h], place_z[0]).wait_recv()
            summed = chunk[h][quarter].astype(F32)
            for o in others_z:
                summed = summed + rz[h][o].astype(F32)
            sums.append(summed)
        left, right = sums
        rank, last = right[:, 0:128], right[:, 128:256]
        gain = k.in_gain[...].reshape(1, RANK + 2 * NST)
        mean = jnp.sum(left * left, axis=1, keepdims=True) + jnp.sum(rank * rank, axis=1, keepdims=True)
        scale = lax.rsqrt(mean / RANK + EPS)
        low[x, quarter, :, 0:384] = (left * scale * gain[:, 0:384]).astype(BF16)
        low[x, quarter, :, 384:RANK] = (rank * scale * gain[:, 384:RANK]).astype(BF16)
        lanes = iota((16, LANES), 1)
        power = last * last
        mean_b = jnp.sum(jnp.where(lanes < NST, power, 0.0), axis=1, keepdims=True) / NST
        mean_c = jnp.sum(jnp.where((lanes >= NST) & (lanes < 2 * NST), power, 0.0), axis=1, keepdims=True) / NST
        inverse = lax.rsqrt(last[:, SQUARES : SQUARES + 1] / FEATURES + EPS)
        coarse = inverse.astype(BF16).astype(F32)
        scale = jnp.where(lanes < NST, lax.rsqrt(mean_b + EPS), lax.rsqrt(mean_c + EPS))
        last = last * jnp.where(lanes < 2 * NST, scale, inverse)
        last = jnp.where(lanes == SQUARES, coarse, jnp.where(lanes == SQUARES + 1, inverse - coarse, last))
        low[x, quarter, :, RANK:PAY] = last.astype(BF16)
        low[x, quarter, :, RANK : RANK + 2 * NST] = (last[:, 0 : 2 * NST] * gain[:, RANK:]).astype(BF16)
        piece = low.at[x, quarter]
        for d, place in enumerate(place_z):
            remote(piece, piece, k.g_s.at[d], k.g_r.at[quarter], place).start()
        forward(quarter)

    for r in range(4):

        @pl.when(z != FIRST + r)
        def _(r=r):
            piece = low.at[x, r]
            remote(piece, piece, k.g_s.at[0], k.g_r.at[r], place_z[0]).wait_recv()
            forward(r)

    remote(k.outgoing, k.outgoing, k.pg_s, k.pg_r, place_p[0]).wait_recv()
    f_copies = []
    for d, place in enumerate(place_q):
        mine = k.out_pages.at[:, my_slot]
        f_copies.append(remote(mine, mine, k.pf_s, k.pf_r, place))
    for copy in f_copies:
        copy.start()


    for n in ("dt", "dt_bias", "a_log", "skip", "routing"):
        loads[n].wait()
    remote(low.at[0:3], low.at[0:3], k.h_s, k.h_r, place_x[0]).wait_recv()
    k.rank[...] = low[...].reshape(ROWS, PAY)[:, 0:RANK]
    shared = low[...].reshape(ROWS, PAY)[:, RANK:PAY]
    k.bc[...] = shared[:, 0 : 2 * NST]

    raw = dot(k.rank[...], k.in_dt[...]) + k.in_dt_bias[...]
    step = jnp.maximum(raw, 0.0) + jnp.log(1.0 + jnp.exp(-jnp.abs(raw)))
    k.driven[...] = step * k.conv[...].astype(F32)
    start = jnp.where(k.ext_seg[7 : 7 + ROWS, :] != k.ext_seg[8:, :], HUGE, 0.0)
    for lane in range(0, WIDTH, LANES):
        k.step[:, lane : lane + LANES] = step[:, lane : lane + LANES] + start
    pick = (iota((NST, 2 * NST), 0) == iota((NST, 2 * NST), 1)).astype(BF16)
    b_all = dot_t(pick, k.bc[...])
    for b in range(16):
        k.b_cols[b, :, 0:16] = b_all[:, 16 * b : 16 * b + 16]
    pick = (iota((2 * NST, 256), 0) == NST + iota((2 * NST, 256), 1) % NST).astype(BF16)
    own = iota((ROWS, 256), 1) // NST == iota((ROWS, 256), 0) % 16
    k.c_blocks[...] = jnp.where(own, dot(k.bc[...], pick), 0.0).astype(BF16)
    rate = jnp.exp(k.in_a_log[...]) * (-LOG2E)

    def scan(b, carry):
        state, left = carry
        rows = pl.ds(pl.multiple_of(b * 16, 16), 16)
        steps, driven, b_cols = k.step[rows, :], k.driven[rows, :], k.b_cols[b]
        for t in range(16):
            span = slice(NST * t, NST * (t + 1))
            decay = jnp.exp2(steps[t : t + 1, :] * rate)
            state = decay * state + b_cols[:, t : t + 1] * driven[t : t + 1, :]
            left = decay * left
            k.states[b, span, :] = state.astype(BF16)
            k.growth[b, span, :] = left.astype(BF16)
        return state, left

    begin = (jnp.zeros((NST, WIDTH), F32), jnp.ones((NST, WIDTH), F32))
    state, _ = lax.fori_loop(0, ROWS // 16, scan, begin)
    steps = jnp.sum(k.step[...], axis=0, keepdims=True)
    for i in range(4):
        k.own_end[NST * i : NST * (i + 1), :] = state[:, i * LANES : (i + 1) * LANES].astype(BF16)
    parts = []
    for _ in range(3):
        part = steps.astype(BF16).astype(F32)
        parts += [part[:, i * LANES : (i + 1) * LANES] for i in range(4)]
        steps = steps - part
    k.own_end[64:80, :] = jnp.concatenate(parts + [jnp.zeros((4, LANES), F32)], axis=0).astype(BF16)
    for place in place_g:
        remote(k.own_end, k.ends.at[grp], k.e_s, k.e_r, place).start()
    k.ends[grp] = k.own_end[...]

    lax.fori_loop(0, 2 * chip, swap_start, 0)
    @pl.when(core == 1)
    def _():
        remote(k.pair, k.kv_all.at[grp - 1], k.kv_s.at[0], k.kv_r.at[grp - 1], twin).wait_recv()
        same = ids_of(grp - 1) == k.ext_seg[8:, 0:1]
        attend(k.kv_all[grp - 1, :, 0:HD], k.kv_all[grp - 1, :, HD:], same, False)

    shared = shared.astype(F32)
    inverse = shared[:, SQUARES : SQUARES + 1] + shared[:, SQUARES + 1 : SQUARES + 2]
    k.out_expert[...] = (k.in_moe[...].astype(F32) * k.in_moe_gain[...] * inverse).astype(BF16)
    logits = shared.T
    experts = iota((LANES, ROWS), 0) - 2 * NST
    first = jnp.sum(jnp.where(experts == k.in_routing[0:1, :], logits, 0.0), axis=0, keepdims=True)
    second = jnp.sum(jnp.where(experts == k.in_routing[1:2, :], logits, 0.0), axis=0, keepdims=True)
    top = jnp.maximum(first, second)
    first, second = jnp.exp(first - top), jnp.exp(second - top)
    k.out_gate[0:1, :] = first / (first + second)
    k.out_gate[1:2, :] = second / (first + second)
    stores["expert"].start()
    stores["gate"].start()
    lax.fori_loop(0, chip, earlier, 0)
    for h in range(2):
        k.out_attn[:, h * HD : (h + 1) * HD] = (k.accum[h, :, 0:HD] / k.accum[h, :, HD:]).astype(BF16)
    stores["attn"].start()

    remote(k.ends.at[0:7], k.ends.at[0:7], k.e_s, k.e_r, place_g[0]).wait_recv()
    sums_of = []
    for j in range(NG):
        part = k.ends[j, 64:80, :].astype(F32)
        sums_of.append(part[0:4] + part[4:8] + part[8:12])
    entering = []
    for i in range(4):
        cols = slice(i * LANES, (i + 1) * LANES)
        state = jnp.zeros((NST, LANES), F32)
        mine = state
        for j in range(NG):
            mine = jnp.where(grp == j, state, mine)
            kept = jnp.exp2(sums_of[j][i : i + 1, :] * rate[:, cols])
            state = kept * state + k.ends[j, NST * i : NST * (i + 1), :].astype(F32)
        entering.append(mine)
        for g in range(NG):
            k.own_final[g, 2 * i : 2 * i + 2, :] = state[2 * g : 2 * g + 2, :]
    final_copy = remote(k.own_final.at[grp], k.landed, k.f_s, k.f_r, across)
    final_copy.start()
    entering = jnp.concatenate(entering, axis=1).astype(BF16)

    def finish(b, carry):
        rows = pl.ds(pl.multiple_of(b * 16, 16), 16)
        grown = k.growth[b].reshape(16, NST, WIDTH) * entering[None] + k.states[b].reshape(16, NST, WIDTH)
        value = dot(k.c_blocks[rows, :], grown.reshape(256, WIDTH))
        value = value + k.in_skip[...] * k.conv[rows, :].astype(F32)
        k.out_mixed[rows, :] = (value * k.silu_z[rows, :]).astype(BF16)
        return carry

    lax.fori_loop(0, ROWS // 16, finish, 0, unroll=4)
    stores["mixed"].start()

    final_copy.wait()
    for i in range(4):
        k.out_final[:, i * LANES : (i + 1) * LANES] = k.landed[2 * i : 2 * i + 2, :]
    stores["final"].start()
    rest = k.out_pages.at[:, 0:3]
    remote(rest, rest, k.pf_s, k.pf_r, place_q[0]).wait()
    remote(k.outgoing, k.outgoing, k.pg_s, k.pg_r, place_p[0]).wait_send()
    remote(k.ends.at[0:7], k.ends.at[0:7], k.e_s, k.e_r, place_g[0]).wait_send()
    for h in range(2):
        remote(rx[h].at[0:3], rx[h].at[0:3], k.x_s.at[h], k.x_r.at[h], place_x[0]).wait_send()

        @pl.when(is_owner)
        def _(h=h):
            remote(rz[h].at[0:3], rz[h].at[0:3], k.z_s.at[h], k.z_r.at[h], place_z[0]).wait_send()

        @pl.when(jnp.logical_not(is_owner))
        def _(h=h):
            remote(rz[h].at[0:4], rz[h].at[0:4], k.z_s.at[h], k.z_r.at[h], place_z[0]).wait_send()

    remote(low.at[0:3], low.at[0:3], k.h_s, k.h_r, place_x[0]).wait_send()

    @pl.when(is_owner)
    def _():
        for d in range(NZ - 1):
            remote(low.at[x, 0], low.at[x, 0], k.g_s.at[d], k.g_r.at[0], place_z[0]).wait_send()

    lax.fori_loop(0, 2 * chip, swap_end, 0)
    for here, copy in kv_copies:
        pl.when(here)(copy.wait_send)
    for store in stores.values():
        store.wait()


def hand_out(*refs):
    count = len(OUTPUTS)
    source, target, stage = refs[:count], refs[count : 2 * count], refs[2 * count : 3 * count]
    read, write = refs[3 * count :]
    inward = [pltpu.make_async_copy(source[i], stage[i], read.at[i]) for i in range(count)]
    outward = [pltpu.make_async_copy(stage[i], target[i], write.at[i]) for i in range(count)]
    for copy in inward:
        copy.start()
    for i in range(count):
        inward[i].wait()
        outward[i].start()
    for copy in outward:
        copy.wait()


def local(
    mamba_x, mamba_z, conv_weight, conv_bias, x_proj, norm_gain, dt_proj, dt_bias, a_log, d_skip,
    segment_ids, queries, keys_values, kv_owner, moe_in, moe_gain, router, routing,
):
    inputs = dict(
        x=mamba_x, seg=segment_ids, conv_w=conv_weight, conv_b=conv_bias.reshape(1, -1), proj=x_proj.T,
        owner=kv_owner.reshape(1, -1), keys_values=keys_values, moe=moe_in, moe_gain=moe_gain.reshape(1, -1), router=router.T, q=queries,
        z=mamba_z, gain=norm_gain, dt=dt_proj, dt_bias=dt_bias.reshape(1, -1), a_log=a_log,
        skip=d_skip.reshape(1, -1), routing=routing.T,
    )
    shapes = tuple(jax.ShapeDtypeStruct(s, t) for _, s, t in OUTPUTS)
    results = pl.pallas_call(
        main_kernel,
        out_shape=shapes,
        in_specs=[ANY] * len(OPERANDS),
        out_specs=tuple([ANY] * len(OUTPUTS)),
        scratch_shapes=[pltpu.VMEM(s, t) for _, s, t in SCRATCH]
        + [pltpu.VMEM(s, t) for _, s, t in INPUTS]
        + [pltpu.VMEM(s, t) for n, s, t in OUTPUTS if n != "pages"]
        + [DMA(s) if s else DMA for _, s in SEMS],
        compiler_params=pltpu.CompilerParams(
            vmem_limit_bytes=62 << 20, collective_id=0, has_side_effects=True
        ),
        name="span",
    )(*[inputs[n] for n in OPERANDS])
    mixed, final, attn, pages, expert, gates = pl.pallas_call(
        hand_out,
        out_shape=shapes,
        in_specs=[ANY] * len(OUTPUTS),
        out_specs=tuple([ANY] * len(OUTPUTS)),
        scratch_shapes=[pltpu.VMEM(s, t) for _, s, t in OUTPUTS] + [DMA((len(OUTPUTS),))] * 2,
        compiler_params=pltpu.CompilerParams(vmem_limit_bytes=62 << 20),
        name="results",
    )(*results)
    return (mixed, final[None], attn, pages.reshape(1, 1, 1, NG * SLOTS, BLK, 2 * HD), expert, gates.T)


def solution(mesh):
    placed = (
        P(("sect", "grp"), "tp"),
        P(("sect", "grp"), "tp"),
        P(None, "tp"),
        P("tp"),
        P("tp", None),
        P(),
        P(None, "tp"),
        P("tp"),
        P(None, "tp"),
        P("tp"),
        P("sect", "grp"),
        P(("sect", "grp"), "tp"),
        P(("sect", "grp"), None, None),
        P("sect", "grp", None),
        P(("sect", "grp"), "tp"),
        P("tp"),
        P("tp", None),
        P(("sect", "grp"), None),
    )
    return jax.shard_map(
        local,
        mesh=mesh,
        in_specs=placed,
        out_specs=(
            P(("sect", "grp"), "tp"),
            P("sect", "grp", "tp"),
            P(("sect", "grp"), "tp"),
            P("sect", "grp", "tp", None, None, None),
            P(("sect", "grp"), "tp"),
            P(("sect", "grp"), None),
        ),
        check_vma=False,
    )
```
